32 devices in a mesh: leaf: 4 (over z), clusters: 8 (over y, x, core).
Axes of the slice: x: 2, y: 2, z: 4, core: 2. Of those that a mesh axis runs over, the one named last changes fastest.
Arguments:
- samples: float32 [16384, 256], P(('clusters', 'leaf')), may hold values from -6 to 6
- probes: float32 [16384, 256], P(('clusters', 'leaf')), may hold values from -6 to 6
- near_blocks: float32 [16384, 2, 512], P(('clusters', 'leaf')), may hold values from -0.15625 to 0.15625
- couplings: float32 [8, 3, 2, 128, 128], P('clusters'), may hold values from -0.375 to 0.375
- node_slot: int32 [8, 3], P('clusters'), may hold values from 0 to 2, each once within a row
Outputs:
- leaf_bases: float32 [16384, 128], P(('clusters', 'leaf'))
- transfer_bases: float32 [32, 2, 256, 128], P(('clusters', 'leaf'))
- top_samples: float32 [8, 128, 256], P('clusters')
- top_probes: float32 [8, 128, 256], P('clusters')
The draws below stay inside these ranges and needn't reach their ends.
Inputs may be any that keep to these rules, and one draw needn't show every extreme that they name: Every row of node_slot names each of 0 to 2 exactly once.
All inputs are finite; a program needn't handle non-finite values.
Results may differ from the reference program's by a relative error of at most 0.00016.
Values sent between devices are 32-bit elements; how exact they have to be, the bound alone decides.
No kernel may reach another device: no remote copies, remote signals or barrier semaphores. Data moves between devices by JAX's collectives and lax.ppermute only.
A program may use at most 64 MiB of HBM per device.

```python
import jax
import jax.numpy as jnp
from jax import lax

K = 128
S = 256
M = 512
SUBTREE = 4
LEVELS = 2
NODES = 3
ROWS = 16384
N_CLUSTERS = 8


def block_levels(own_key, shape, cuts, low, top_value):
    def one(axis_at, parts):
        draws = jax.random.uniform(jax.random.fold_in(jax.random.fold_in(own_key, 6), axis_at), (parts,), jnp.float32, low / len(cuts), top_value / len(cuts))
        return jnp.repeat(jnp.exp(draws), shape[axis_at] // parts).reshape((-1,) + (1,) * (len(shape) - axis_at - 1))

    factor_of = one(*cuts[0])
    for cut in cuts[1:]:
        factor_of = factor_of * one(*cut)
    return factor_of


def noise(rng, extent, width, reach, cuts=(), dtype=jnp.bfloat16):
    array = jax.random.normal(rng, extent, jnp.float32) * width
    if len(cuts) > 0:
        array = block_levels(rng, extent, cuts, -0.22, 0.18) * array
    return jnp.clip(array, min=-reach, max=reach).astype(dtype)


def setup_inputs(seed: int = 0) -> dict:
    keys = jax.random.split(jax.random.key(seed), 6)
    return {
        "samples": noise(keys[0], (ROWS, S), 1.0, 6.0, ((0, 32),), jnp.float32),
        "probes": noise(keys[1], (ROWS, S), 1.0, 6.0, ((0, 32),), jnp.float32),
        "near_blocks": noise(keys[2], (ROWS, 2, M), (3 * M) ** -0.5, 0.15625, ((0, 32),), jnp.float32),
        "couplings": noise(keys[3], (N_CLUSTERS, NODES, 2, K, K), (2 * K) ** -0.5, 0.375, ((0, 8),), jnp.float32),
        "node_slot": jax.vmap(lambda own: jax.random.permutation(own, NODES))(jax.random.split(keys[4], N_CLUSTERS)).reshape((N_CLUSTERS, NODES)).astype(jnp.int32),
    }


full_precision = lax.Precision.HIGHEST

def orthonormal(tall_block):
    gram_matrix = jnp.einsum('...rk,...rj->...kj', tall_block, tall_block, precision=full_precision)
    lower_factor = jnp.linalg.cholesky(gram_matrix)
    flipped = jax.scipy.linalg.solve_triangular(lower_factor, jnp.swapaxes(tall_block, -1, -2), lower=True)
    return jnp.swapaxes(flipped, -1, -2)

def project(node_basis, target):
    return jnp.einsum('...rk,...rs->...ks', node_basis, target, precision=full_precision)

def reference(samples, probes, near_blocks, couplings, node_slot):
    leaves = samples.shape[0] // M
    sample_blocks = samples.reshape(leaves, M, S)
    probe_blocks = probes.reshape(leaves, M, S)
    near_split = near_blocks.reshape(leaves, M, 2, M)
    zeros_block = jnp.zeros((1, M, S), jnp.float32)
    diag_term = jnp.einsum('tmn,tns->tms', near_split[:, :, 0, :], probe_blocks, precision=full_precision)
    next_blocks = jnp.concatenate([probe_blocks[1:], zeros_block], axis=0)
    upper_term = jnp.einsum('tmn,tns->tms', near_split[:, :, 1, :], next_blocks, precision=full_precision)
    lower_prod = jnp.einsum('tnm,tns->tms', near_split[:, :, 1, :], probe_blocks, precision=full_precision)
    lower_term = jnp.concatenate([zeros_block, lower_prod[:-1]], axis=0)
    far_samples = sample_blocks - diag_term - upper_term - lower_term
    leaf_basis = orthonormal(far_samples[:, :, :K])
    sample_coef = project(leaf_basis, far_samples)
    probe_coef = project(leaf_basis, probe_blocks)
    ancestors = []
    for level_index in range(1, LEVELS + 1):
        children = sample_coef.shape[0]
        parents = children // 2
        zeros_coef = jnp.zeros((2, K, S), jnp.float32)
        left_far = jnp.concatenate([zeros_coef, probe_coef[:-2]], axis=0)
        right_far = jnp.concatenate([probe_coef[2:], zeros_coef], axis=0)
        parity = (jnp.arange(children) % 2)[:, None, None]
        main_far = jnp.where(parity == 0, left_far, right_far)
        other_far = jnp.where(parity == 0, right_far, left_far)
        per_tree = SUBTREE >> level_index
        parent_ids = jnp.arange(parents)
        subtree_index = parent_ids // per_tree
        node_index = SUBTREE - (SUBTREE >> level_index - 1) + parent_ids % per_tree
        slot_index = node_slot[subtree_index, node_index]
        chosen = couplings[subtree_index, slot_index]
        child_coupling = chosen.reshape(children, K, K)
        main_term = jnp.einsum('tij,tjs->tis', child_coupling, main_far, precision=full_precision)
        other_term = jnp.einsum('tji,tjs->tis', child_coupling, other_far, precision=full_precision)
        corrected = sample_coef - main_term - other_term
        stacked = corrected.reshape(parents, 2 * K, S)
        stacked_probes = probe_coef.reshape(parents, 2 * K, S)
        node_basis = orthonormal(stacked[:, :, :K])
        ancestors.append(jnp.repeat(node_basis, 2 ** level_index, axis=0))
        sample_coef = project(node_basis, stacked)
        probe_coef = project(node_basis, stacked_probes)
    transfer_bases = jnp.stack(ancestors, axis=1)
    return (leaf_basis.reshape(leaves * M, K), transfer_bases, sample_coef, probe_coef)
```

```python
import functools

import jax
import jax.numpy as jnp
from jax import lax
from jax.experimental import pallas as pl
from jax.experimental.pallas import tpu as pltpu
from jax.sharding import PartitionSpec as P

HIGHEST = lax.Precision.HIGHEST
ROWS = 8
GROUP = 4
BOTH = ("leaf", "clusters")


def dot(a, b, ca=1, cb=0):
    return lax.dot_general(
        a, b, (((ca,), (cb,)), ((), ())), precision=HIGHEST, preferred_element_type=jnp.float32
    )


def across_lanes(tile, lane):
    return jnp.broadcast_to(tile[:, lane : lane + 1], tile.shape)


def across_rows(tile, row):
    return jnp.broadcast_to(tile[row : row + 1, :], tile.shape)


def inverse_factor(gram):
    size = gram.shape[0]
    blocks = size // ROWS
    sub = lax.broadcasted_iota(jnp.int32, (ROWS, size), 0)
    lane = lax.broadcasted_iota(jnp.int32, (ROWS, size), 1)
    left = [gram[ROWS * i : ROWS * (i + 1), :] for i in range(blocks)]
    right = [jnp.where(lane == sub + ROWS * i, 1.0, 0.0).astype(jnp.float32) for i in range(blocks)]
    scaled = [None] * blocks
    for first in range(0, blocks, GROUP):
        last = first + GROUP
        scales = []
        for k in range(first, last):
            cols = {
                i: [across_lanes(left[i], ROWS * k + c) for c in range(ROWS)] for i in range(k, last)
            }
            pivots = jnp.ones((ROWS, size), jnp.float32)
            for j in range(ROWS):
                pivot = across_rows(cols[k][j], j)
                inverse = 1.0 / pivot
                pivots = jnp.where(sub == j, pivot, pivots)
                left_row = across_rows(left[k], j)
                right_row = across_rows(right[k], j)
                col_row = [across_rows(cols[k][c], j) for c in range(j + 1, ROWS)]
                for i in range(k, last):
                    if i == k and j == ROWS - 1:
                        continue
                    col = cols[i][j]
                    if i == k:
                        col = jnp.where(sub > j, col, 0.0)
                    factor = col * inverse
                    for c in range(j + 1, ROWS):
                        cols[i][c] = cols[i][c] - factor * col_row[c - j - 1]
                    left[i] = left[i] - factor * left_row
                    right[i] = right[i] - factor * right_row
            scales.append(lax.rsqrt(pivots))
        for k in range(first, last):
            scaled[k] = right[k] * scales[k - first]
        if last < blocks:
            upper = jnp.concatenate([left[k] * scales[k - first] for k in range(first, last)], axis=0)
            lower = jnp.concatenate(scaled[first:last], axis=0)
            change = dot(upper, jnp.concatenate([upper, lower], axis=1), 0, 0)
            for i in range(last, blocks):
                piece = change[ROWS * i : ROWS * (i + 1), :]
                left[i] = left[i] - piece[:, :size]
                right[i] = right[i] - piece[:, size:]
    return jnp.concatenate(scaled, axis=0)


def near_half(view, which, rows):
    chunks = rows // 128
    return jnp.concatenate(
        [view[pl.ds(2 * c + which, rows, stride=2 * chunks), :] for c in range(chunks)], axis=1
    )


def handed_first_kernel(near, probes, out):
    upper = near_half(near, 1, probes.shape[0])
    out[...] = dot(probes[:, : out.shape[1]].T, upper).T


def near_kernel(near, probes, samples, rest, handed):
    rows = probes.shape[0]
    half = handed.shape[1]
    upper = near_half(near, 1, rows)
    handed[...] = dot(probes[:, half:].T, upper).T
    diag = near_half(near, 0, rows)
    rest[...] = samples[...] - dot(diag, probes[...])


def leaf_kernel(near, rest, following, handed, probes, far, inverse, probe_coef, basis, sample_coef):
    columns = far.shape[1]
    upper = near_half(near, 1, rest.shape[0])
    block = rest[:, :columns] - dot(upper, following[...]) - handed[...]
    far[...] = block
    gram = dot(block, block, 0, 0)
    cross = dot(block, probes[...], 0, 0)
    factor = inverse_factor(gram)
    inverse[...] = factor
    probe_coef[...] = dot(factor, cross)
    sample_coef[...] = dot(factor, gram)
    basis[...] = dot(block, factor, 1, 1)


def second_kernel(near, rest, following, handed, basis, sample_coef):
    columns = handed.shape[1]
    upper = near_half(near, 1, rest.shape[0])
    block = rest[:, columns:] - dot(upper, following[...]) - handed[...]
    sample_coef[...] = dot(basis[...], block, 0, 0)


def coupling_kernel(where, couplings, main, other, out):
    block = couplings[where[0], where[1]]
    out[...] = dot(block, main[...]) + dot(block, other[...], 0, 0)


def corrected_kernel(where, couplings, main, other, coef, out):
    block = couplings[where[0], where[1]]
    out[...] = coef[...] - dot(block, main[...]) - dot(block, other[...], 0, 0)


def node_kernel(where, own, sibling, own_probes, sibling_probes, basis, sample_coef, probe_coef):
    size = own.shape[0]
    mine = own[...]
    theirs = sibling[...]
    gram_all = dot(mine[:, :size], mine, 0, 0) + dot(theirs[:, :size], theirs, 0, 0)
    cross = dot(mine[:, :size], own_probes[...], 0, 0) + dot(
        theirs[:, :size], sibling_probes[...], 0, 0
    )
    factor = inverse_factor(gram_all[:, :size])
    sample_coef[...] = dot(factor, gram_all)
    probe_coef[...] = dot(factor, cross)
    at = pl.multiple_of(where[1] * size, size)
    basis[pl.ds(at, size), :] = dot(mine[:, :size], factor, 1, 1)
    at = pl.multiple_of((1 - where[1]) * size, size)
    basis[pl.ds(at, size), :] = dot(theirs[:, :size], factor, 1, 1)


VMEM = pl.BlockSpec(memory_space=pltpu.VMEM)
SMEM = pl.BlockSpec(memory_space=pltpu.SMEM)


def call(kernel, shapes, *operands, scalars=0, flops=0):
    outs = [jax.ShapeDtypeStruct(shape, jnp.float32) for shape in shapes]
    specs = [SMEM] * scalars + [VMEM] * (len(operands) - scalars)
    moved = 4 * (sum(o.size for o in operands) + sum(o.size for o in outs))
    return pl.pallas_call(
        kernel,
        out_shape=outs,
        in_specs=specs,
        out_specs=[VMEM] * len(outs),
        compiler_params=pltpu.CompilerParams(vmem_limit_bytes=32 * 2**20),
        cost_estimate=pl.CostEstimate(flops=flops, bytes_accessed=moved, transcendentals=0),
    )(*operands)


def permuted(value, target):
    trees, subtree = lax.axis_size("clusters"), lax.axis_size("leaf")
    pairs = []
    for member in range(subtree):
        for tree in range(trees):
            to_tree, to_member = target(tree, member)
            if 0 <= to_tree < trees:
                pairs.append((member * trees + tree, to_member * trees + to_tree))
    return lax.ppermute(value, BOTH, pairs)


def flat_shift(value, by):
    subtree = lax.axis_size("leaf")
    return permuted(value, lambda tree, member: divmod(tree * subtree + member + by, subtree))


def tree_shift(value, by):
    peers = lax.axis_size("clusters")
    pairs = [(i, i + by) for i in range(peers) if 0 <= i + by < peers]
    return lax.ppermute(value, "clusters", pairs)


def swapped(value, mask):
    pairs = [(i, i ^ mask) for i in range(lax.axis_size("leaf"))]
    return lax.ppermute(value, "leaf", pairs)


def outward(value, half):
    return permuted(value, lambda tree, member: (tree - 1 if member < half else tree + 1, member))


def body(samples, probes, near_blocks, couplings, node_slot):
    rows, width = probes.shape
    columns = couplings.shape[-1]
    subtree = lax.axis_size("leaf")
    levels = subtree.bit_length() - 1
    member = lax.axis_index("leaf")
    chunks = rows // 128
    near = near_blocks.reshape(rows, 2, chunks, 128).transpose(0, 2, 1, 3).reshape(-1, 128)
    table = couplings[0]

    following = flat_shift(probes[:, :columns], -1)
    (handed,) = call(handed_first_kernel, [(rows, columns)], near, probes, flops=2 * rows * rows * columns)
    handed = flat_shift(handed, 1)
    rest, handed_2 = call(
        near_kernel, [(rows, width), (rows, width - columns)], near, probes, samples,
        flops=12 * rows * rows * width,
    )
    following_2 = flat_shift(probes[:, columns:], -1)
    handed_2 = flat_shift(handed_2, 1)
    far, inverse, probe_coef, leaf_basis, sample_first = call(
        leaf_kernel,
        [(rows, columns), (columns, columns), (columns, width), (rows, columns), (columns, columns)],
        near, rest, following, handed, probes, flops=10 * rows * rows * width,
    )
    (sample_last,) = call(
        second_kernel, [(columns, width - columns)], near, rest, following_2, handed_2, leaf_basis,
        flops=4 * rows * rows * width,
    )
    sample_coef = jnp.concatenate([sample_first, sample_last], axis=1)

    def place(level, node):
        index = subtree - (subtree >> level - 1) + (node >> 1)
        slot = lax.dynamic_index_in_dim(node_slot[0], index, 0, keepdims=False)
        return jnp.stack([slot, node & 1]).astype(jnp.int32)

    shape = (columns, width)
    ancestors = []
    for level in range(1, levels + 1):
        copies = 2 ** (level - 1)
        node = member // copies
        count = subtree // copies
        own_place = place(level, node)
        if count == 4:
            away = outward(probe_coef, 2 * copies)
            outer = (node == 0) | (node == 3)
            main = jnp.where(outer, probe_coef, away)
            other = jnp.where(outer, away, probe_coef)
            (term,) = call(coupling_kernel, [shape], place(level, node ^ 2), table, main, other, scalars=1)
            sibling_coef, sibling_probes = swapped((sample_coef, probe_coef), copies)
            own = sample_coef - swapped(term, 2 * copies)
            sibling = sibling_coef - swapped(term, 3 * copies)
        else:
            if count == 2:
                from_left, from_right = tree_shift(probe_coef, 1), tree_shift(probe_coef, -1)
            else:
                from_left = flat_shift(probe_coef, 2 * copies)
                from_right = flat_shift(probe_coef, -2 * copies)
            even = node & 1 == 0
            main = jnp.where(even, from_left, from_right)
            other = jnp.where(even, from_right, from_left)
            (own,) = call(
                corrected_kernel, [shape], own_place, table, main, other, sample_coef, scalars=1
            )
            sibling, sibling_probes = swapped((own, probe_coef), copies)
        basis, sample_coef, probe_coef = call(
            node_kernel, [(2 * columns, columns), shape, shape],
            own_place, own, sibling, probe_coef, sibling_probes, scalars=1,
        )
        ancestors.append(basis)
    transfer_bases = jnp.stack(ancestors, axis=0)[None]
    return (leaf_basis, transfer_bases, sample_coef[None], probe_coef[None])


def solution(mesh):
    in_specs = (
        P(("clusters", "leaf"), None),
        P(("clusters", "leaf"), None),
        P(("clusters", "leaf"), None, None),
        P("clusters", None, None, None, None),
        P("clusters", None),
    )
    out_specs = (
        P(("clusters", "leaf"), None),
        P(("clusters", "leaf"), None, None, None),
        P("clusters", None, None),
        P("clusters", None, None),
    )
    return jax.shard_map(body, mesh=mesh, in_specs=in_specs, out_specs=out_specs, check_vma=False)
```

```python
import functools

import jax
import jax.numpy as jnp
from jax import lax
from jax.experimental import pallas as pl
from jax.experimental.pallas import tpu as pltpu
from jax.sharding import PartitionSpec as P

HIGHEST = lax.Precision.HIGHEST
ROWS = 8
GROUP = 4
BOTH = ("leaf", "clusters")


def dot(a, b, ca=1, cb=0):
    return lax.dot_general(
        a, b, (((ca,), (cb,)), ((), ())), precision=HIGHEST, preferred_element_type=jnp.float32
    )


def across_lanes(tile, lane):
    return jnp.broadcast_to(tile[:, lane : lane + 1], tile.shape)


def across_rows(tile, row):
    return jnp.broadcast_to(tile[row : row + 1, :], tile.shape)


def inverse_factor(gram):
    size = gram.shape[0]
    blocks = size // ROWS
    sub = lax.broadcasted_iota(jnp.int32, (ROWS, size), 0)
    lane = lax.broadcasted_iota(jnp.int32, (ROWS, size), 1)
    left = [gram[ROWS * i : ROWS * (i + 1), :] for i in range(blocks)]
    right = [jnp.where(lane == sub + ROWS * i, 1.0, 0.0).astype(jnp.float32) for i in range(blocks)]
    scaled = [None] * blocks
    for first in range(0, blocks, GROUP):
        last = first + GROUP
        scales = []
        for k in range(first, last):
            cols = {
                i: [across_lanes(left[i], ROWS * k + c) for c in range(ROWS)] for i in range(k, last)
            }
            pivots = jnp.ones((ROWS, size), jnp.float32)
            for j in range(ROWS):
                pivot = across_rows(cols[k][j], j)
                inverse = 1.0 / pivot
                pivots = jnp.where(sub == j, pivot, pivots)
                left_row = across_rows(left[k], j)
                right_row = across_rows(right[k], j)
                col_row = [across_rows(cols[k][c], j) for c in range(j + 1, ROWS)]
                for i in range(k, last):
                    if i == k and j == ROWS - 1:
                        continue
                    col = cols[i][j]
                    if i == k:
                        col = jnp.where(sub > j, col, 0.0)
                    factor = col * inverse
                    for c in range(j + 1, ROWS):
                        cols[i][c] = cols[i][c] - factor * col_row[c - j - 1]
                    left[i] = left[i] - factor * left_row
                    right[i] = right[i] - factor * right_row
            scales.append(lax.rsqrt(pivots))
        for k in range(first, last):
            scaled[k] = right[k] * scales[k - first]
        if last < blocks:
            upper = jnp.concatenate([left[k] * scales[k - first] for k in range(first, last)], axis=0)
            lower = jnp.concatenate(scaled[first:last], axis=0)
            change = dot(upper, jnp.concatenate([upper, lower], axis=1), 0, 0)
            for i in range(last, blocks):
                piece = change[ROWS * i : ROWS * (i + 1), :]
                left[i] = left[i] - piece[:, :size]
                right[i] = right[i] - piece[:, size:]
    return jnp.concatenate(scaled, axis=0)


def near_half(view, which, rows):
    chunks = rows // 128
    return jnp.concatenate(
        [view[pl.ds(2 * c + which, rows, stride=2 * chunks), :] for c in range(chunks)], axis=1
    )


def handed_kernel(near, probes, first, last, probes_last):
    columns = first.shape[1]
    upper = near_half(near, 1, probes.shape[0])
    handed = dot(probes[...].T, upper).T
    first[...] = handed[:, :columns]
    last[...] = handed[:, columns:]
    probes_last[...] = probes[:, columns:]


def rest_kernel(near, probes, samples, rest):
    rest[...] = samples[...] - dot(near_half(near, 0, probes.shape[0]), probes[...])


def leaf_kernel(near, rest, following, handed, probes, far, inverse, sample_coef, probe_coef):
    columns = far.shape[1]
    upper = near_half(near, 1, rest.shape[0])
    block = rest[:, :columns] - dot(upper, following[...]) - handed[...]
    far[...] = block
    gram = dot(block, block, 0, 0)
    cross = dot(block, probes[...], 0, 0)
    factor = inverse_factor(gram)
    inverse[...] = factor
    probe_coef[...] = dot(factor, cross)
    sample_coef[...] = dot(factor, gram)


def leaf_last_kernel(near, rest, following, handed, far, inverse, basis, sample_coef):
    columns = far.shape[1]
    upper = near_half(near, 1, rest.shape[0])
    basis[...] = dot(far[...], inverse[...], 1, 1)
    block = rest[:, columns:] - dot(upper, following[...]) - handed[...]
    sample_coef[...] = dot(basis[...], block, 0, 0)


def coupling_of(slots, couplings, level, node):
    subtree = lax.axis_size("leaf")
    index = subtree - (subtree >> level - 1) + (node >> 1)
    return couplings[0, slots[0, index], node & 1]


def member_node(level):
    return lax.axis_index("leaf") >> level - 1


def term_kernel(level, slots, couplings, mine, away, out):
    node = member_node(level)
    block = coupling_of(slots, couplings, level, node ^ 2)
    outer = (node == 0) | (node == 3)
    main = jnp.where(outer, mine[...], away[...])
    other = jnp.where(outer, away[...], mine[...])
    out[...] = dot(block, main) + dot(block, other, 0, 0)


def corrected_kernel(level, slots, couplings, from_left, from_right, first, last, out_first, out_last):
    columns = first.shape[1]
    node = member_node(level)
    block = coupling_of(slots, couplings, level, node)
    even = node & 1 == 0
    main = jnp.where(even, from_left[...], from_right[...])
    other = jnp.where(even, from_right[...], from_left[...])
    term = dot(block, main) + dot(block, other, 0, 0)
    out_first[...] = first[...] - term[:, :columns]
    out_last[...] = last[...] - term[:, columns:]


def factor_kernel(level, mine, theirs, *refs):
    earlier, (inverse, bases) = refs[:-2], refs[-2:]
    for at, done in enumerate(earlier):
        bases[0, at] = done[0, 0]
    size = mine.shape[0]
    gram = dot(mine[...], mine[...], 0, 0) + dot(theirs[...], theirs[...], 0, 0)
    factor = inverse_factor(gram)
    inverse[...] = factor
    parity = member_node(level) & 1
    at = pl.multiple_of(parity * size, size)
    bases[0, len(earlier), pl.ds(at, size), :] = dot(mine[...], factor, 1, 1)
    at = pl.multiple_of((1 - parity) * size, size)
    bases[0, len(earlier), pl.ds(at, size), :] = dot(theirs[...], factor, 1, 1)


def node_kernel(inverse, mine, mine_last, mine_probes, theirs, theirs_last, theirs_probes, first, last, probe_coef):
    def both(own, sibling):
        return dot(mine[...], own[...], 0, 0) + dot(theirs[...], sibling[...], 0, 0)

    factor = inverse[...]
    probe_coef[...] = dot(factor, both(mine_probes, theirs_probes))
    first[...] = dot(factor, both(mine, theirs))
    last[...] = dot(factor, both(mine_last, theirs_last))


def top_kernel(inverse, mine, mine_last, mine_probes, theirs, theirs_last, theirs_probes, samples, probe_coef):
    size = mine.shape[0]

    def both(own, sibling):
        return dot(mine[...], own[...], 0, 0) + dot(theirs[...], sibling[...], 0, 0)

    factor = inverse[...]
    probe_coef[0] = dot(factor, both(mine_probes, theirs_probes))
    samples[0, :, :size] = dot(factor, both(mine, theirs))
    samples[0, :, size:] = dot(factor, both(mine_last, theirs_last))


VMEM = pl.BlockSpec(memory_space=pltpu.VMEM)
SMEM = pl.BlockSpec(memory_space=pltpu.SMEM)


def call(kernel, shapes, *operands, slots=None, flops=0):
    outs = [jax.ShapeDtypeStruct(shape, jnp.float32) for shape in shapes]
    specs = [VMEM] * len(operands)
    if slots is not None:
        operands = (slots,) + operands
        specs = [SMEM] + specs
    moved = 4 * (sum(o.size for o in operands) + sum(o.size for o in outs))
    return pl.pallas_call(
        kernel,
        out_shape=outs,
        in_specs=specs,
        out_specs=[VMEM] * len(outs),
        compiler_params=pltpu.CompilerParams(vmem_limit_bytes=32 * 2**20),
        cost_estimate=pl.CostEstimate(flops=flops, bytes_accessed=moved, transcendentals=0),
    )(*operands)


def permuted(value, target):
    trees, subtree = lax.axis_size("clusters"), lax.axis_size("leaf")
    pairs = []
    for member in range(subtree):
        for tree in range(trees):
            to_tree, to_member = target(tree, member)
            if 0 <= to_tree < trees:
                pairs.append((member * trees + tree, to_member * trees + to_tree))
    return lax.ppermute(value, BOTH, pairs)


def flat_shift(value, by):
    subtree = lax.axis_size("leaf")
    return permuted(value, lambda tree, member: divmod(tree * subtree + member + by, subtree))


def tree_shift(value, by):
    peers = lax.axis_size("clusters")
    pairs = [(i, i + by) for i in range(peers) if 0 <= i + by < peers]
    return lax.ppermute(value, "clusters", pairs)


def swapped(value, mask):
    pairs = [(i, i ^ mask) for i in range(lax.axis_size("leaf"))]
    return lax.ppermute(value, "leaf", pairs)


def outward(value, half):
    return permuted(value, lambda tree, member: (tree - 1 if member < half else tree + 1, member))


def body(samples, probes, near_blocks, couplings, node_slot):
    rows, width = probes.shape
    columns = couplings.shape[-1]
    subtree = lax.axis_size("leaf")
    levels = subtree.bit_length() - 1
    chunks = rows // 128
    near = near_blocks.reshape(rows, 2, chunks, 128).transpose(0, 2, 1, 3).reshape(-1, 128)
    work = 12 * rows * rows * width

    tall, tall_last = (rows, columns), (rows, width - columns)
    following = flat_shift(probes[:, :columns], -1)
    handed, handed_last, probes_last = call(
        handed_kernel, [tall, tall_last, tall_last], near, probes, flops=work
    )
    handed = flat_shift(handed, 1)
    handed_last = flat_shift(handed_last, 1)
    following_last = flat_shift(probes_last, -1)
    (rest,) = call(rest_kernel, [(rows, width)], near, probes, samples, flops=work)
    square, square_last, shape = (columns, columns), (columns, width - columns), (columns, width)
    far, inverse, first, probe_coef = call(
        leaf_kernel, [tall, square, square, shape], near, rest, following, handed, probes, flops=work
    )
    leaf_basis, last = call(
        leaf_last_kernel, [tall, square_last],
        near, rest, following_last, handed_last, far, inverse, flops=work,
    )

    ancestors = []
    for level in range(1, levels + 1):
        copies = 2 ** (level - 1)
        count = subtree // copies
        if count == 4:
            away = outward(probe_coef, 2 * copies)
            (term,) = call(
                functools.partial(term_kernel, level), [shape], couplings, probe_coef, away,
                slots=node_slot,
            )
            term = swapped(term, 2 * copies)
            first = first - term[:, :columns]
            last = last - term[:, columns:]
        else:
            if count == 2:
                from_left, from_right = tree_shift(probe_coef, 1), tree_shift(probe_coef, -1)
            else:
                from_left = flat_shift(probe_coef, 2 * copies)
                from_right = flat_shift(probe_coef, -2 * copies)
            first, last = call(
                functools.partial(corrected_kernel, level), [square, square_last],
                couplings, from_left, from_right, first, last, slots=node_slot,
            )
        mine = (first, last, probe_coef)
        theirs = tuple(swapped(value, copies) for value in mine)
        final = level == levels
        bases = (1, level if final else 1, 2 * columns, columns)
        inverse, basis = call(
            functools.partial(factor_kernel, level), [square, bases],
            mine[0], theirs[0], *(ancestors if final else []), flops=work,
        )
        ancestors.append(basis)
        if final:
            top_samples, top_probes = call(
                top_kernel, [(1,) + shape, (1,) + shape], inverse, *mine, *theirs
            )
        else:
            first, last, probe_coef = call(
                node_kernel, [square, square_last, shape], inverse, *mine, *theirs
            )
    return (leaf_basis, ancestors[-1], top_samples, top_probes)


def solution(mesh):
    in_specs = (
        P(("clusters", "leaf"), None),
        P(("clusters", "leaf"), None),
        P(("clusters", "leaf"), None, None),
        P("clusters", None, None, None, None),
        P("clusters", None),
    )
    out_specs = (
        P(("clusters", "leaf"), None),
        P(("clusters", "leaf"), None, None, None),
        P("clusters", None, None),
        P("clusters", None, None),
    )
    return jax.shard_map(body, mesh=mesh, in_specs=in_specs, out_specs=out_specs, check_vma=False)
```

```python
import functools

import jax
import jax.numpy as jnp
from jax import lax
from jax.experimental import pallas as pl
from jax.experimental.pallas import tpu as pltpu
from jax.sharding import PartitionSpec as P

HIGHEST = lax.Precision.HIGHEST
ROWS = 8
GROUP = 4
BOTH = ("leaf", "clusters")


def dot(a, b, ca=1, cb=0):
    return lax.dot_general(
        a, b, (((ca,), (cb,)), ((), ())), precision=HIGHEST, preferred_element_type=jnp.float32
    )


def across_lanes(tile, lane):
    return jnp.broadcast_to(tile[:, lane : lane + 1], tile.shape)


def across_rows(tile, row):
    return jnp.broadcast_to(tile[row : row + 1, :], tile.shape)


def inverse_factor(gram):
    size = gram.shape[0]
    blocks = size // ROWS
    sub = lax.broadcasted_iota(jnp.int32, (ROWS, size), 0)
    lane = lax.broadcasted_iota(jnp.int32, (ROWS, size), 1)
    left = [gram[ROWS * i : ROWS * (i + 1), :] for i in range(blocks)]
    right = [jnp.where(lane == sub + ROWS * i, 1.0, 0.0).astype(jnp.float32) for i in range(blocks)]
    scaled = [None] * blocks
    for first in range(0, blocks, GROUP):
        last = first + GROUP
        ahead = min(last + 1, blocks)
        scales = []
        for k in range(first, last):
            cols = {
                i: [across_lanes(left[i], ROWS * k + c) for c in range(ROWS)] for i in range(k, ahead)
            }
            pivots = jnp.ones((ROWS, size), jnp.float32)
            for j in range(0, ROWS, 2):
                a = across_rows(cols[k][j], j)
                b = across_rows(cols[k][j], j + 1)
                c = across_rows(cols[k][j + 1], j + 1)
                det = a * c - b * b
                inverse = 1.0 / det
                inverse_a = 1.0 / a
                ratio = b * inverse_a
                pivots = jnp.where(sub == j, a, jnp.where(sub == j + 1, det * inverse_a, pivots))
                left_rows = across_rows(left[k], j), across_rows(left[k], j + 1)
                right_rows = across_rows(right[k], j), across_rows(right[k], j + 1)
                col_rows = [
                    (across_rows(cols[k][n], j), across_rows(cols[k][n], j + 1))
                    for n in range(j + 2, ROWS)
                ]
                for i in range(k, ahead):
                    u, v = cols[i][j], cols[i][j + 1]
                    f = (u * c - v * b) * inverse
                    g = (v * a - u * b) * inverse
                    if i == k:
                        f = jnp.where(sub > j + 1, f, jnp.where(sub == j + 1, ratio, 0.0))
                        g = jnp.where(sub > j + 1, g, 0.0)
                    for n in range(j + 2, ROWS):
                        x, y = col_rows[n - j - 2]
                        cols[i][n] = cols[i][n] - (f * x + g * y)
                    left[i] = left[i] - (f * left_rows[0] + g * left_rows[1])
                    right[i] = right[i] - (f * right_rows[0] + g * right_rows[1])
            scales.append(lax.rsqrt(pivots))
        for k in range(first, last):
            scaled[k] = right[k] * scales[k - first]
        if ahead < blocks:
            upper = jnp.concatenate([left[k] * scales[k - first] for k in range(first, last)], axis=0)
            lower = jnp.concatenate(scaled[first:last], axis=0)
            change = dot(upper, jnp.concatenate([upper, lower], axis=1), 0, 0)
            for i in range(ahead, blocks):
                piece = change[ROWS * i : ROWS * (i + 1), :]
                left[i] = left[i] - piece[:, :size]
                right[i] = right[i] - piece[:, size:]
    return jnp.concatenate(scaled, axis=0)


def near_half(view, which, rows):
    chunks = rows // 128
    return jnp.concatenate(
        [view[pl.ds(2 * c + which, rows, stride=2 * chunks), :] for c in range(chunks)], axis=1
    )


def handed_kernel(near, probes, first):
    upper = near_half(near, 1, probes.shape[0])
    first[...] = dot(probes[:, : first.shape[1]].T, upper).T


def rest_kernel(near, probes, samples, rest, handed_last, probes_last):
    rows = probes.shape[0]
    columns = rest.shape[1] - probes_last.shape[1]
    probes_last[...] = probes[:, columns:]
    rest[...] = samples[...] - dot(near_half(near, 0, rows), probes[...])
    handed_last[...] = dot(probes[:, columns:].T, near_half(near, 1, rows)).T


def leaf_kernel(near, rest, following, handed, probes, far, inverse, sample_coef, probe_first, probe_last):
    columns = far.shape[1]
    upper = near_half(near, 1, rest.shape[0])
    block = rest[:, :columns] - dot(upper, following[...]) - handed[...]
    far[...] = block
    gram = dot(block, block, 0, 0)
    cross = dot(block, probes[...], 0, 0)
    factor = inverse_factor(gram)
    inverse[...] = factor
    coef = dot(factor, jnp.concatenate([cross, gram], axis=1))
    width = cross.shape[1]
    probe_first[...] = coef[:, :columns]
    probe_last[...] = coef[:, columns:width]
    sample_coef[...] = coef[:, width:]


def leaf_last_kernel(near, rest, following, handed, far, inverse, basis, sample_coef):
    columns = far.shape[1]
    upper = near_half(near, 1, rest.shape[0])
    basis[...] = dot(far[...], inverse[...], 1, 1)
    block = rest[:, columns:] - dot(upper, following[...]) - handed[...]
    sample_coef[...] = dot(basis[...], block, 0, 0)


def coupling_of(slots, couplings, level, node):
    subtree = lax.axis_size("leaf")
    index = subtree - (subtree >> level - 1) + (node >> 1)
    return couplings[0, slots[0, index], node & 1]


def member_node(level):
    return lax.axis_index("leaf") >> level - 1


def corrected_kernel(level, kind, slots, couplings, one, two, *refs):
    node = member_node(level)
    block = coupling_of(slots, couplings, level, node)
    if kind == "given":
        first_main = node >= 0
    elif kind == "quad":
        first_main = (node == 1) | (node == 2)
    else:
        first_main = (lax.axis_index("clusters") ^ node) & 1 == 1
    main = jnp.where(first_main, one[...], two[...])
    other = jnp.where(first_main, two[...], one[...])
    term = dot(block, main) + dot(block, other, 0, 0)
    half, at = len(refs) // 2, 0
    for coef, out in zip(refs[:half], refs[half:]):
        out[...] = coef[...] - term[:, at : at + out.shape[1]]
        at += out.shape[1]


def factor_kernel(level, mine, theirs, *refs):
    earlier, (inverse, bases) = refs[:-2], refs[-2:]
    for at, done in enumerate(earlier):
        bases[0, at] = done[0, 0]
    size = mine.shape[0]
    gram = dot(mine[...], mine[...], 0, 0) + dot(theirs[...], theirs[...], 0, 0)
    factor = inverse_factor(gram)
    inverse[...] = factor
    parity = member_node(level) & 1
    at = pl.multiple_of(parity * size, size)
    bases[0, len(earlier), pl.ds(at, size), :] = dot(mine[...], factor, 1, 1)
    at = pl.multiple_of((1 - parity) * size, size)
    bases[0, len(earlier), pl.ds(at, size), :] = dot(theirs[...], factor, 1, 1)


def level_coefs(refs):
    half = len(refs) // 2
    inverse = refs[0][...]
    mine, theirs = [ref[...] for ref in refs[1 : half + 1]], [ref[...] for ref in refs[half + 1 :]]
    own, sibling = jnp.concatenate(mine, axis=1), jnp.concatenate(theirs, axis=1)
    mine, theirs = mine[0], theirs[0]
    return dot(inverse, dot(mine, own, 0, 0) + dot(theirs, sibling, 0, 0))


def node_kernel(inputs, *refs):
    coef = level_coefs(refs[:inputs])
    at = 0
    for out in refs[inputs:]:
        out[...] = coef[:, at : at + out.shape[1]]
        at += out.shape[1]


def top_kernel(*refs):
    coef = level_coefs(refs[:-2])
    samples, probe_coef = refs[-2:]
    width = samples.shape[2]
    samples[0] = coef[:, :width]
    probe_coef[0] = coef[:, width:]


VMEM = pl.BlockSpec(memory_space=pltpu.VMEM)
SMEM = pl.BlockSpec(memory_space=pltpu.SMEM)


def call(kernel, shapes, *operands, slots=None, flops=0):
    outs = [jax.ShapeDtypeStruct(shape, jnp.float32) for shape in shapes]
    specs = [VMEM] * len(operands)
    if slots is not None:
        operands = (slots,) + operands
        specs = [SMEM] + specs
    moved = 4 * (sum(o.size for o in operands) + sum(o.size for o in outs))
    return pl.pallas_call(
        kernel,
        out_shape=outs,
        in_specs=specs,
        out_specs=[VMEM] * len(outs),
        compiler_params=pltpu.CompilerParams(vmem_limit_bytes=32 * 2**20),
        cost_estimate=pl.CostEstimate(flops=flops, bytes_accessed=moved, transcendentals=0),
    )(*operands)


def permuted(value, target):
    trees, subtree = lax.axis_size("clusters"), lax.axis_size("leaf")
    pairs = []
    for member in range(subtree):
        for tree in range(trees):
            to_tree, to_member = target(tree, member)
            if 0 <= to_tree < trees:
                pairs.append((member * trees + tree, to_member * trees + to_tree))
    return lax.ppermute(value, BOTH, pairs)


def flat_shift(value, by):
    subtree = lax.axis_size("leaf")
    return permuted(value, lambda tree, member: divmod(tree * subtree + member + by, subtree))


def swapped(value, mask):
    return permuted(value, lambda tree, member: (tree, member ^ mask))


def outer_swapped(value, half):
    return permuted(
        value, lambda tree, member: (tree - 1 if member < half else tree + 1, member ^ half)
    )


def tree_swapped(value, odd):
    return permuted(value, lambda tree, member: (tree + 1 if tree & 1 == odd else tree - 1, member))


def body(samples, probes, near_blocks, couplings, node_slot):
    rows, width = probes.shape
    columns = couplings.shape[-1]
    subtree = lax.axis_size("leaf")
    levels = subtree.bit_length() - 1
    chunks = rows // 128
    near = near_blocks.reshape(rows, 2, chunks, 128).transpose(0, 2, 1, 3).reshape(-1, 128)
    work = 12 * rows * rows * width

    tall, tall_last = (rows, columns), (rows, width - columns)
    following = flat_shift(probes[:, :columns], -1)
    (handed,) = call(handed_kernel, [tall], near, probes, flops=work)
    handed = flat_shift(handed, 1)
    rest, handed_last, probes_last = call(
        rest_kernel, [(rows, width), tall_last, tall_last], near, probes, samples, flops=work
    )
    handed_last = flat_shift(handed_last, 1)
    following_last = flat_shift(probes_last, -1)
    square, square_last = (columns, columns), (columns, width - columns)
    far, inverse, first, *probe_coefs = call(
        leaf_kernel, [tall, square, square, square, square_last],
        near, rest, following, handed, probes, flops=work,
    )
    leaf_basis, last = call(
        leaf_last_kernel, [tall, square_last],
        near, rest, following_last, handed_last, far, inverse, flops=work,
    )

    ancestors = []
    for level in range(1, levels + 1):
        copies = 2 ** (level - 1)
        count = subtree // copies
        if count == 2:
            meet = [functools.partial(tree_swapped, odd=odd) for odd in (0, 1)]
        elif count == 4:
            meet = [
                functools.partial(swapped, mask=2 * copies),
                functools.partial(outer_swapped, half=2 * copies),
            ]
        else:
            meet = [functools.partial(flat_shift, by=by) for by in (2 * copies, -2 * copies)]
        fields = [[go(coef) for go in meet] for coef in probe_coefs]
        if count > 4:
            even = (lax.axis_index("leaf") >> level - 1) & 1 == 0
            fields = [[jnp.where(even, *pair), jnp.where(even, *pair[::-1])] for pair in fields]
        kind = "given" if count > 4 else "quad" if count == 4 else "trees"
        correct = functools.partial(corrected_kernel, level, kind)
        if count == 2:
            first, last = call(
                correct, [square, square_last], couplings, *fields[0], first, last, slots=node_slot
            )
        else:
            (first,) = call(correct, [square], couplings, *fields[0], first, slots=node_slot)
            (last,) = call(correct, [square_last], couplings, *fields[1], last, slots=node_slot)
        mine = first, last, *probe_coefs
        theirs = [swapped(value, copies) for value in mine]
        final = level == levels
        bases = (1, level if final else 1, 2 * columns, columns)
        inverse, basis = call(
            functools.partial(factor_kernel, level), [square, bases],
            mine[0], theirs[0], *(ancestors if final else []), flops=work,
        )
        ancestors.append(basis)
        if final:
            top_samples, top_probes = call(
                top_kernel, [(1, columns, width), (1, columns, width)], inverse, *mine, *theirs
            )
        else:
            pieces = [(columns, width)] if count == 4 else [square, square_last]
            first, last, *probe_coefs = call(
                functools.partial(node_kernel, 1 + 2 * len(mine)),
                [square, square_last, *pieces], inverse, *mine, *theirs,
            )
    return (leaf_basis, ancestors[-1], top_samples, top_probes)


def solution(mesh):
    in_specs = (
        P(("clusters", "leaf"), None),
        P(("clusters", "leaf"), None),
        P(("clusters", "leaf"), None, None),
        P("clusters", None, None, None, None),
        P("clusters", None),
    )
    out_specs = (
        P(("clusters", "leaf"), None),
        P(("clusters", "leaf"), None, None, None),
        P("clusters", None, None),
        P("clusters", None, None),
    )
    return jax.shard_map(body, mesh=mesh, in_specs=in_specs, out_specs=out_specs, check_vma=False)
```

```python
import functools

import jax
import jax.numpy as jnp
from jax import lax
from jax.experimental import pallas as pl
from jax.experimental.pallas import tpu as pltpu
from jax.sharding import PartitionSpec as P

HIGHEST = lax.Precision.HIGHEST
ROWS = 8
GROUP = 4
BOTH = ("leaf", "clusters")


def dot(a, b, ca=1, cb=0):
    return lax.dot_general(
        a, b, (((ca,), (cb,)), ((), ())), precision=HIGHEST, preferred_element_type=jnp.float32
    )


def across_lanes(tile, lane):
    return jnp.broadcast_to(tile[:, lane : lane + 1], tile.shape)


def across_rows(tile, row):
    return jnp.broadcast_to(tile[row : row + 1, :], tile.shape)


def inverse_factor(gram):
    size = gram.shape[0]
    blocks = size // ROWS
    sub = lax.broadcasted_iota(jnp.int32, (ROWS, size), 0)
    lane = lax.broadcasted_iota(jnp.int32, (ROWS, size), 1)
    left = [gram[ROWS * i : ROWS * (i + 1), :] for i in range(blocks)]
    right = [jnp.where(lane == sub + ROWS * i, 1.0, 0.0).astype(jnp.float32) for i in range(blocks)]
    scaled = [None] * blocks
    for first in range(0, blocks, GROUP):
        last = first + GROUP
        ahead = min(last + 1, blocks)
        scales = []
        for k in range(first, last):
            cols = {
                i: [across_lanes(left[i], ROWS * k + c) for c in range(ROWS)] for i in range(k, ahead)
            }
            pivots = jnp.ones((ROWS, size), jnp.float32)
            for j in range(0, ROWS, 2):
                a = across_rows(cols[k][j], j)
                b = across_rows(cols[k][j], j + 1)
                c = across_rows(cols[k][j + 1], j + 1)
                det = a * c - b * b
                inverse = 1.0 / det
                inverse_a = 1.0 / a
                ratio = b * inverse_a
                pivots = jnp.where(sub == j, a, jnp.where(sub == j + 1, det * inverse_a, pivots))
                left_rows = across_rows(left[k], j), across_rows(left[k], j + 1)
                right_rows = across_rows(right[k], j), across_rows(right[k], j + 1)
                col_rows = [
                    (across_rows(cols[k][n], j), across_rows(cols[k][n], j + 1))
                    for n in range(j + 2, ROWS)
                ]
                for i in range(k, ahead):
                    u, v = cols[i][j], cols[i][j + 1]
                    f = (u * c - v * b) * inverse
                    g = (v * a - u * b) * inverse
                    if i == k:
                        f = jnp.where(sub > j + 1, f, jnp.where(sub == j + 1, ratio, 0.0))
                        g = jnp.where(sub > j + 1, g, 0.0)
                    for n in range(j + 2, ROWS):
                        x, y = col_rows[n - j - 2]
                        cols[i][n] = cols[i][n] - (f * x + g * y)
                    left[i] = left[i] - (f * left_rows[0] + g * left_rows[1])
                    right[i] = right[i] - (f * right_rows[0] + g * right_rows[1])
            scales.append(lax.rsqrt(pivots))
        for k in range(first, last):
            scaled[k] = right[k] * scales[k - first]
        if ahead < blocks:
            upper = jnp.concatenate([left[k] * scales[k - first] for k in range(first, last)], axis=0)
            lower = jnp.concatenate(scaled[first:last], axis=0)
            change = dot(upper, jnp.concatenate([upper, lower], axis=1), 0, 0)
            for i in range(ahead, blocks):
                piece = change[ROWS * i : ROWS * (i + 1), :]
                left[i] = left[i] - piece[:, :size]
                right[i] = right[i] - piece[:, size:]
    return jnp.concatenate(scaled, axis=0)


def near_half(view, which, rows, chunks=None):
    chunks = rows // 128 if chunks is None else chunks
    return jnp.concatenate(
        [view[pl.ds(2 * c + which, rows, stride=2 * chunks), :] for c in range(chunks)], axis=1
    )


def handed_kernel(near, probes, handed, probes_first, near_copy, arrived):
    rows, columns = handed.shape
    chunks = rows // 128
    part = near.shape[0] // chunks
    coming = [pltpu.make_async_copy(probes.at[:, pl.ds(0, columns)], probes_first, arrived.at[chunks])]
    for c in range(chunks):
        at = pl.ds(c * part, part)
        coming.append(pltpu.make_async_copy(near.at[at, :], near_copy.at[at, :], arrived.at[c]))
    for copy in coming:
        copy.start()
    coming[0].wait()
    total = jnp.zeros((columns, rows), jnp.float32)
    for c in range(chunks):
        coming[c + 1].wait()
        upper = near_half(near_copy.at[pl.ds(c * part, part), :], 1, 128, chunks)
        total += dot(probes_first[128 * c : 128 * (c + 1), :].T, upper)
    handed[...] = total.T


def rest_kernel(near, probes, samples, rest, handed_last, probes_last):
    rows = probes.shape[0]
    columns = rest.shape[1] - probes_last.shape[1]
    probes_last[...] = probes[:, columns:]
    rest[...] = samples[...] - dot(near_half(near, 0, rows), probes[...])
    handed_last[...] = dot(probes[:, columns:].T, near_half(near, 1, rows)).T


def following_kernel(near, rest, following, handed_last, probes_last, out, *passed):
    columns = out.shape[1]
    out[...] = rest[:, :columns] - dot(near_half(near, 1, rest.shape[0]), following[...])


def leaf_kernel(rest, handed, probes, far, inverse, sample_coef, probe_coef):
    columns = far.shape[1]
    block = rest[...] - handed[...]
    far[...] = block
    gram = dot(block, block, 0, 0)
    cross = dot(block, probes[...], 0, 0)
    factor = inverse_factor(gram)
    inverse[...] = factor
    coef = dot(factor, jnp.concatenate([gram, cross], axis=1))
    sample_coef[...] = coef[:, :columns]
    probe_coef[...] = coef[:, columns:]


def leaf_last_kernel(near, rest, following, handed, far, inverse, basis, sample_coef):
    columns = far.shape[1]
    upper = near_half(near, 1, rest.shape[0])
    basis[...] = dot(far[...], inverse[...], 1, 1)
    block = rest[:, columns:] - dot(upper, following[...]) - handed[...]
    sample_coef[...] = dot(basis[...], block, 0, 0)


def coupling_of(slots, couplings, level, node):
    subtree = lax.axis_size("leaf")
    index = subtree - (subtree >> level - 1) + (node >> 1)
    return couplings[0, slots[0, index], node & 1]


def member_node(level):
    return lax.axis_index("leaf") >> level - 1


def term_kernel(level, slots, couplings, mine, away, first, last):
    node = member_node(level)
    block = coupling_of(slots, couplings, level, node ^ 2)
    outer = (node == 0) | (node == 3)
    main = jnp.where(outer, mine[...], away[...])
    other = jnp.where(outer, away[...], mine[...])
    term = dot(block, main) + dot(block, other, 0, 0)
    first[...] = term[:, : first.shape[1]]
    last[...] = term[:, first.shape[1] :]


def corrected_kernel(level, trees, slots, couplings, one, two, first, last, out_first, out_last):
    columns = first.shape[1]
    node = member_node(level)
    block = coupling_of(slots, couplings, level, node)
    main, other = one[...], two[...]
    if trees:
        straight = (lax.axis_index("clusters") ^ node) & 1 == 1
        main, other = jnp.where(straight, main, other), jnp.where(straight, other, main)
    term = dot(block, main) + dot(block, other, 0, 0)
    out_first[...] = first[...] - term[:, :columns]
    out_last[...] = last[...] - term[:, columns:]


def factor_kernel(mine, theirs, inverse):
    gram = dot(mine[...], mine[...], 0, 0) + dot(theirs[...], theirs[...], 0, 0)
    inverse[...] = inverse_factor(gram)


def write_basis(level, at, mine, theirs, inverse, bases):
    size = mine.shape[0]
    own = (lax.axis_index("leaf") >> level - 1) & 1
    for block, half in ((mine, own), (theirs, 1 - own)):
        rows = pl.ds(pl.multiple_of(half * size, size), size)
        bases[0, at, rows, :] = dot(block, inverse, 1, 1)


def basis_kernel(level, inverse, mine, theirs, basis):
    write_basis(level, 0, mine[...], theirs[...], inverse[...], basis)


def level_coefs(inverse, mine, theirs):
    own = jnp.concatenate([ref[...] for ref in mine], axis=1)
    sibling = jnp.concatenate([ref[...] for ref in theirs], axis=1)
    return dot(inverse, dot(mine[0][...], own, 0, 0) + dot(theirs[0][...], sibling, 0, 0))


def node_kernel(inverse, *refs):
    coef = level_coefs(inverse[...], refs[:3], refs[3:6])
    at = 0
    for out in refs[6:]:
        out[...] = coef[:, at : at + out.shape[1]]
        at += out.shape[1]


def top_kernel(level, inverse, *refs):
    factor = inverse[...]
    earlier, (bases, samples, probe_coef) = refs[6:-3], refs[-3:]
    coef = level_coefs(factor, refs[:3], refs[3:6])
    width = samples.shape[2]
    samples[0] = coef[:, :width]
    probe_coef[0] = coef[:, width:]
    for at, done in enumerate(earlier):
        bases[0, at] = done[0, 0]
    write_basis(level, len(earlier), refs[0][...], refs[3][...], factor, bases)


VMEM = pl.BlockSpec(memory_space=pltpu.VMEM)
SMEM = pl.BlockSpec(memory_space=pltpu.SMEM)
HBM = pl.BlockSpec(memory_space=pltpu.HBM)
ANY = pl.BlockSpec(memory_space=pl.ANY)


def call(kernel, shapes, *operands, slots=None, flops=0, specs=None, out_specs=None, **options):
    outs = [jax.ShapeDtypeStruct(shape, jnp.float32) for shape in shapes]
    specs = [VMEM] * len(operands) if specs is None else specs
    out_specs = [VMEM] * len(outs) if out_specs is None else out_specs
    if slots is not None:
        operands = (slots,) + operands
        specs = [SMEM] + specs
    moved = 4 * (sum(o.size for o in operands) + sum(o.size for o in outs))
    return pl.pallas_call(
        kernel,
        out_shape=outs,
        in_specs=specs,
        out_specs=out_specs,
        compiler_params=pltpu.CompilerParams(vmem_limit_bytes=32 * 2**20),
        cost_estimate=pl.CostEstimate(flops=flops, bytes_accessed=moved, transcendentals=0),
        **options,
    )(*operands)


def permuted(value, target):
    trees, subtree = lax.axis_size("clusters"), lax.axis_size("leaf")
    pairs = []
    for member in range(subtree):
        for tree in range(trees):
            to_tree, to_member = target(tree, member)
            if 0 <= to_tree < trees:
                pairs.append((member * trees + tree, to_member * trees + to_tree))
    return lax.ppermute(value, BOTH, pairs)


def flat_shift(value, by):
    subtree = lax.axis_size("leaf")
    return permuted(value, lambda tree, member: divmod(tree * subtree + member + by, subtree))


def swapped(value, mask):
    return permuted(value, lambda tree, member: (tree, member ^ mask))


def outward(value, half):
    return permuted(value, lambda tree, member: (tree - 1 if member < half else tree + 1, member))


def tree_swapped(value, odd):
    return permuted(value, lambda tree, member: (tree + 1 if tree & 1 == odd else tree - 1, member))


def body(samples, probes, near_blocks, couplings, node_slot):
    rows, width = probes.shape
    columns = couplings.shape[-1]
    subtree = lax.axis_size("leaf")
    levels = subtree.bit_length() - 1
    chunks = rows // 128
    near = near_blocks.reshape(rows, 2, chunks, 128).transpose(0, 2, 1, 3).reshape(-1, 128)
    work = 12 * rows * rows * width
    tall, tall_last = (rows, columns), (rows, width - columns)
    square, square_last = (columns, columns), (columns, width - columns)

    handed, probes_first = call(
        handed_kernel, [tall, tall], near, probes, flops=work, specs=[HBM, HBM],
        scratch_shapes=[pltpu.VMEM(near.shape, jnp.float32), pltpu.SemaphoreType.DMA((chunks + 1,))],
    )
    following = flat_shift(probes_first, -1)
    handed = flat_shift(handed, 1)
    rest, handed_last, probes_last = call(
        rest_kernel, [(rows, width), tall_last, tall_last], near, probes, samples, flops=work
    )
    rest_first, handed_last, probes_last = call(
        following_kernel, [tall, tall_last, tall_last],
        near, rest, following, handed_last, probes_last, flops=work,
        specs=[VMEM, VMEM, VMEM, ANY, ANY], out_specs=[VMEM, ANY, ANY],
        input_output_aliases={3: 1, 4: 2},
    )
    following_last = flat_shift(probes_last, -1)
    handed_last = flat_shift(handed_last, 1)
    far, inverse, first, probe_coef = call(
        leaf_kernel, [tall, square, square, (columns, width)], rest_first, handed, probes, flops=work
    )
    leaf_basis, last = call(
        leaf_last_kernel, [tall, square_last],
        near, rest, following_last, handed_last, far, inverse, flops=work,
    )

    ancestors = []
    for level in range(1, levels + 1):
        copies = 2 ** (level - 1)
        count = subtree // copies
        theirs_probe = swapped(probe_coef, copies)
        if count == 4:
            away = outward(probe_coef, 2 * copies)
            terms = call(
                functools.partial(term_kernel, level), [square, square_last],
                couplings, probe_coef, away, slots=node_slot,
            )
            first = first - swapped(terms[0], 2 * copies)
            last = last - swapped(terms[1], 2 * copies)
        else:
            if count == 2:
                fields = [tree_swapped(probe_coef, odd) for odd in (0, 1)]
            else:
                even = (lax.axis_index("leaf") >> level - 1) & 1 == 0
                fields = [flat_shift(probe_coef, by) for by in (2 * copies, -2 * copies)]
                fields = [jnp.where(even, *fields), jnp.where(even, *fields[::-1])]
            first, last = call(
                functools.partial(corrected_kernel, level, count == 2), [square, square_last],
                couplings, *fields, first, last, slots=node_slot,
            )
        mine = first, last, probe_coef
        theirs = swapped(first, copies), swapped(last, copies), theirs_probe
        (inverse,) = call(factor_kernel, [square], mine[0], theirs[0])
        if level < levels:
            ancestors += call(
                functools.partial(basis_kernel, level), [(1, 1, 2 * columns, columns)],
                inverse, mine[0], theirs[0],
            )
            first, last, probe_coef = call(
                node_kernel, [square, square_last, (columns, width)], inverse, *mine, *theirs
            )
    transfer_bases, top_samples, top_probes = call(
        functools.partial(top_kernel, levels),
        [(1, levels, 2 * columns, columns), (1, columns, width), (1, columns, width)],
        inverse, *mine, *theirs, *ancestors,
    )
    return (leaf_basis, transfer_bases, top_samples, top_probes)


def solution(mesh):
    in_specs = (
        P(("clusters", "leaf"), None),
        P(("clusters", "leaf"), None),
        P(("clusters", "leaf"), None, None),
        P("clusters", None, None, None, None),
        P("clusters", None),
    )
    out_specs = (
        P(("clusters", "leaf"), None),
        P(("clusters", "leaf"), None, None, None),
        P("clusters", None, None),
        P("clusters", None, None),
    )
    return jax.shard_map(body, mesh=mesh, in_specs=in_specs, out_specs=out_specs, check_vma=False)
```

```python
import functools

import jax
import jax.numpy as jnp
from jax import lax
from jax.experimental import pallas as pl
from jax.experimental.pallas import tpu as pltpu
from jax.sharding import PartitionSpec as P

HIGHEST = lax.Precision.HIGHEST
ROWS = 8
GROUP = 4
BOTH = ("leaf", "clusters")


def dot(a, b, ca=1, cb=0):
    return lax.dot_general(
        a, b, (((ca,), (cb,)), ((), ())), precision=HIGHEST, preferred_element_type=jnp.float32
    )


def across_lanes(tile, lane):
    return jnp.broadcast_to(tile[:, lane : lane + 1], tile.shape)


def row_of(ref, row):
    return jnp.broadcast_to(ref[pl.ds(row, 1), :], (ROWS, ref.shape[1]))


def inverse_factor(gram, scratch):
    size = gram.shape[0]
    blocks = size // ROWS
    sub = lax.broadcasted_iota(jnp.int32, (ROWS, size), 0)
    lane = lax.broadcasted_iota(jnp.int32, (ROWS, size), 1)
    rows = [gram[ROWS * i : ROWS * (i + 1), :] for i in range(blocks)]
    scaled = [None] * blocks
    used = 0
    for first in range(0, blocks, GROUP):
        last = first + GROUP
        ahead = min(last + 1, blocks)
        for k in range(first, last):
            cols = {
                i: [across_lanes(rows[i], ROWS * k + c) for c in range(ROWS)] for i in range(k, ahead)
            }
            pivots = jnp.ones((ROWS, size), jnp.float32)
            for j in range(0, ROWS, 2):
                pair = (lane == ROWS * k + j) | (lane == ROWS * k + j + 1)
                for i in range(k, ahead):
                    rows[i] = jnp.where(pair, 0.0, rows[i])
                rows[k] = jnp.where(pair & (lane == sub + ROWS * k), 1.0, rows[k])
                held = scratch.at[pl.ds(used, ROWS * (ROWS - j + 1)), :]
                used += ROWS * (ROWS - j + 1)
                held[pl.ds(0, ROWS), :] = rows[k]
                for n in range(j, ROWS):
                    held[pl.ds(ROWS * (n - j + 1), ROWS), :] = cols[k][n]
                a = row_of(held, ROWS + j)
                b = row_of(held, ROWS + j + 1)
                c = row_of(held, 2 * ROWS + j + 1)
                det = a * c - b * b
                inverse = 1.0 / det
                inverse_a = 1.0 / a
                ratio = b * inverse_a
                pivots = jnp.where(sub == j, a, jnp.where(sub == j + 1, det * inverse_a, pivots))
                row, next_row = row_of(held, j), row_of(held, j + 1)
                col_rows = [
                    (row_of(held, ROWS * (n - j + 1) + j), row_of(held, ROWS * (n - j + 1) + j + 1))
                    for n in range(j + 2, ROWS)
                ]
                for i in range(k, ahead):
                    u, v = cols[i][j], cols[i][j + 1]
                    f = (u * c - v * b) * inverse
                    g = (v * a - u * b) * inverse
                    if i == k:
                        f = jnp.where(sub > j + 1, f, jnp.where(sub == j + 1, ratio, 0.0))
                        g = jnp.where(sub > j + 1, g, 0.0)
                    for n in range(j + 2, ROWS):
                        x, y = col_rows[n - j - 2]
                        cols[i][n] = cols[i][n] - (f * x + g * y)
                    rows[i] = rows[i] - (f * row + g * next_row)
            kept = (lane <= sub + ROWS * k) | (lane >= ROWS * last)
            scaled[k] = jnp.where(kept, rows[k] * lax.rsqrt(pivots), 0.0)
        if ahead < blocks:
            done = jnp.concatenate(scaled[first:last], axis=0)
            change = dot(done.T[ROWS * ahead :, :], done)
            old = (lane >= ROWS * first) & (lane < ROWS * last)
            for i in range(ahead, blocks):
                piece = change[ROWS * (i - ahead) : ROWS * (i - ahead + 1), :]
                rows[i] = jnp.where(old, 0.0, rows[i]) - piece
    return jnp.concatenate(
        [jnp.where(lane <= sub + ROWS * k, scaled[k], 0.0) for k in range(blocks)], axis=0
    )


def scratch_rows(size):
    return size // ROWS * sum(ROWS * (ROWS - j + 1) for j in range(0, ROWS, 2))


def near_half(view, which, rows, chunks=None):
    chunks = rows // 128 if chunks is None else chunks
    return jnp.concatenate(
        [view[pl.ds(2 * c + which, rows, stride=2 * chunks), :] for c in range(chunks)], axis=1
    )


def handed_kernel(near, probes, first, last, probes_first, probes_last, near_copy, arrived):
    rows, columns = first.shape
    chunks = rows // 128
    part = near.shape[0] // chunks
    coming = [
        pltpu.make_async_copy(probes.at[:, pl.ds(0, columns)], probes_first, arrived.at[chunks]),
        pltpu.make_async_copy(
            probes.at[:, pl.ds(columns, probes_last.shape[1])], probes_last, arrived.at[chunks + 1]
        ),
    ]
    for c in range(chunks):
        at = pl.ds(c * part, part)
        coming.append(pltpu.make_async_copy(near.at[at, :], near_copy.at[at, :], arrived.at[c]))
    for copy in coming:
        copy.start()
    coming[0].wait()
    coming[1].wait()
    total = jnp.zeros((columns + probes_last.shape[1], rows), jnp.float32)
    for c in range(chunks):
        coming[c + 2].wait()
        upper = near_half(near_copy.at[pl.ds(c * part, part), :], 1, 128, chunks)
        at = pl.ds(128 * c, 128)
        piece = jnp.concatenate([probes_first[at, :], probes_last[at, :]], axis=1)
        total += dot(piece.T, upper)
    first[...] = total[:columns].T
    last[...] = total[columns:].T


def rest_kernel(near, probes, samples, rest):
    rest[...] = samples[...] - dot(near_half(near, 0, probes.shape[0]), probes[...])


def following_kernel(near, rest, following, out):
    columns = out.shape[1]
    out[...] = rest[:, :columns] - dot(near_half(near, 1, rest.shape[0]), following[...])


def leaf_kernel(rest, handed, probes, far, inverse, sample_coef, probe_coef, scratch):
    columns = far.shape[1]
    block = rest[...] - handed[...]
    far[...] = block
    gram = dot(block, block, 0, 0)
    cross = dot(block, probes[...], 0, 0)
    factor = inverse_factor(gram, scratch)
    inverse[...] = factor
    coef = dot(factor, jnp.concatenate([gram, cross], axis=1))
    sample_coef[...] = coef[:, :columns]
    probe_coef[...] = coef[:, columns:]


def leaf_last_kernel(near, rest, following, handed, far, inverse, basis, sample_coef):
    columns = far.shape[1]
    upper = near_half(near, 1, rest.shape[0])
    basis[...] = dot(far[...], inverse[...], 1, 1)
    block = rest[:, columns:] - dot(upper, following[...]) - handed[...]
    sample_coef[...] = dot(basis[...], block, 0, 0)


def coupling_of(slots, couplings, level, node):
    subtree = lax.axis_size("leaf")
    index = subtree - (subtree >> level - 1) + (node >> 1)
    return couplings[0, slots[0, index], node & 1]


def member_node(level):
    return lax.axis_index("leaf") >> level - 1


def term_kernel(level, slots, couplings, mine, away, unused, first, last):
    node = member_node(level)
    block = coupling_of(slots, couplings, level, node ^ 2)
    outer = (node == 0) | (node == 3)
    main = jnp.where(outer, mine[...], away[...])
    other = jnp.where(outer, away[...], mine[...])
    term = dot(block, main) + dot(block, other, 0, 0)
    first[...] = term[:, : first.shape[1]]
    last[...] = term[:, first.shape[1] :]


def corrected_kernel(level, trees, slots, couplings, one, two, first, last, out_first, out_last):
    columns = first.shape[1]
    node = member_node(level)
    block = coupling_of(slots, couplings, level, node)
    main, other = one[...], two[...]
    if trees:
        straight = (lax.axis_index("clusters") ^ node) & 1 == 1
        main, other = jnp.where(straight, main, other), jnp.where(straight, other, main)
    term = dot(block, main) + dot(block, other, 0, 0)
    out_first[...] = first[...] - term[:, :columns]
    out_last[...] = last[...] - term[:, columns:]


def factor_kernel(mine, theirs, inverse, scratch):
    gram = dot(mine[...], mine[...], 0, 0) + dot(theirs[...], theirs[...], 0, 0)
    inverse[...] = inverse_factor(gram, scratch)


def write_basis(level, at, mine, theirs, inverse, bases):
    size = mine.shape[0]
    own = (lax.axis_index("leaf") >> level - 1) & 1
    for block, half in ((mine, own), (theirs, 1 - own)):
        rows = pl.ds(pl.multiple_of(half * size, size), size)
        bases[0, at, rows, :] = dot(block, inverse, 1, 1)


def basis_kernel(level, inverse, mine, theirs, basis):
    write_basis(level, 0, mine[...], theirs[...], inverse[...], basis)


def level_coefs(inverse, mine, theirs):
    own = jnp.concatenate([ref[...] for ref in mine], axis=1)
    sibling = jnp.concatenate([ref[...] for ref in theirs], axis=1)
    return dot(inverse, dot(mine[0][...], own, 0, 0) + dot(theirs[0][...], sibling, 0, 0))


def node_kernel(inverse, *refs):
    coef = level_coefs(inverse[...], refs[:3], refs[3:6])
    at = 0
    for out in refs[6:]:
        out[...] = coef[:, at : at + out.shape[1]]
        at += out.shape[1]


def top_kernel(level, inverse, *refs):
    factor = inverse[...]
    earlier, (bases, samples, probe_coef) = refs[6:-3], refs[-3:]
    coef = level_coefs(factor, refs[:3], refs[3:6])
    width = samples.shape[2]
    samples[0] = coef[:, :width]
    probe_coef[0] = coef[:, width:]
    for at, done in enumerate(earlier):
        bases[0, at] = done[0, 0]
    write_basis(level, len(earlier), refs[0][...], refs[3][...], factor, bases)


VMEM = pl.BlockSpec(memory_space=pltpu.VMEM)
SMEM = pl.BlockSpec(memory_space=pltpu.SMEM)
ANY = pl.BlockSpec(memory_space=pl.ANY)


def call(kernel, shapes, *operands, slots=None, flops=0, specs=None, out_specs=None, vmem=32, **options):
    outs = [jax.ShapeDtypeStruct(shape, jnp.float32) for shape in shapes]
    specs = [VMEM] * len(operands) if specs is None else specs
    out_specs = [VMEM] * len(outs) if out_specs is None else out_specs
    if slots is not None:
        operands = (slots,) + operands
        specs = [SMEM] + specs
    moved = 4 * (sum(o.size for o in operands) + sum(o.size for o in outs))
    return pl.pallas_call(
        kernel,
        out_shape=outs,
        in_specs=specs,
        out_specs=out_specs,
        compiler_params=pltpu.CompilerParams(vmem_limit_bytes=vmem * 2**20),
        cost_estimate=pl.CostEstimate(flops=flops, bytes_accessed=moved, transcendentals=0),
        **options,
    )(*operands)


def permuted(value, target):
    trees, subtree = lax.axis_size("clusters"), lax.axis_size("leaf")
    pairs = []
    for member in range(subtree):
        for tree in range(trees):
            to_tree, to_member = target(tree, member)
            if 0 <= to_tree < trees:
                pairs.append((member * trees + tree, to_member * trees + to_tree))
    return lax.ppermute(value, BOTH, pairs)


def flat_shift(value, by):
    subtree = lax.axis_size("leaf")
    return permuted(value, lambda tree, member: divmod(tree * subtree + member + by, subtree))


def swapped(value, mask):
    return permuted(value, lambda tree, member: (tree, member ^ mask))


def outward(value, half):
    return permuted(value, lambda tree, member: (tree - 1 if member < half else tree + 1, member))


def tree_swapped(value, odd):
    return permuted(value, lambda tree, member: (tree + 1 if tree & 1 == odd else tree - 1, member))


def body(samples, probes, near_blocks, couplings, node_slot):
    rows, width = probes.shape
    columns = couplings.shape[-1]
    subtree = lax.axis_size("leaf")
    levels = subtree.bit_length() - 1
    chunks = rows // 128
    near = near_blocks.reshape(rows, 2, chunks, 128).transpose(0, 2, 1, 3).reshape(-1, 128)
    work = 12 * rows * rows * width
    tall, tall_last = (rows, columns), (rows, width - columns)
    square, square_last = (columns, columns), (columns, width - columns)

    handed, handed_last, probes_first, probes_last = call(
        handed_kernel, [tall, tall_last, tall, tall_last], near, probes, flops=work,
        specs=[ANY, ANY], vmem=62,
        scratch_shapes=[pltpu.VMEM(near.shape, jnp.float32), pltpu.SemaphoreType.DMA((chunks + 2,))],
    )
    following = flat_shift(probes_first, -1)
    handed = flat_shift(handed, 1)
    following_last = flat_shift(probes_last, -1)
    handed_last = flat_shift(handed_last, 1)
    (rest,) = call(rest_kernel, [(rows, width)], near, probes, samples, flops=work)
    (rest_first,) = call(following_kernel, [tall], near, rest, following, flops=work)
    scratch = dict(scratch_shapes=[pltpu.VMEM((scratch_rows(columns), columns), jnp.float32)])
    far, inverse, first, probe_coef = call(
        leaf_kernel, [tall, square, square, (columns, width)], rest_first, handed, probes,
        flops=work, **scratch,
    )
    leaf_basis, last = call(
        leaf_last_kernel, [tall, square_last],
        near, rest, following_last, handed_last, far, inverse, flops=work,
    )

    ancestors = []
    for level in range(1, levels + 1):
        copies = 2 ** (level - 1)
        count = subtree // copies
        theirs_probe = swapped(probe_coef, copies)
        if count == 4:
            away = outward(probe_coef, 2 * copies)
            terms = call(
                functools.partial(term_kernel, level), [square, square_last],
                couplings, probe_coef, away, last, specs=[VMEM, VMEM, VMEM, ANY], slots=node_slot,
            )
            first = first - swapped(terms[0], 2 * copies)
            last = last - swapped(terms[1], 2 * copies)
        else:
            if count == 2:
                fields = [tree_swapped(probe_coef, odd) for odd in (0, 1)]
            else:
                even = (lax.axis_index("leaf") >> level - 1) & 1 == 0
                fields = [flat_shift(probe_coef, by) for by in (2 * copies, -2 * copies)]
                fields = [jnp.where(even, *fields), jnp.where(even, *fields[::-1])]
            first, last = call(
                functools.partial(corrected_kernel, level, count == 2), [square, square_last],
                couplings, *fields, first, last, slots=node_slot,
            )
        mine = first, last, probe_coef
        theirs = swapped(first, copies), swapped(last, copies), theirs_probe
        (inverse,) = call(factor_kernel, [square], mine[0], theirs[0], **scratch)
        if level < levels:
            ancestors += call(
                functools.partial(basis_kernel, level), [(1, 1, 2 * columns, columns)],
                inverse, mine[0], theirs[0],
            )
            first, last, probe_coef = call(
                node_kernel, [square, square_last, (columns, width)], inverse, *mine, *theirs
            )
    transfer_bases, top_samples, top_probes = call(
        functools.partial(top_kernel, levels),
        [(1, levels, 2 * columns, columns), (1, columns, width), (1, columns, width)],
        inverse, *mine, *theirs, *ancestors,
    )
    return (leaf_basis, transfer_bases, top_samples, top_probes)


def solution(mesh):
    in_specs = (
        P(("clusters", "leaf"), None),
        P(("clusters", "leaf"), None),
        P(("clusters", "leaf"), None, None),
        P("clusters", None, None, None, None),
        P("clusters", None),
    )
    out_specs = (
        P(("clusters", "leaf"), None),
        P(("clusters", "leaf"), None, None, None),
        P("clusters", None, None),
        P("clusters", None, None),
    )
    return jax.shard_map(body, mesh=mesh, in_specs=in_specs, out_specs=out_specs, check_vma=False)
```

```python
import functools

import jax
import jax.numpy as jnp
from jax import lax
from jax.experimental import pallas as pl
from jax.experimental.pallas import tpu as pltpu
from jax.sharding import PartitionSpec as P

HIGHEST = lax.Precision.HIGHEST
ROWS = 8
GROUP = 4
BOTH = ("leaf", "clusters")


def dot(a, b, ca=1, cb=0):
    return lax.dot_general(
        a, b, (((ca,), (cb,)), ((), ())), precision=HIGHEST, preferred_element_type=jnp.float32
    )


def across_lanes(tile, lane):
    return jnp.broadcast_to(tile[:, lane : lane + 1], tile.shape)


def row_of(ref, row):
    return jnp.broadcast_to(ref[pl.ds(row, 1), :], (ROWS, ref.shape[1]))


def inverse_factor(gram, scratch):
    size = gram.shape[0]
    blocks = size // ROWS
    sub = lax.broadcasted_iota(jnp.int32, (ROWS, size), 0)
    lane = lax.broadcasted_iota(jnp.int32, (ROWS, size), 1)
    rows = [gram[ROWS * i : ROWS * (i + 1), :] for i in range(blocks)]
    scaled = [None] * blocks
    used = 0
    for first in range(0, blocks, GROUP):
        last = first + GROUP
        ahead = min(last + 1, blocks)
        for k in range(first, last):
            cols = {
                i: [across_lanes(rows[i], ROWS * k + c) for c in range(ROWS)] for i in range(k, ahead)
            }
            pivots = jnp.ones((ROWS, size), jnp.float32)
            for j in range(0, ROWS, 2):
                pair = (lane == ROWS * k + j) | (lane == ROWS * k + j + 1)
                for i in range(k, ahead):
                    rows[i] = jnp.where(pair, 0.0, rows[i])
                rows[k] = jnp.where(pair & (lane == sub + ROWS * k), 1.0, rows[k])
                held = scratch.at[pl.ds(used, ROWS * (ROWS - j + 1)), :]
                used += ROWS * (ROWS - j + 1)
                held[pl.ds(0, ROWS), :] = rows[k]
                for n in range(j, ROWS):
                    held[pl.ds(ROWS * (n - j + 1), ROWS), :] = cols[k][n]
                a = row_of(held, ROWS + j)
                b = row_of(held, ROWS + j + 1)
                c = row_of(held, 2 * ROWS + j + 1)
                det = a * c - b * b
                inverse = 1.0 / det
                inverse_a = 1.0 / a
                ratio = b * inverse_a
                pivots = jnp.where(sub == j, a, jnp.where(sub == j + 1, det * inverse_a, pivots))
                row, next_row = row_of(held, j), row_of(held, j + 1)
                col_rows = [
                    (row_of(held, ROWS * (n - j + 1) + j), row_of(held, ROWS * (n - j + 1) + j + 1))
                    for n in range(j + 2, ROWS)
                ]
                for i in range(k, ahead):
                    u, v = cols[i][j], cols[i][j + 1]
                    f = (u * c - v * b) * inverse
                    g = (v * a - u * b) * inverse
                    if i == k:
                        f = jnp.where(sub > j + 1, f, jnp.where(sub == j + 1, ratio, 0.0))
                        g = jnp.where(sub > j + 1, g, 0.0)
                    for n in range(j + 2, ROWS):
                        x, y = col_rows[n - j - 2]
                        cols[i][n] = cols[i][n] - (f * x + g * y)
                    rows[i] = rows[i] - (f * row + g * next_row)
            kept = (lane <= sub + ROWS * k) | (lane >= ROWS * last)
            scaled[k] = jnp.where(kept, rows[k] * lax.rsqrt(pivots), 0.0)
        if ahead < blocks:
            done = jnp.concatenate(scaled[first:last], axis=0)
            change = dot(done.T[ROWS * ahead :, :], done)
            old = (lane >= ROWS * first) & (lane < ROWS * last)
            for i in range(ahead, blocks):
                piece = change[ROWS * (i - ahead) : ROWS * (i - ahead + 1), :]
                rows[i] = jnp.where(old, 0.0, rows[i]) - piece
    return jnp.concatenate(
        [jnp.where(lane <= sub + ROWS * k, scaled[k], 0.0) for k in range(blocks)], axis=0
    )


def scratch_rows(size):
    return size // ROWS * sum(ROWS * (ROWS - j + 1) for j in range(0, ROWS, 2))


def near_half(view, which, rows, chunks=None):
    chunks = rows // 128 if chunks is None else chunks
    return jnp.concatenate(
        [view[pl.ds(2 * c + which, rows, stride=2 * chunks), :] for c in range(chunks)], axis=1
    )


def handed_kernel(near, probes, handed, probes_first, near_copy, arrived):
    rows, columns = handed.shape
    chunks = rows // 128
    pieces = chunks // 2
    part = near.shape[0] // pieces
    coming = [pltpu.make_async_copy(probes.at[:, pl.ds(0, columns)], probes_first, arrived.at[pieces])]
    for c in range(pieces):
        at = pl.ds(c * part, part)
        coming.append(pltpu.make_async_copy(near.at[at, :], near_copy.at[at, :], arrived.at[c]))
    for copy in coming:
        copy.start()
    coming[0].wait()
    total = None
    for c in range(pieces):
        coming[c + 1].wait()
        upper = near_half(near_copy.at[pl.ds(c * part, part), :], 1, 256, chunks)
        piece = dot(probes_first[pl.ds(256 * c, 256), :].T, upper)
        total = piece if total is None else total + piece
    handed[...] = total.T


def rest_kernel(near, probes, samples, rest, handed_last, probes_last):
    rows = probes.shape[0]
    columns = rest.shape[1] - probes_last.shape[1]
    probes_last[...] = probes[:, columns:]
    rest[...] = samples[...] - dot(near_half(near, 0, rows), probes[...])
    handed_last[...] = dot(probes[:, columns:].T, near_half(near, 1, rows)).T


def following_kernel(near, rest, following, out):
    columns = out.shape[1]
    out[...] = rest[:, :columns] - dot(near_half(near, 1, rest.shape[0]), following[...])


def leaf_kernel(rest, handed, probes, _h, _p, far, inverse, sample_coef, probe_coef, _hout, _pout, scratch):
    columns = far.shape[1]
    block = rest[...] - handed[...]
    far[...] = block
    gram = dot(block, block, 0, 0)
    cross = dot(block, probes[...], 0, 0)
    factor = inverse_factor(gram, scratch)
    inverse[...] = factor
    coef = dot(factor, jnp.concatenate([gram, cross], axis=1))
    sample_coef[...] = coef[:, :columns]
    probe_coef[...] = coef[:, columns:]


def leaf_last_kernel(near, rest, following, handed, far, inverse, basis, sample_coef):
    columns = far.shape[1]
    upper = near_half(near, 1, rest.shape[0])
    basis[...] = dot(far[...], inverse[...], 1, 1)
    block = rest[:, columns:] - dot(upper, following[...]) - handed[...]
    sample_coef[...] = dot(basis[...], block, 0, 0)


def coupling_of(slots, couplings, level, node):
    subtree = lax.axis_size("leaf")
    index = subtree - (subtree >> level - 1) + (node >> 1)
    return couplings[0, slots[0, index], node & 1]


def member_node(level):
    return lax.axis_index("leaf") >> level - 1


def term_kernel(level, slots, couplings, mine, away, _h, first, last, _hout):
    node = member_node(level)
    block = coupling_of(slots, couplings, level, node ^ 2)
    outer = (node == 0) | (node == 3)
    main = jnp.where(outer, mine[...], away[...])
    other = jnp.where(outer, away[...], mine[...])
    term = dot(block, main) + dot(block, other, 0, 0)
    first[...] = term[:, : first.shape[1]]
    last[...] = term[:, first.shape[1] :]


def corrected_kernel(level, trees, slots, couplings, one, two, first, out_first, out_last):
    columns = first.shape[1]
    node = member_node(level)
    block = coupling_of(slots, couplings, level, node)
    main, other = one[...], two[...]
    if trees:
        straight = (lax.axis_index("clusters") ^ node) & 1 == 1
        main, other = jnp.where(straight, main, other), jnp.where(straight, other, main)
    term = dot(block, main) + dot(block, other, 0, 0)
    out_first[...] = first[...] - term[:, :columns]
    out_last[...] = term[:, columns:]


def factor_kernel(mine, theirs, inverse, scratch):
    gram = dot(mine[...], mine[...], 0, 0) + dot(theirs[...], theirs[...], 0, 0)
    inverse[...] = inverse_factor(gram, scratch)


def write_basis(level, at, mine, theirs, inverse, bases):
    size = mine.shape[0]
    own = (lax.axis_index("leaf") >> level - 1) & 1
    for block, half in ((mine, own), (theirs, 1 - own)):
        rows = pl.ds(pl.multiple_of(half * size, size), size)
        bases[0, at, rows, :] = dot(block, inverse, 1, 1)


def basis_kernel(level, inverse, mine, theirs, basis):
    write_basis(level, 0, mine[...], theirs[...], inverse[...], basis)


def level_coefs(inverse, mine, theirs):
    own = jnp.concatenate([ref[...] for ref in mine], axis=1)
    sibling = jnp.concatenate([ref[...] for ref in theirs], axis=1)
    return dot(inverse, dot(mine[0][...], own, 0, 0) + dot(theirs[0][...], sibling, 0, 0))


def node_kernel(inverse, mine, mine_probes, theirs, theirs_probes, first, probe_coef):
    columns = first.shape[1]
    coef = level_coefs(inverse[...], (mine, mine_probes), (theirs, theirs_probes))
    first[...] = coef[:, :columns]
    probe_coef[...] = coef[:, columns:]


def node_last_kernel(inverse, mine, mine_last, theirs, theirs_last, last):
    both = dot(mine[...], mine_last[...], 0, 0) + dot(theirs[...], theirs_last[...], 0, 0)
    last[...] = dot(inverse[...], both)


def top_kernel(level, inverse, *refs):
    factor = inverse[...]
    earlier, (bases, samples, probe_coef) = refs[6:-3], refs[-3:]
    coef = level_coefs(factor, refs[:3], refs[3:6])
    width = samples.shape[2]
    samples[0] = coef[:, :width]
    probe_coef[0] = coef[:, width:]
    for at, done in enumerate(earlier):
        bases[0, at] = done[0, 0]
    write_basis(level, len(earlier), refs[0][...], refs[3][...], factor, bases)


VMEM = pl.BlockSpec(memory_space=pltpu.VMEM)
SMEM = pl.BlockSpec(memory_space=pltpu.SMEM)
ANY = pl.BlockSpec(memory_space=pl.ANY)


def call(kernel, shapes, *operands, slots=None, flops=0, specs=None, out_specs=None, vmem=32, **options):
    outs = [jax.ShapeDtypeStruct(shape, jnp.float32) for shape in shapes]
    specs = [VMEM] * len(operands) if specs is None else specs
    out_specs = [VMEM] * len(outs) if out_specs is None else out_specs
    if slots is not None:
        operands = (slots,) + operands
        specs = [SMEM] + specs
    moved = 4 * (sum(o.size for o in operands) + sum(o.size for o in outs))
    return pl.pallas_call(
        kernel,
        out_shape=outs,
        in_specs=specs,
        out_specs=out_specs,
        compiler_params=pltpu.CompilerParams(vmem_limit_bytes=vmem * 2**20),
        cost_estimate=pl.CostEstimate(flops=flops, bytes_accessed=moved, transcendentals=0),
        **options,
    )(*operands)


def permuted(value, target):
    trees, subtree = lax.axis_size("clusters"), lax.axis_size("leaf")
    pairs = []
    for member in range(subtree):
        for tree in range(trees):
            to_tree, to_member = target(tree, member)
            if 0 <= to_tree < trees:
                pairs.append((member * trees + tree, to_member * trees + to_tree))
    return lax.ppermute(value, BOTH, pairs)


def flat_shift(value, by):
    subtree = lax.axis_size("leaf")
    return permuted(value, lambda tree, member: divmod(tree * subtree + member + by, subtree))


def swapped(value, mask):
    return permuted(value, lambda tree, member: (tree, member ^ mask))


def outward(value, half):
    return permuted(value, lambda tree, member: (tree - 1 if member < half else tree + 1, member))


def tree_swapped(value, odd):
    return permuted(value, lambda tree, member: (tree + 1 if tree & 1 == odd else tree - 1, member))


def body(samples, probes, near_blocks, couplings, node_slot):
    rows, width = probes.shape
    columns = couplings.shape[-1]
    subtree = lax.axis_size("leaf")
    levels = subtree.bit_length() - 1
    chunks = rows // 128
    near = near_blocks.reshape(rows, 2, chunks, 128).transpose(0, 2, 1, 3).reshape(-1, 128)
    work = 12 * rows * rows * width
    tall, tall_last = (rows, columns), (rows, width - columns)
    square, square_last = (columns, columns), (columns, width - columns)

    handed, probes_first = call(
        handed_kernel, [tall, tall], near, probes, flops=work, specs=[ANY, ANY], vmem=62,
        scratch_shapes=[
            pltpu.VMEM(near.shape, jnp.float32), pltpu.SemaphoreType.DMA((chunks // 2 + 1,))
        ],
    )
    following = flat_shift(probes_first, -1)
    handed = flat_shift(handed, 1)
    rest, handed_last, probes_last = call(
        rest_kernel, [(rows, width), tall_last, tall_last], near, probes, samples, flops=work
    )
    (rest_first,) = call(following_kernel, [tall], near, rest, following, flops=work)
    scratch = dict(scratch_shapes=[pltpu.VMEM((scratch_rows(columns), columns), jnp.float32)])
    far, inverse, first, probe_coef, handed_last, probes_last = call(
        leaf_kernel, [tall, square, square, (columns, width), tall_last, tall_last],
        rest_first, handed, probes, handed_last, probes_last, flops=work,
        specs=[VMEM, VMEM, VMEM, ANY, ANY], out_specs=[VMEM, VMEM, VMEM, VMEM, ANY, ANY],
        input_output_aliases={3: 4, 4: 5}, **scratch,
    )
    following_last = flat_shift(probes_last, -1)

    ancestors = []
    last = None
    for level in range(1, levels + 1):
        copies = 2 ** (level - 1)
        count = subtree // copies
        theirs_probe = swapped(probe_coef, copies)
        if count == 4:
            away = outward(probe_coef, 2 * copies)
            term_first, term_last, handed_last = call(
                functools.partial(term_kernel, level), [square, square_last, tall_last],
                couplings, probe_coef, away, handed_last, slots=node_slot,
                specs=[VMEM, VMEM, VMEM, ANY], out_specs=[VMEM, VMEM, ANY],
                input_output_aliases={4: 2},
            )
            first = first - swapped(term_first, 2 * copies)
            term_last = swapped(term_last, 2 * copies)
        else:
            if count == 2:
                fields = [tree_swapped(probe_coef, odd) for odd in (0, 1)]
            else:
                even = (lax.axis_index("leaf") >> level - 1) & 1 == 0
                fields = [flat_shift(probe_coef, by) for by in (2 * copies, -2 * copies)]
                fields = [jnp.where(even, *fields), jnp.where(even, *fields[::-1])]
            first, term_last = call(
                functools.partial(corrected_kernel, level, count == 2), [square, square_last],
                couplings, *fields, first, slots=node_slot,
            )
        if last is None:
            leaf_basis, last = call(
                leaf_last_kernel, [tall, square_last],
                near, rest, following_last, flat_shift(handed_last, 1), far, inverse, flops=work,
            )
        last = last - term_last
        mine = first, last, probe_coef
        theirs = swapped(first, copies), swapped(last, copies), theirs_probe
        (inverse,) = call(factor_kernel, [square], mine[0], theirs[0], **scratch)
        if level < levels:
            ancestors += call(
                functools.partial(basis_kernel, level), [(1, 1, 2 * columns, columns)],
                inverse, mine[0], theirs[0],
            )
            first, probe_coef = call(
                node_kernel, [square, (columns, width)],
                inverse, mine[0], mine[2], theirs[0], theirs[2],
            )
            (last,) = call(
                node_last_kernel, [square_last], inverse, mine[0], mine[1], theirs[0], theirs[1]
            )
    transfer_bases, top_samples, top_probes = call(
        functools.partial(top_kernel, levels),
        [(1, levels, 2 * columns, columns), (1, columns, width), (1, columns, width)],
        inverse, *mine, *theirs, *ancestors,
    )
    return (leaf_basis, transfer_bases, top_samples, top_probes)


def solution(mesh):
    in_specs = (
        P(("clusters", "leaf"), None),
        P(("clusters", "leaf"), None),
        P(("clusters", "leaf"), None, None),
        P("clusters", None, None, None, None),
        P("clusters", None),
    )
    out_specs = (
        P(("clusters", "leaf"), None),
        P(("clusters", "leaf"), None, None, None),
        P("clusters", None, None),
        P("clusters", None, None),
    )
    return jax.shard_map(body, mesh=mesh, in_specs=in_specs, out_specs=out_specs, check_vma=False)
```

```python
import functools

import jax
import jax.numpy as jnp
from jax import lax
from jax.experimental import pallas as pl
from jax.experimental.pallas import tpu as pltpu
from jax.sharding import PartitionSpec as P

HIGHEST = lax.Precision.HIGHEST
ROWS = 8
GROUP = 4
BOTH = ("leaf", "clusters")


def dot(a, b, ca=1, cb=0):
    return lax.dot_general(
        a, b, (((ca,), (cb,)), ((), ())), precision=HIGHEST, preferred_element_type=jnp.float32
    )


def across_lanes(tile, lane):
    return jnp.broadcast_to(tile[:, lane : lane + 1], tile.shape)


def row_of(ref, row):
    return jnp.broadcast_to(ref[pl.ds(row, 1), :], (ROWS, ref.shape[1]))


def inverse_factor(gram, scratch):
    size = gram.shape[0]
    blocks = size // ROWS
    sub = lax.broadcasted_iota(jnp.int32, (ROWS, size), 0)
    lane = lax.broadcasted_iota(jnp.int32, (ROWS, size), 1)
    rows = [gram[ROWS * i : ROWS * (i + 1), :] for i in range(blocks)]
    scaled = [None] * blocks
    used = 0
    for first in range(0, blocks, GROUP):
        last = first + GROUP
        ahead = min(last + 1, blocks)
        for k in range(first, last):
            cols = {
                i: [across_lanes(rows[i], ROWS * k + c) for c in range(ROWS)] for i in range(k, ahead)
            }
            pivots = jnp.ones((ROWS, size), jnp.float32)
            for j in range(0, ROWS, 2):
                pair = (lane == ROWS * k + j) | (lane == ROWS * k + j + 1)
                for i in range(k, ahead):
                    rows[i] = jnp.where(pair, 0.0, rows[i])
                rows[k] = jnp.where(pair & (lane == sub + ROWS * k), 1.0, rows[k])
                held = scratch.at[pl.ds(used, ROWS * (ROWS - j + 1)), :]
                used += ROWS * (ROWS - j + 1)
                held[pl.ds(0, ROWS), :] = rows[k]
                for n in range(j, ROWS):
                    held[pl.ds(ROWS * (n - j + 1), ROWS), :] = cols[k][n]
                a = row_of(held, ROWS + j)
                b = row_of(held, ROWS + j + 1)
                c = row_of(held, 2 * ROWS + j + 1)
                det = a * c - b * b
                inverse = 1.0 / det
                inverse_a = 1.0 / a
                ratio = b * inverse_a
                pivots = jnp.where(sub == j, a, jnp.where(sub == j + 1, det * inverse_a, pivots))
                row, next_row = row_of(held, j), row_of(held, j + 1)
                col_rows = [
                    (row_of(held, ROWS * (n - j + 1) + j), row_of(held, ROWS * (n - j + 1) + j + 1))
                    for n in range(j + 2, ROWS)
                ]
                for i in range(k, ahead):
                    u, v = cols[i][j], cols[i][j + 1]
                    f = (u * c - v * b) * inverse
                    g = (v * a - u * b) * inverse
                    if i == k:
                        f = jnp.where(sub > j + 1, f, jnp.where(sub == j + 1, ratio, 0.0))
                        g = jnp.where(sub > j + 1, g, 0.0)
                    for n in range(j + 2, ROWS):
                        x, y = col_rows[n - j - 2]
                        cols[i][n] = cols[i][n] - (f * x + g * y)
                    rows[i] = rows[i] - (f * row + g * next_row)
            kept = (lane <= sub + ROWS * k) | (lane >= ROWS * last)
            scaled[k] = jnp.where(kept, rows[k] * lax.rsqrt(pivots), 0.0)
        if ahead < blocks:
            done = jnp.concatenate(scaled[first:last], axis=0)
            change = dot(done.T[ROWS * ahead :, :], done)
            old = (lane >= ROWS * first) & (lane < ROWS * last)
            for i in range(ahead, blocks):
                piece = change[ROWS * (i - ahead) : ROWS * (i - ahead + 1), :]
                rows[i] = jnp.where(old, 0.0, rows[i]) - piece
    return jnp.concatenate(
        [jnp.where(lane <= sub + ROWS * k, scaled[k], 0.0) for k in range(blocks)], axis=0
    )


def scratch_rows(size):
    return size // ROWS * sum(ROWS * (ROWS - j + 1) for j in range(0, ROWS, 2))


def near_half(view, which, rows, chunks=None):
    chunks = rows // 128 if chunks is None else chunks
    return jnp.concatenate(
        [view[pl.ds(2 * c + which, rows, stride=2 * chunks), :] for c in range(chunks)], axis=1
    )


def handed_kernel(near, probes, handed):
    handed[...] = dot(probes[:, : handed.shape[1]].T, near_half(near, 1, probes.shape[0])).T


def rest_kernel(near, probes, samples, rest, handed_last):
    rows, columns = handed_last.shape
    rest[...] = samples[...] - dot(near_half(near, 0, rows), probes[...])
    handed_last[...] = dot(probes[:, probes.shape[1] - columns :].T, near_half(near, 1, rows)).T


def following_kernel(near, rest, following, _h, first, last, _hout):
    columns = first.shape[1]
    block = rest[...] - dot(near_half(near, 1, rest.shape[0]), following[...])
    first[...] = block[:, :columns]
    last[...] = block[:, columns:]


def leaf_kernel(rest, handed, probes, far, inverse, sample_coef, probe_coef, scratch):
    columns = far.shape[1]
    block = rest[...] - handed[...]
    far[...] = block
    gram = dot(block, block, 0, 0)
    cross = dot(block, probes[...], 0, 0)
    factor = inverse_factor(gram, scratch)
    inverse[...] = factor
    coef = dot(factor, jnp.concatenate([gram, cross], axis=1))
    sample_coef[...] = coef[:, :columns]
    probe_coef[...] = coef[:, columns:]


def leaf_last_kernel(rest, handed, far, inverse, basis, sample_coef):
    basis[...] = dot(far[...], inverse[...], 1, 1)
    sample_coef[...] = dot(basis[...], rest[...] - handed[...], 0, 0)


def coupling_of(slots, couplings, level, node):
    subtree = lax.axis_size("leaf")
    index = subtree - (subtree >> level - 1) + (node >> 1)
    return couplings[0, slots[0, index], node & 1]


def member_node(level):
    return lax.axis_index("leaf") >> level - 1


def term_kernel(level, slots, couplings, mine, away, _last, first, last):
    node = member_node(level)
    block = coupling_of(slots, couplings, level, node ^ 2)
    outer = (node == 0) | (node == 3)
    main = jnp.where(outer, mine[...], away[...])
    other = jnp.where(outer, away[...], mine[...])
    term = dot(block, main) + dot(block, other, 0, 0)
    first[...] = term[:, : first.shape[1]]
    last[...] = term[:, first.shape[1] :]


def corrected_kernel(level, trees, slots, couplings, one, two, first, out_first, out_last):
    columns = first.shape[1]
    node = member_node(level)
    block = coupling_of(slots, couplings, level, node)
    main, other = one[...], two[...]
    if trees:
        straight = (lax.axis_index("clusters") ^ node) & 1 == 1
        main, other = jnp.where(straight, main, other), jnp.where(straight, other, main)
    term = dot(block, main) + dot(block, other, 0, 0)
    out_first[...] = first[...] - term[:, :columns]
    out_last[...] = term[:, columns:]


def factor_kernel(mine, theirs, inverse, scratch):
    gram = dot(mine[...], mine[...], 0, 0) + dot(theirs[...], theirs[...], 0, 0)
    inverse[...] = inverse_factor(gram, scratch)


def write_basis(level, at, mine, theirs, inverse, bases):
    size = mine.shape[0]
    own = (lax.axis_index("leaf") >> level - 1) & 1
    for block, half in ((mine, own), (theirs, 1 - own)):
        rows = pl.ds(pl.multiple_of(half * size, size), size)
        bases[0, at, rows, :] = dot(block, inverse, 1, 1)


def basis_kernel(level, inverse, mine, theirs, basis):
    write_basis(level, 0, mine[...], theirs[...], inverse[...], basis)


def level_coefs(inverse, mine, theirs):
    own = jnp.concatenate([ref[...] for ref in mine], axis=1)
    sibling = jnp.concatenate([ref[...] for ref in theirs], axis=1)
    return dot(inverse, dot(mine[0][...], own, 0, 0) + dot(theirs[0][...], sibling, 0, 0))


def node_kernel(inverse, *refs):
    coef = level_coefs(inverse[...], refs[:3], refs[3:6])
    at = 0
    for out in refs[6:]:
        out[...] = coef[:, at : at + out.shape[1]]
        at += out.shape[1]


def top_kernel(level, inverse, *refs):
    factor = inverse[...]
    earlier, (bases, samples, probe_coef) = refs[6:-3], refs[-3:]
    coef = level_coefs(factor, refs[:3], refs[3:6])
    width = samples.shape[2]
    samples[0] = coef[:, :width]
    probe_coef[0] = coef[:, width:]
    for at, done in enumerate(earlier):
        bases[0, at] = done[0, 0]
    write_basis(level, len(earlier), refs[0][...], refs[3][...], factor, bases)


VMEM = pl.BlockSpec(memory_space=pltpu.VMEM)
SMEM = pl.BlockSpec(memory_space=pltpu.SMEM)
ANY = pl.BlockSpec(memory_space=pl.ANY)


def call(kernel, shapes, *operands, slots=None, flops=0, specs=None, out_specs=None, vmem=32, **options):
    outs = [jax.ShapeDtypeStruct(shape, jnp.float32) for shape in shapes]
    specs = [VMEM] * len(operands) if specs is None else specs
    out_specs = [VMEM] * len(outs) if out_specs is None else out_specs
    if slots is not None:
        operands = (slots,) + operands
        specs = [SMEM] + specs
    moved = 4 * (sum(o.size for o in operands) + sum(o.size for o in outs))
    return pl.pallas_call(
        kernel,
        out_shape=outs,
        in_specs=specs,
        out_specs=out_specs,
        compiler_params=pltpu.CompilerParams(vmem_limit_bytes=vmem * 2**20),
        cost_estimate=pl.CostEstimate(flops=flops, bytes_accessed=moved, transcendentals=0),
        **options,
    )(*operands)


def permuted(value, target):
    trees, subtree = lax.axis_size("clusters"), lax.axis_size("leaf")
    pairs = []
    for member in range(subtree):
        for tree in range(trees):
            to_tree, to_member = target(tree, member)
            if 0 <= to_tree < trees:
                pairs.append((member * trees + tree, to_member * trees + to_tree))
    return lax.ppermute(value, BOTH, pairs)


def flat_shift(value, by):
    subtree = lax.axis_size("leaf")
    return permuted(value, lambda tree, member: divmod(tree * subtree + member + by, subtree))


def swapped(value, mask):
    return permuted(value, lambda tree, member: (tree, member ^ mask))


def outward(value, half):
    return permuted(value, lambda tree, member: (tree - 1 if member < half else tree + 1, member))


def tree_swapped(value, odd):
    return permuted(value, lambda tree, member: (tree + 1 if tree & 1 == odd else tree - 1, member))


def body(samples, probes, near_blocks, couplings, node_slot):
    rows, width = probes.shape
    columns = couplings.shape[-1]
    subtree = lax.axis_size("leaf")
    levels = subtree.bit_length() - 1
    chunks = rows // 128
    near = near_blocks.reshape(rows, 2, chunks, 128).transpose(0, 2, 1, 3).reshape(-1, 128)
    work = 12 * rows * rows * width
    tall, tall_last = (rows, columns), (rows, width - columns)
    square, square_last = (columns, columns), (columns, width - columns)

    following = flat_shift(probes, -1)
    (handed,) = call(handed_kernel, [tall], near, probes, flops=work)
    handed = flat_shift(handed, 1)
    rest, handed_last = call(
        rest_kernel, [(rows, width), tall_last], near, probes, samples, flops=work
    )
    rest_first, rest_last, handed_last = call(
        following_kernel, [tall, tall_last, tall_last], near, rest, following, handed_last, flops=work,
        specs=[VMEM, VMEM, VMEM, ANY], out_specs=[VMEM, VMEM, ANY], input_output_aliases={3: 2},
    )
    handed_last = flat_shift(handed_last, 1)
    scratch = dict(scratch_shapes=[pltpu.VMEM((scratch_rows(columns), columns), jnp.float32)])
    far, inverse, first, probe_coef = call(
        leaf_kernel, [tall, square, square, (columns, width)], rest_first, handed, probes,
        flops=work, **scratch,
    )
    leaf_basis, last = call(
        leaf_last_kernel, [tall, square_last], rest_last, handed_last, far, inverse, flops=work
    )

    ancestors = []
    for level in range(1, levels + 1):
        copies = 2 ** (level - 1)
        count = subtree // copies
        theirs_probe = swapped(probe_coef, copies)
        if count == 4:
            away = outward(probe_coef, 2 * copies)
            term_first, term_last = call(
                functools.partial(term_kernel, level), [square, square_last],
                couplings, probe_coef, away, last, slots=node_slot, specs=[VMEM, VMEM, VMEM, ANY],
            )
            first = first - swapped(term_first, 2 * copies)
            term_last = swapped(term_last, 2 * copies)
        else:
            if count == 2:
                fields = [tree_swapped(probe_coef, odd) for odd in (0, 1)]
            else:
                even = (lax.axis_index("leaf") >> level - 1) & 1 == 0
                fields = [flat_shift(probe_coef, by) for by in (2 * copies, -2 * copies)]
                fields = [jnp.where(even, *fields), jnp.where(even, *fields[::-1])]
            first, term_last = call(
                functools.partial(corrected_kernel, level, count == 2), [square, square_last],
                couplings, *fields, first, slots=node_slot,
            )
        last = last - term_last
        mine = first, last, probe_coef
        theirs = swapped(first, copies), swapped(last, copies), theirs_probe
        (inverse,) = call(factor_kernel, [square], mine[0], theirs[0], **scratch)
        if level < levels:
            ancestors += call(
                functools.partial(basis_kernel, level), [(1, 1, 2 * columns, columns)],
                inverse, mine[0], theirs[0],
            )
            first, last, probe_coef = call(
                node_kernel, [square, square_last, (columns, width)], inverse, *mine, *theirs
            )
    transfer_bases, top_samples, top_probes = call(
        functools.partial(top_kernel, levels),
        [(1, levels, 2 * columns, columns), (1, columns, width), (1, columns, width)],
        inverse, *mine, *theirs, *ancestors,
    )
    return (leaf_basis, transfer_bases, top_samples, top_probes)


def solution(mesh):
    in_specs = (
        P(("clusters", "leaf"), None),
        P(("clusters", "leaf"), None),
        P(("clusters", "leaf"), None, None),
        P("clusters", None, None, None, None),
        P("clusters", None),
    )
    out_specs = (
        P(("clusters", "leaf"), None),
        P(("clusters", "leaf"), None, None, None),
        P("clusters", None, None),
        P("clusters", None, None),
    )
    return jax.shard_map(body, mesh=mesh, in_specs=in_specs, out_specs=out_specs, check_vma=False)
```

```python
import functools

import jax
import jax.numpy as jnp
from jax import lax
from jax.experimental import pallas as pl
from jax.experimental.pallas import tpu as pltpu
from jax.sharding import PartitionSpec as P

HIGHEST = lax.Precision.HIGHEST
ROWS = 8
GROUP = 4
BOTH = ("leaf", "clusters")


def dot(a, b, ca=1, cb=0):
    return lax.dot_general(
        a, b, (((ca,), (cb,)), ((), ())), precision=HIGHEST, preferred_element_type=jnp.float32
    )


def across_lanes(tile, lane):
    return jnp.broadcast_to(tile[:, lane : lane + 1], tile.shape)


def row_of(ref, row):
    return jnp.broadcast_to(ref[pl.ds(row, 1), :], (ROWS, ref.shape[1]))


def inverse_factor(gram, scratch):
    size = gram.shape[0]
    blocks = size // ROWS
    sub = lax.broadcasted_iota(jnp.int32, (ROWS, size), 0)
    lane = lax.broadcasted_iota(jnp.int32, (ROWS, size), 1)
    rows = [gram[ROWS * i : ROWS * (i + 1), :] for i in range(blocks)]
    scaled = [None] * blocks
    used = 0
    coming = None

    def spread(tile, panel):
        return [across_lanes(tile, ROWS * panel + n) for n in range(ROWS)]

    for first in range(0, blocks, GROUP):
        last = first + GROUP
        ahead = min(last + 1, blocks)
        for k in range(first, last):
            cols = {i: spread(rows[i], k) for i in range(k, ahead) if i > k or coming is None}
            if coming is not None:
                cols[k], coming = coming, None
            pivots = jnp.ones((ROWS, size), jnp.float32)
            for j in range(0, ROWS, 2):
                pair = (lane == ROWS * k + j) | (lane == ROWS * k + j + 1)
                for i in range(k, ahead):
                    rows[i] = jnp.where(pair, 0.0, rows[i])
                rows[k] = jnp.where(pair & (lane == sub + ROWS * k), 1.0, rows[k])
                held = scratch.at[pl.ds(used, ROWS * (ROWS - j + 1)), :]
                used += ROWS * (ROWS - j + 1)
                held[pl.ds(0, ROWS), :] = rows[k]
                for n in range(j, ROWS):
                    held[pl.ds(ROWS * (n - j + 1), ROWS), :] = cols[k][n]
                a = row_of(held, ROWS + j)
                b = row_of(held, ROWS + j + 1)
                c = row_of(held, 2 * ROWS + j + 1)
                det = a * c - b * b
                inverse = pltpu.reciprocal(det, approx=True)
                inverse_a = pltpu.reciprocal(a, approx=True)
                ratio = b * inverse_a
                pivots = jnp.where(sub == j, a, jnp.where(sub == j + 1, det * inverse_a, pivots))
                row, next_row = row_of(held, j), row_of(held, j + 1)
                col_rows = [
                    (row_of(held, ROWS * (n - j + 1) + j), row_of(held, ROWS * (n - j + 1) + j + 1))
                    for n in range(j + 2, ROWS)
                ]
                for i in range(k, ahead):
                    u, v = cols[i][j], cols[i][j + 1]
                    f = (u * c - v * b) * inverse
                    g = (v * a - u * b) * inverse
                    if i == k:
                        f = jnp.where(sub > j + 1, f, jnp.where(sub == j + 1, ratio, 0.0))
                        g = jnp.where(sub > j + 1, g, 0.0)
                    for n in range(j + 2, ROWS):
                        x, y = col_rows[n - j - 2]
                        cols[i][n] = cols[i][n] - (f * x + g * y)
                    if i == k + 1 and j == ROWS - 2:
                        now, one, two = spread(rows[i], i), spread(row, i), spread(next_row, i)
                        coming = [now[n] - (f * one[n] + g * two[n]) for n in range(ROWS)]
                    rows[i] = rows[i] - (f * row + g * next_row)
            kept = (lane <= sub + ROWS * k) | (lane >= ROWS * last)
            scaled[k] = jnp.where(kept, rows[k] * lax.rsqrt(pivots), 0.0)
        if ahead < blocks:
            done = jnp.concatenate(scaled[first:last], axis=0)
            change = dot(done.T[ROWS * ahead :, :], done)
            old = (lane >= ROWS * first) & (lane < ROWS * last)
            for i in range(ahead, blocks):
                piece = change[ROWS * (i - ahead) : ROWS * (i - ahead + 1), :]
                rows[i] = jnp.where(old, 0.0, rows[i]) - piece
    return jnp.concatenate(
        [jnp.where(lane <= sub + ROWS * k, scaled[k], 0.0) for k in range(blocks)], axis=0
    )


def scratch_rows(size):
    return size // ROWS * sum(ROWS * (ROWS - j + 1) for j in range(0, ROWS, 2))


def near_half(view, which, rows, chunks=None):
    chunks = rows // 128 if chunks is None else chunks
    return jnp.concatenate(
        [view[pl.ds(2 * c + which, rows, stride=2 * chunks), :] for c in range(chunks)], axis=1
    )


def handed_kernel(near, probes, handed):
    handed[...] = dot(probes[:, : handed.shape[1]].T, near_half(near, 1, probes.shape[0])).T


def rest_kernel(near, probes, samples, rest, handed_last):
    rows, columns = handed_last.shape
    rest[...] = samples[...] - dot(near_half(near, 0, rows), probes[...])
    handed_last[...] = dot(probes[:, probes.shape[1] - columns :].T, near_half(near, 1, rows)).T


def following_kernel(near, rest, following, _h, first, last, _hout):
    columns = first.shape[1]
    block = rest[...] - dot(near_half(near, 1, rest.shape[0]), following[...])
    first[...] = block[:, :columns]
    last[...] = block[:, columns:]


def leaf_kernel(rest, handed, probes, far, inverse, sample_coef, probe_coef, scratch):
    columns = far.shape[1]
    block = rest[...] - handed[...]
    far[...] = block
    gram = dot(block, block, 0, 0)
    cross = dot(block, probes[...], 0, 0)
    factor = inverse_factor(gram, scratch)
    inverse[...] = factor
    coef = dot(factor, jnp.concatenate([gram, cross], axis=1))
    sample_coef[...] = coef[:, :columns]
    probe_coef[...] = coef[:, columns:]


def leaf_last_kernel(rest, handed, far, inverse, basis, sample_coef):
    basis[...] = dot(far[...], inverse[...], 1, 1)
    sample_coef[...] = dot(basis[...], rest[...] - handed[...], 0, 0)


def coupling_of(slots, couplings, level, node):
    subtree = lax.axis_size("leaf")
    index = subtree - (subtree >> level - 1) + (node >> 1)
    return couplings[0, slots[0, index], node & 1]


def member_node(level):
    return lax.axis_index("leaf") >> level - 1


def term_kernel(level, slots, couplings, mine, away, _theirs, _last, first, last):
    node = member_node(level)
    block = coupling_of(slots, couplings, level, node ^ 2)
    outer = (node == 0) | (node == 3)
    main = jnp.where(outer, mine[...], away[...])
    other = jnp.where(outer, away[...], mine[...])
    term = dot(block, main) + dot(block, other, 0, 0)
    first[...] = term[:, : first.shape[1]]
    last[...] = term[:, first.shape[1] :]


def corrected_kernel(level, trees, slots, couplings, one, two, first, out_first, out_last):
    columns = first.shape[1]
    node = member_node(level)
    block = coupling_of(slots, couplings, level, node)
    main, other = one[...], two[...]
    if trees:
        straight = (lax.axis_index("clusters") ^ node) & 1 == 1
        main, other = jnp.where(straight, main, other), jnp.where(straight, other, main)
    term = dot(block, main) + dot(block, other, 0, 0)
    out_first[...] = first[...] - term[:, :columns]
    out_last[...] = term[:, columns:]


def factor_kernel(mine, theirs, inverse, scratch):
    gram = dot(mine[...], mine[...], 0, 0) + dot(theirs[...], theirs[...], 0, 0)
    inverse[...] = inverse_factor(gram, scratch)


def write_basis(level, at, mine, theirs, inverse, bases):
    size = mine.shape[0]
    own = (lax.axis_index("leaf") >> level - 1) & 1
    for block, half in ((mine, own), (theirs, 1 - own)):
        rows = pl.ds(pl.multiple_of(half * size, size), size)
        bases[0, at, rows, :] = dot(block, inverse, 1, 1)


def basis_kernel(level, inverse, mine, theirs, basis):
    write_basis(level, 0, mine[...], theirs[...], inverse[...], basis)


def level_coefs(inverse, mine, theirs):
    own = jnp.concatenate([ref[...] for ref in mine], axis=1)
    sibling = jnp.concatenate([ref[...] for ref in theirs], axis=1)
    return dot(inverse, dot(mine[0][...], own, 0, 0) + dot(theirs[0][...], sibling, 0, 0))


def node_kernel(inverse, mine, mine_probes, theirs, theirs_probes, first, probe_coef):
    columns = first.shape[1]
    coef = level_coefs(inverse[...], (mine, mine_probes), (theirs, theirs_probes))
    first[...] = coef[:, :columns]
    probe_coef[...] = coef[:, columns:]


def node_last_kernel(inverse, mine, mine_last, theirs, theirs_last, last):
    both = dot(mine[...], mine_last[...], 0, 0) + dot(theirs[...], theirs_last[...], 0, 0)
    last[...] = dot(inverse[...], both)


def top_kernel(level, inverse, *refs):
    factor = inverse[...]
    earlier, (bases, samples, probe_coef) = refs[6:-3], refs[-3:]
    coef = level_coefs(factor, refs[:3], refs[3:6])
    width = samples.shape[2]
    samples[0] = coef[:, :width]
    probe_coef[0] = coef[:, width:]
    for at, done in enumerate(earlier):
        bases[0, at] = done[0, 0]
    write_basis(level, len(earlier), refs[0][...], refs[3][...], factor, bases)


VMEM = pl.BlockSpec(memory_space=pltpu.VMEM)
SMEM = pl.BlockSpec(memory_space=pltpu.SMEM)
ANY = pl.BlockSpec(memory_space=pl.ANY)


def call(kernel, shapes, *operands, slots=None, flops=0, specs=None, out_specs=None, vmem=32, **options):
    outs = [jax.ShapeDtypeStruct(shape, jnp.float32) for shape in shapes]
    specs = [VMEM] * len(operands) if specs is None else specs
    out_specs = [VMEM] * len(outs) if out_specs is None else out_specs
    if slots is not None:
        operands = (slots,) + operands
        specs = [SMEM] + specs
    moved = 4 * (sum(o.size for o in operands) + sum(o.size for o in outs))
    return pl.pallas_call(
        kernel,
        out_shape=outs,
        in_specs=specs,
        out_specs=out_specs,
        compiler_params=pltpu.CompilerParams(vmem_limit_bytes=vmem * 2**20),
        cost_estimate=pl.CostEstimate(flops=flops, bytes_accessed=moved, transcendentals=0),
        **options,
    )(*operands)


def permuted(value, target):
    trees, subtree = lax.axis_size("clusters"), lax.axis_size("leaf")
    pairs = []
    for member in range(subtree):
        for tree in range(trees):
            to_tree, to_member = target(tree, member)
            if 0 <= to_tree < trees:
                pairs.append((member * trees + tree, to_member * trees + to_tree))
    return lax.ppermute(value, BOTH, pairs)


def flat_shift(value, by):
    subtree = lax.axis_size("leaf")
    return permuted(value, lambda tree, member: divmod(tree * subtree + member + by, subtree))


def swapped(value, mask):
    return permuted(value, lambda tree, member: (tree, member ^ mask))


def outward(value, half):
    return permuted(value, lambda tree, member: (tree - 1 if member < half else tree + 1, member))


def tree_swapped(value, odd):
    return permuted(value, lambda tree, member: (tree + 1 if tree & 1 == odd else tree - 1, member))


def body(samples, probes, near_blocks, couplings, node_slot):
    rows, width = probes.shape
    columns = couplings.shape[-1]
    subtree = lax.axis_size("leaf")
    levels = subtree.bit_length() - 1
    chunks = rows // 128
    near = near_blocks.reshape(rows, 2, chunks, 128).transpose(0, 2, 1, 3).reshape(-1, 128)
    work = 12 * rows * rows * width
    tall, tall_last = (rows, columns), (rows, width - columns)
    square, square_last = (columns, columns), (columns, width - columns)

    following = flat_shift(probes, -1)
    (handed,) = call(handed_kernel, [tall], near, probes, flops=work)
    handed = flat_shift(handed, 1)
    rest, handed_last = call(
        rest_kernel, [(rows, width), tall_last], near, probes, samples, flops=work
    )
    rest_first, rest_last, handed_last = call(
        following_kernel, [tall, tall_last, tall_last], near, rest, following, handed_last, flops=work,
        specs=[VMEM, VMEM, VMEM, ANY], out_specs=[VMEM, VMEM, ANY], input_output_aliases={3: 2},
    )
    handed_last = flat_shift(handed_last, 1)
    scratch = dict(scratch_shapes=[pltpu.VMEM((scratch_rows(columns), columns), jnp.float32)])
    far, inverse, first, probe_coef = call(
        leaf_kernel, [tall, square, square, (columns, width)], rest_first, handed, probes,
        flops=work, **scratch,
    )
    leaf_basis, last = call(
        leaf_last_kernel, [tall, square_last], rest_last, handed_last, far, inverse, flops=work
    )

    ancestors = []
    for level in range(1, levels + 1):
        copies = 2 ** (level - 1)
        count = subtree // copies
        theirs_probe = swapped(probe_coef, copies)
        if count == 4:
            away = outward(probe_coef, 2 * copies)
            term_first, term_last = call(
                functools.partial(term_kernel, level), [square, square_last],
                couplings, probe_coef, away, theirs_probe, last, slots=node_slot,
                specs=[VMEM, VMEM, VMEM, ANY, ANY],
            )
            first = first - swapped(term_first, 2 * copies)
            term_last = swapped(term_last, 2 * copies)
        else:
            if count == 2:
                fields = [tree_swapped(probe_coef, odd) for odd in (0, 1)]
            else:
                even = (lax.axis_index("leaf") >> level - 1) & 1 == 0
                fields = [flat_shift(probe_coef, by) for by in (2 * copies, -2 * copies)]
                fields = [jnp.where(even, *fields), jnp.where(even, *fields[::-1])]
            first, term_last = call(
                functools.partial(corrected_kernel, level, count == 2), [square, square_last],
                couplings, *fields, first, slots=node_slot,
            )
        last = last - term_last
        mine = first, last, probe_coef
        theirs = swapped(first, copies), swapped(last, copies), theirs_probe
        (inverse,) = call(factor_kernel, [square], mine[0], theirs[0], **scratch)
        if level < levels:
            ancestors += call(
                functools.partial(basis_kernel, level), [(1, 1, 2 * columns, columns)],
                inverse, mine[0], theirs[0],
            )
            first, probe_coef = call(
                node_kernel, [square, (columns, width)],
                inverse, mine[0], mine[2], theirs[0], theirs[2],
            )
            (last,) = call(
                node_last_kernel, [square_last], inverse, mine[0], mine[1], theirs[0], theirs[1]
            )
    transfer_bases, top_samples, top_probes = call(
        functools.partial(top_kernel, levels),
        [(1, levels, 2 * columns, columns), (1, columns, width), (1, columns, width)],
        inverse, *mine, *theirs, *ancestors,
    )
    return (leaf_basis, transfer_bases, top_samples, top_probes)


def solution(mesh):
    in_specs = (
        P(("clusters", "leaf"), None),
        P(("clusters", "leaf"), None),
        P(("clusters", "leaf"), None, None),
        P("clusters", None, None, None, None),
        P("clusters", None),
    )
    out_specs = (
        P(("clusters", "leaf"), None),
        P(("clusters", "leaf"), None, None, None),
        P("clusters", None, None),
        P("clusters", None, None),
    )
    return jax.shard_map(body, mesh=mesh, in_specs=in_specs, out_specs=out_specs, check_vma=False)
```

```python
import functools

import jax
import jax.numpy as jnp
from jax import lax
from jax.experimental import pallas as pl
from jax.experimental.pallas import tpu as pltpu
from jax.sharding import PartitionSpec as P

HIGHEST = lax.Precision.HIGHEST
ROWS = 8
GROUP = 2
BOTH = ("leaf", "clusters")


def dot(a, b, ca=1, cb=0):
    return lax.dot_general(
        a, b, (((ca,), (cb,)), ((), ())), precision=HIGHEST, preferred_element_type=jnp.float32
    )


def across_lanes(tile, lane):
    return jnp.broadcast_to(tile[:, lane : lane + 1], tile.shape)


def row_of(ref, row):
    return jnp.broadcast_to(ref[pl.ds(row, 1), :], (ROWS, ref.shape[1]))


def inverse_factor(gram, scratch):
    size = gram.shape[0]
    blocks = size // ROWS
    sub = lax.broadcasted_iota(jnp.int32, (ROWS, size), 0)
    lane = lax.broadcasted_iota(jnp.int32, (ROWS, size), 1)
    rows = [gram[ROWS * i : ROWS * (i + 1), :] for i in range(blocks)]
    scaled = [None] * blocks
    used = 0
    for first in range(0, blocks, GROUP):
        last = first + GROUP
        ahead = min(last + 1, blocks)
        for k in range(first, last):
            cols = {
                i: [across_lanes(rows[i], ROWS * k + c) for c in range(ROWS)] for i in range(k, ahead)
            }
            pivots = jnp.ones((ROWS, size), jnp.float32)
            for j in range(0, ROWS, 2):
                pair = (lane == ROWS * k + j) | (lane == ROWS * k + j + 1)
                for i in range(k, ahead):
                    rows[i] = jnp.where(pair, 0.0, rows[i])
                rows[k] = jnp.where(pair & (lane == sub + ROWS * k), 1.0, rows[k])
                held = scratch.at[pl.ds(used, ROWS * (ROWS - j + 1)), :]
                used += ROWS * (ROWS - j + 1)
                held[pl.ds(0, ROWS), :] = rows[k]
                for n in range(j, ROWS):
                    held[pl.ds(ROWS * (n - j + 1), ROWS), :] = cols[k][n]
                a = row_of(held, ROWS + j)
                b = row_of(held, ROWS + j + 1)
                c = row_of(held, 2 * ROWS + j + 1)
                det = a * c - b * b
                inverse = pltpu.reciprocal(det, approx=True)
                inverse_a = pltpu.reciprocal(a, approx=True)
                ratio = b * inverse_a
                pivots = jnp.where(sub == j, a, jnp.where(sub == j + 1, det * inverse_a, pivots))
                row, next_row = row_of(held, j), row_of(held, j + 1)
                col_rows = [
                    (row_of(held, ROWS * (n - j + 1) + j), row_of(held, ROWS * (n - j + 1) + j + 1))
                    for n in range(j + 2, ROWS)
                ]
                for i in range(k, ahead):
                    u, v = cols[i][j], cols[i][j + 1]
                    f = (u * c - v * b) * inverse
                    g = (v * a - u * b) * inverse
                    if i == k:
                        f = jnp.where(sub > j + 1, f, jnp.where(sub == j + 1, ratio, 0.0))
                        g = jnp.where(sub > j + 1, g, 0.0)
                    for n in range(j + 2, ROWS):
                        x, y = col_rows[n - j - 2]
                        cols[i][n] = cols[i][n] - (f * x + g * y)
                    rows[i] = rows[i] - (f * row + g * next_row)
            kept = (lane <= sub + ROWS * k) | (lane >= ROWS * last)
            scaled[k] = jnp.where(kept, rows[k] * lax.rsqrt(pivots), 0.0)
        if ahead < blocks:
            done = jnp.concatenate(scaled[first:last], axis=0)
            change = dot(done.T[ROWS * ahead :, :], done)
            old = (lane >= ROWS * first) & (lane < ROWS * last)
            for i in range(ahead, blocks):
                piece = change[ROWS * (i - ahead) : ROWS * (i - ahead + 1), :]
                rows[i] = jnp.where(old, 0.0, rows[i]) - piece
    return jnp.concatenate(
        [jnp.where(lane <= sub + ROWS * k, scaled[k], 0.0) for k in range(blocks)], axis=0
    )


def scratch_rows(size):
    return size // ROWS * sum(ROWS * (ROWS - j + 1) for j in range(0, ROWS, 2))


def near_half(view, which, rows, chunks=None):
    chunks = rows // 128 if chunks is None else chunks
    return jnp.concatenate(
        [view[pl.ds(2 * c + which, rows, stride=2 * chunks), :] for c in range(chunks)], axis=1
    )


def handed_kernel(near, probes, handed):
    handed[...] = dot(probes[:, : handed.shape[1]].T, near_half(near, 1, probes.shape[0])).T


def rest_kernel(near, probes, samples, rest, handed_last):
    rows, columns = handed_last.shape
    rest[...] = samples[...] - dot(near_half(near, 0, rows), probes[...])
    handed_last[...] = dot(probes[:, probes.shape[1] - columns :].T, near_half(near, 1, rows)).T


def following_kernel(near, rest, following, _h, first, last, _hout):
    columns = first.shape[1]
    block = rest[...] - dot(near_half(near, 1, rest.shape[0]), following[...])
    first[...] = block[:, :columns]
    last[...] = block[:, columns:]


def leaf_kernel(rest, handed, probes, far, inverse, coefs, sample_coef, probe_coef, scratch):
    columns = far.shape[1]
    block = rest[...] - handed[...]
    far[...] = block
    gram = dot(block, block, 0, 0)
    cross = dot(block, probes[...], 0, 0)
    factor = inverse_factor(gram, scratch)
    inverse[...] = factor
    coef = dot(factor, jnp.concatenate([gram, cross], axis=1))
    coefs[...] = coef
    sample_coef[...] = coef[:, :columns]
    probe_coef[...] = coef[:, columns:]


def leaf_last_kernel(rest, handed, far, inverse, basis, sample_coef):
    basis[...] = dot(far[...], inverse[...], 1, 1)
    sample_coef[...] = dot(basis[...], rest[...] - handed[...], 0, 0)


def coupling_of(slots, couplings, level, node):
    subtree = lax.axis_size("leaf")
    index = subtree - (subtree >> level - 1) + (node >> 1)
    return couplings[0, slots[0, index], node & 1]


def member_node(level):
    return lax.axis_index("leaf") >> level - 1


def term_kernel(level, slots, couplings, mine, away, _theirs, _last, first, last):
    node = member_node(level)
    block = coupling_of(slots, couplings, level, node ^ 2)
    outer = (node == 0) | (node == 3)
    main = jnp.where(outer, mine[...], away[...])
    other = jnp.where(outer, away[...], mine[...])
    term = dot(block, main) + dot(block, other, 0, 0)
    first[...] = term[:, : first.shape[1]]
    last[...] = term[:, first.shape[1] :]


def corrected_kernel(level, trees, slots, couplings, one, two, first, out_first, out_last):
    columns = first.shape[1]
    node = member_node(level)
    block = coupling_of(slots, couplings, level, node)
    main, other = one[...], two[...]
    if trees:
        straight = (lax.axis_index("clusters") ^ node) & 1 == 1
        main, other = jnp.where(straight, main, other), jnp.where(straight, other, main)
    term = dot(block, main) + dot(block, other, 0, 0)
    out_first[...] = first[...] - term[:, :columns]
    out_last[...] = term[:, columns:]


def factor_kernel(mine, theirs, inverse, scratch):
    gram = dot(mine[...], mine[...], 0, 0) + dot(theirs[...], theirs[...], 0, 0)
    inverse[...] = inverse_factor(gram, scratch)


def write_basis(level, at, mine, theirs, inverse, bases):
    size = mine.shape[0]
    own = (lax.axis_index("leaf") >> level - 1) & 1
    for block, half in ((mine, own), (theirs, 1 - own)):
        rows = pl.ds(pl.multiple_of(half * size, size), size)
        bases[0, at, rows, :] = dot(block, inverse, 1, 1)


def basis_kernel(level, inverse, mine, theirs, basis):
    write_basis(level, 0, mine[...], theirs[...], inverse[...], basis)


def level_coefs(inverse, mine, theirs):
    own = jnp.concatenate([ref[...] for ref in mine], axis=1)
    sibling = jnp.concatenate([ref[...] for ref in theirs], axis=1)
    return dot(inverse, dot(mine[0][...], own, 0, 0) + dot(theirs[0][...], sibling, 0, 0))


def node_kernel(inverse, mine, mine_probes, theirs, theirs_probes, _last, coefs, first, probe_coef):
    columns = first.shape[1]
    coef = level_coefs(inverse[...], (mine, mine_probes), (theirs, theirs_probes))
    coefs[...] = coef
    first[...] = coef[:, :columns]
    probe_coef[...] = coef[:, columns:]


def node_last_kernel(inverse, mine, mine_last, theirs, theirs_last, term, last):
    both = dot(mine[...], mine_last[...], 0, 0) + dot(theirs[...], theirs_last[...], 0, 0)
    last[...] = dot(inverse[...], both) - term[...]


def top_kernel(level, inverse, *refs):
    factor = inverse[...]
    earlier, (bases, samples, probe_coef) = refs[6:-3], refs[-3:]
    coef = level_coefs(factor, refs[:3], refs[3:6])
    width = samples.shape[2]
    samples[0] = coef[:, :width]
    probe_coef[0] = coef[:, width:]
    for at, done in enumerate(earlier):
        bases[0, at] = done[0, 0]
    write_basis(level, len(earlier), refs[0][...], refs[3][...], factor, bases)


VMEM = pl.BlockSpec(memory_space=pltpu.VMEM)
SMEM = pl.BlockSpec(memory_space=pltpu.SMEM)
ANY = pl.BlockSpec(memory_space=pl.ANY)


def call(kernel, shapes, *operands, slots=None, flops=0, specs=None, out_specs=None, vmem=32, **options):
    outs = [jax.ShapeDtypeStruct(shape, jnp.float32) for shape in shapes]
    specs = [VMEM] * len(operands) if specs is None else specs
    out_specs = [VMEM] * len(outs) if out_specs is None else out_specs
    if slots is not None:
        operands = (slots,) + operands
        specs = [SMEM] + specs
    moved = 4 * (sum(o.size for o in operands) + sum(o.size for o in outs))
    return pl.pallas_call(
        kernel,
        out_shape=outs,
        in_specs=specs,
        out_specs=out_specs,
        compiler_params=pltpu.CompilerParams(vmem_limit_bytes=vmem * 2**20),
        cost_estimate=pl.CostEstimate(flops=flops, bytes_accessed=moved, transcendentals=0),
        **options,
    )(*operands)


def permuted(value, target):
    trees, subtree = lax.axis_size("clusters"), lax.axis_size("leaf")
    pairs = []
    for member in range(subtree):
        for tree in range(trees):
            to_tree, to_member = target(tree, member)
            if 0 <= to_tree < trees:
                pairs.append((member * trees + tree, to_member * trees + to_tree))
    return lax.ppermute(value, BOTH, pairs)


def flat_shift(value, by):
    subtree = lax.axis_size("leaf")
    return permuted(value, lambda tree, member: divmod(tree * subtree + member + by, subtree))


def swapped(value, mask):
    return permuted(value, lambda tree, member: (tree, member ^ mask))


def outward(value, half):
    return permuted(value, lambda tree, member: (tree - 1 if member < half else tree + 1, member))


def tree_swapped(value, odd):
    return permuted(value, lambda tree, member: (tree + 1 if tree & 1 == odd else tree - 1, member))


def body(samples, probes, near_blocks, couplings, node_slot):
    rows, width = probes.shape
    columns = couplings.shape[-1]
    subtree = lax.axis_size("leaf")
    levels = subtree.bit_length() - 1
    chunks = rows // 128
    near = near_blocks.reshape(rows, 2, chunks, 128).transpose(0, 2, 1, 3).reshape(-1, 128)
    work = 12 * rows * rows * width
    tall, tall_last = (rows, columns), (rows, width - columns)
    square, square_last = (columns, columns), (columns, width - columns)

    following = flat_shift(probes, -1)
    (handed,) = call(handed_kernel, [tall], near, probes, flops=work)
    handed = flat_shift(handed, 1)
    rest, handed_last = call(
        rest_kernel, [(rows, width), tall_last], near, probes, samples, flops=work
    )
    rest_first, rest_last, handed_last = call(
        following_kernel, [tall, tall_last, tall_last], near, rest, following, handed_last, flops=work,
        specs=[VMEM, VMEM, VMEM, ANY], out_specs=[VMEM, VMEM, ANY], input_output_aliases={3: 2},
    )
    handed_last = flat_shift(handed_last, 1)
    scratch = dict(scratch_shapes=[pltpu.VMEM((scratch_rows(columns), columns), jnp.float32)])
    both = (columns, columns + width)
    far, inverse, coefs, first, probe_coef = call(
        leaf_kernel, [tall, square, both, square, (columns, width)], rest_first, handed, probes,
        flops=work, **scratch,
    )
    leaf_basis, last = call(
        leaf_last_kernel, [tall, square_last], rest_last, handed_last, far, inverse, flops=work
    )

    ancestors = []
    below = None
    for level in range(1, levels + 1):
        copies = 2 ** (level - 1)
        count = subtree // copies
        if count == 4:
            theirs_coefs = swapped(coefs, copies)
            away = outward(probe_coef, 2 * copies)
            term_first, term_last = call(
                functools.partial(term_kernel, level), [square, square_last],
                couplings, probe_coef, away, theirs_coefs, last, slots=node_slot,
                specs=[VMEM, VMEM, VMEM, ANY, ANY],
            )
            first = first - swapped(term_first, 2 * copies)
            theirs_first = theirs_coefs[:, :columns] - swapped(term_first, 3 * copies)
            theirs_probe = theirs_coefs[:, columns:]
            term_last = swapped(term_last, 2 * copies)
        else:
            theirs_probe = swapped(probe_coef, copies)
            if count == 2:
                fields = [tree_swapped(probe_coef, odd) for odd in (0, 1)]
            else:
                even = (lax.axis_index("leaf") >> level - 1) & 1 == 0
                fields = [flat_shift(probe_coef, by) for by in (2 * copies, -2 * copies)]
                fields = [jnp.where(even, *fields), jnp.where(even, *fields[::-1])]
            first, term_last = call(
                functools.partial(corrected_kernel, level, count == 2), [square, square_last],
                couplings, *fields, first, slots=node_slot,
            )
            theirs_first = swapped(first, copies)
        if below is None:
            last = last - term_last
        else:
            (last,) = call(node_last_kernel, [square_last], *below, term_last)
        theirs_last = swapped(last, copies)
        mine, theirs = (first, last, probe_coef), (theirs_first, theirs_last, theirs_probe)
        (inverse,) = call(
            factor_kernel, [square], first, theirs_first, flops=8 * work if count == 4 else 0, **scratch
        )
        if level < levels:
            ancestors += call(
                functools.partial(basis_kernel, level), [(1, 1, 2 * columns, columns)],
                inverse, first, theirs_first,
            )
            below = inverse, first, last, theirs_first, theirs_last
            coefs, first, probe_coef = call(
                node_kernel, [both, square, (columns, width)],
                inverse, first, probe_coef, theirs_first, theirs_probe, last,
                specs=[VMEM] * 5 + [ANY],
            )
    transfer_bases, top_samples, top_probes = call(
        functools.partial(top_kernel, levels),
        [(1, levels, 2 * columns, columns), (1, columns, width), (1, columns, width)],
        inverse, *mine, *theirs, *ancestors,
    )
    return (leaf_basis, transfer_bases, top_samples, top_probes)


def solution(mesh):
    in_specs = (
        P(("clusters", "leaf"), None),
        P(("clusters", "leaf"), None),
        P(("clusters", "leaf"), None, None),
        P("clusters", None, None, None, None),
        P("clusters", None),
    )
    out_specs = (
        P(("clusters", "leaf"), None),
        P(("clusters", "leaf"), None, None, None),
        P("clusters", None, None),
        P("clusters", None, None),
    )
    return jax.shard_map(body, mesh=mesh, in_specs=in_specs, out_specs=out_specs, check_vma=False)
```

```python
import functools

import jax
import jax.numpy as jnp
from jax import lax
from jax.experimental import pallas as pl
from jax.experimental.pallas import tpu as pltpu
from jax.sharding import PartitionSpec as P

HIGHEST = lax.Precision.HIGHEST
ROWS = 8
GROUP = 4
BOTH = ("leaf", "clusters")


def dot(a, b, ca=1, cb=0):
    return lax.dot_general(
        a, b, (((ca,), (cb,)), ((), ())), precision=HIGHEST, preferred_element_type=jnp.float32
    )


def across_lanes(tile, lane):
    return jnp.broadcast_to(tile[:, lane : lane + 1], tile.shape)


def row_of(ref, row):
    return jnp.broadcast_to(ref[pl.ds(row, 1), :], (ROWS, ref.shape[1]))


def inverse_factor(gram, scratch):
    size = gram.shape[0]
    blocks = size // ROWS
    sub = lax.broadcasted_iota(jnp.int32, (ROWS, size), 0)
    lane = lax.broadcasted_iota(jnp.int32, (ROWS, size), 1)
    rows = [gram[ROWS * i : ROWS * (i + 1), :] for i in range(blocks)]
    scaled = [None] * blocks
    used = 0

    def pair_of(k, j):
        return (lane == ROWS * k + j) | (lane == ROWS * k + j + 1)

    def columns_of(tile, k):
        return [across_lanes(tile, ROWS * k + n) for n in range(ROWS)]

    def factors(cols, j, step):
        a, b, c, inverse = step[:4]
        u, v = cols[j], cols[j + 1]
        return (u * c - v * b) * inverse, (v * a - u * b) * inverse

    def eliminated(tile, cols, j, f, g, step):
        row, next_row, col_rows = step[4:]
        for n, (x, y) in enumerate(col_rows, j + 2):
            cols[n] = cols[n] - (f * x + g * y)
        return tile - (f * row + g * next_row)

    def diagonal(k):
        nonlocal used
        tile, cols, steps = rows[k], columns_of(rows[k], k), []
        pivots = jnp.ones((ROWS, size), jnp.float32)
        for j in range(0, ROWS, 2):
            tile = jnp.where(pair_of(k, j), jnp.where(lane == sub + ROWS * k, 1.0, 0.0), tile)
            held = scratch.at[pl.ds(used, ROWS * (ROWS - j + 1)), :]
            used += ROWS * (ROWS - j + 1)
            for n in range(j, ROWS):
                held[pl.ds(ROWS * (n - j + 1), ROWS), :] = cols[n]
            held[pl.ds(0, ROWS), :] = tile
            a = row_of(held, ROWS + j)
            b = row_of(held, ROWS + j + 1)
            c = row_of(held, 2 * ROWS + j + 1)
            det = a * c - b * b
            inverse = pltpu.reciprocal(det, approx=True)
            inverse_a = pltpu.reciprocal(a, approx=True)
            pivots = jnp.where(sub == j, a, jnp.where(sub == j + 1, det * inverse_a, pivots))
            col_rows = [
                (row_of(held, ROWS * (n - j + 1) + j), row_of(held, ROWS * (n - j + 1) + j + 1))
                for n in range(j + 2, ROWS)
            ]
            step = a, b, c, inverse, row_of(held, j), row_of(held, j + 1), col_rows
            steps.append(step)
            f, g = factors(cols, j, step)
            f = jnp.where(sub > j + 1, f, jnp.where(sub == j + 1, b * inverse_a, 0.0))
            g = jnp.where(sub > j + 1, g, 0.0)
            tile = eliminated(tile, cols, j, f, g, step)
        rows[k] = tile
        return steps, pivots

    def below(i, k, steps):
        tile, cols = rows[i], columns_of(rows[i], k)
        for j, step in zip(range(0, ROWS, 2), steps):
            f, g = factors(cols, j, step)
            tile = eliminated(jnp.where(pair_of(k, j), 0.0, tile), cols, j, f, g, step)
        rows[i] = tile

    waiting = None
    for first in range(0, blocks, GROUP):
        last = first + GROUP
        ahead = min(last + 1, blocks)
        for k in range(first, last):
            steps, pivots = diagonal(k)
            if waiting is not None:
                done, start, stop = waiting
                change = dot(done.T[ROWS * (stop + 1) :, :], done)
                old = (lane >= ROWS * start) & (lane < ROWS * stop)
                for i in range(stop + 1, blocks):
                    piece = change[ROWS * (i - stop - 1) : ROWS * (i - stop), :]
                    rows[i] = jnp.where(old, 0.0, rows[i]) - piece
                waiting = None
            for i in range(k + 1, ahead):
                below(i, k, steps)
            kept = (lane <= sub + ROWS * k) | (lane >= ROWS * last)
            scaled[k] = jnp.where(kept, rows[k] * lax.rsqrt(pivots), 0.0)
        if ahead < blocks:
            waiting = jnp.concatenate(scaled[first:last], axis=0), first, last
    return jnp.concatenate(
        [jnp.where(lane <= sub + ROWS * k, scaled[k], 0.0) for k in range(blocks)], axis=0
    )


def scratch_rows(size):
    return size // ROWS * sum(ROWS * (ROWS - j + 1) for j in range(0, ROWS, 2))


def near_half(view, which, rows, chunks=None):
    chunks = rows // 128 if chunks is None else chunks
    return jnp.concatenate(
        [view[pl.ds(2 * c + which, rows, stride=2 * chunks), :] for c in range(chunks)], axis=1
    )


def handed_kernel(near, probes, handed):
    handed[...] = dot(probes[:, : handed.shape[1]].T, near_half(near, 1, probes.shape[0])).T


def rest_kernel(near, probes, samples, rest, handed_last):
    rows, columns = handed_last.shape
    rest[...] = samples[...] - dot(near_half(near, 0, rows), probes[...])
    handed_last[...] = dot(probes[:, probes.shape[1] - columns :].T, near_half(near, 1, rows)).T


def following_kernel(near, rest, following, _h, first, last, _hout):
    columns = first.shape[1]
    block = rest[...] - dot(near_half(near, 1, rest.shape[0]), following[...])
    first[...] = block[:, :columns]
    last[...] = block[:, columns:]


def leaf_kernel(rest, handed, probes, far, inverse, sample_coef, probe_coef, scratch):
    columns = far.shape[1]
    block = rest[...] - handed[...]
    far[...] = block
    gram = dot(block, block, 0, 0)
    cross = dot(block, probes[...], 0, 0)
    factor = inverse_factor(gram, scratch)
    inverse[...] = factor
    coef = dot(factor, jnp.concatenate([gram, cross], axis=1))
    sample_coef[...] = coef[:, :columns]
    probe_coef[...] = coef[:, columns:]


def leaf_last_kernel(rest, handed, far, inverse, basis, sample_coef):
    basis[...] = dot(far[...], inverse[...], 1, 1)
    sample_coef[...] = dot(basis[...], rest[...] - handed[...], 0, 0)


def coupling_of(slots, couplings, level, node):
    subtree = lax.axis_size("leaf")
    index = subtree - (subtree >> level - 1) + (node >> 1)
    return couplings[0, slots[0, index], node & 1]


def member_node(level):
    return lax.axis_index("leaf") >> level - 1


def term_kernel(level, slots, couplings, mine, away, _last, first, last):
    node = member_node(level)
    block = coupling_of(slots, couplings, level, node ^ 2)
    outer = (node == 0) | (node == 3)
    main = jnp.where(outer, mine[...], away[...])
    other = jnp.where(outer, away[...], mine[...])
    term = dot(jnp.concatenate([block, block.T], axis=1), jnp.concatenate([main, other], axis=0))
    first[...] = term[:, : first.shape[1]]
    last[...] = term[:, first.shape[1] :]


def corrected_kernel(level, trees, slots, couplings, one, two, first, *outs):
    out_first, out_last = outs[-3:-1] if trees else outs
    columns = first.shape[1]
    node = member_node(level)
    block = coupling_of(slots, couplings, level, node)
    main, other = one[...], two[...]
    if trees:
        straight = (lax.axis_index("clusters") ^ node) & 1 == 1
        main, other = jnp.where(straight, main, other), jnp.where(straight, other, main)
    term = dot(jnp.concatenate([block, block.T], axis=1), jnp.concatenate([main, other], axis=0))
    out_first[...] = first[...] - term[:, :columns]
    out_last[...] = term[:, columns:]


def factor_kernel(mine, theirs, inverse, scratch):
    both = jnp.concatenate([mine[...], theirs[...]], axis=0)
    gram = dot(both, both, 0, 0)
    inverse[...] = inverse_factor(gram, scratch)


def write_basis(level, at, mine, theirs, inverse, bases):
    size = mine.shape[0]
    own = (lax.axis_index("leaf") >> level - 1) & 1
    for block, half in ((mine, own), (theirs, 1 - own)):
        rows = pl.ds(pl.multiple_of(half * size, size), size)
        bases[0, at, rows, :] = dot(block, inverse, 1, 1)


def basis_kernel(level, inverse, mine, theirs, basis):
    write_basis(level, 0, mine[...], theirs[...], inverse[...], basis)


def level_coefs(inverse, mine, theirs):
    own = jnp.concatenate(mine, axis=1)
    sibling = jnp.concatenate(theirs, axis=1)
    size = inverse.shape[0]
    both = jnp.concatenate([own, sibling], axis=0)
    return dot(inverse, dot(both[:, :size], both, 0, 0))


def node_kernel(inverse, mine, mine_probes, theirs, theirs_probes, _last, first, probe_coef, half):
    columns = first.shape[1]
    coef = level_coefs(inverse[...], (mine[...], mine_probes[...]), (theirs[...], theirs_probes[...]))
    first[...] = coef[:, :columns]
    probe_coef[...] = coef[:, columns:]
    width = half.shape[1]
    upper = lax.axis_index("leaf") & 1 == 1
    half[...] = jnp.where(upper, coef[:, columns + width :], coef[:, columns : columns + width])


def node_last_kernel(inverse, mine, mine_last, theirs, theirs_last, term, last):
    mine, theirs = mine[...], theirs[...]
    both = dot(mine, mine_last[...], 0, 0) + dot(theirs, theirs_last[...], 0, 0)
    last[...] = dot(inverse[...], both) - term[...]


def top_kernel(level, inverse, *refs):
    factor = inverse[...]
    earlier, (bases, samples, probe_coef) = refs[7:-3], refs[-3:]
    mine, theirs, (half, passed) = [r[...] for r in refs[:3]], [r[...] for r in refs[3:5]], refs[5:7]
    upper = lax.axis_index("leaf") & 1 == 1
    theirs.append(jnp.where(upper, passed[...], half[...]))
    theirs.append(jnp.where(upper, half[...], passed[...]))
    coef = level_coefs(factor, mine, theirs)
    width = samples.shape[2]
    samples[0] = coef[:, :width]
    probe_coef[0] = coef[:, width:]
    for at, done in enumerate(earlier):
        bases[0, at] = done[0, 0]
    write_basis(level, len(earlier), mine[0], theirs[0], factor, bases)


VMEM = pl.BlockSpec(memory_space=pltpu.VMEM)
SMEM = pl.BlockSpec(memory_space=pltpu.SMEM)
ANY = pl.BlockSpec(memory_space=pl.ANY)


def call(kernel, shapes, *operands, slots=None, flops=0, specs=None, out_specs=None, vmem=32, **options):
    outs = [jax.ShapeDtypeStruct(shape, jnp.float32) for shape in shapes]
    specs = [VMEM] * len(operands) if specs is None else specs
    out_specs = [VMEM] * len(outs) if out_specs is None else out_specs
    if slots is not None:
        operands = (slots,) + operands
        specs = [SMEM] + specs
    moved = 4 * (sum(o.size for o in operands) + sum(o.size for o in outs))
    return pl.pallas_call(
        kernel,
        out_shape=outs,
        in_specs=specs,
        out_specs=out_specs,
        compiler_params=pltpu.CompilerParams(vmem_limit_bytes=vmem * 2**20),
        cost_estimate=pl.CostEstimate(flops=flops, bytes_accessed=moved, transcendentals=0),
        **options,
    )(*operands)


def permuted(value, target):
    trees, subtree = lax.axis_size("clusters"), lax.axis_size("leaf")
    pairs = []
    for member in range(subtree):
        for tree in range(trees):
            to_tree, to_member = target(tree, member)
            if 0 <= to_tree < trees:
                pairs.append((member * trees + tree, to_member * trees + to_tree))
    return lax.ppermute(value, BOTH, pairs)


def flat_shift(value, by):
    subtree = lax.axis_size("leaf")
    return permuted(value, lambda tree, member: divmod(tree * subtree + member + by, subtree))


def swapped(value, mask):
    return permuted(value, lambda tree, member: (tree, member ^ mask))


def outward(value, half):
    return permuted(value, lambda tree, member: (tree - 1 if member < half else tree + 1, member))


def tree_swapped(value, odd):
    return permuted(value, lambda tree, member: (tree + 1 if tree & 1 == odd else tree - 1, member))


def body(samples, probes, near_blocks, couplings, node_slot):
    rows, width = probes.shape
    columns = couplings.shape[-1]
    subtree = lax.axis_size("leaf")
    levels = subtree.bit_length() - 1
    chunks = rows // 128
    near = near_blocks.reshape(rows, 2, chunks, 128).transpose(0, 2, 1, 3).reshape(-1, 128)
    work = 12 * rows * rows * width
    tall, tall_last = (rows, columns), (rows, width - columns)
    square, square_last = (columns, columns), (columns, width - columns)

    following = flat_shift(probes, -1)
    (handed,) = call(handed_kernel, [tall], near, probes, flops=work)
    handed = flat_shift(handed, 1)
    rest, handed_last = call(
        rest_kernel, [(rows, width), tall_last], near, probes, samples, flops=work
    )
    rest_first, rest_last, handed_last = call(
        following_kernel, [tall, tall_last, tall_last], near, rest, following, handed_last, flops=work,
        specs=[VMEM, VMEM, VMEM, ANY], out_specs=[VMEM, VMEM, ANY], input_output_aliases={3: 2},
    )
    handed_last = flat_shift(handed_last, 1)
    scratch = dict(scratch_shapes=[pltpu.VMEM((scratch_rows(columns), columns), jnp.float32)])
    far, inverse, first, probe_coef = call(
        leaf_kernel, [tall, square, square, (columns, width)], rest_first, handed, probes,
        flops=work, **scratch,
    )
    leaf_basis, last = call(
        leaf_last_kernel, [tall, square_last], rest_last, handed_last, far, inverse, flops=work
    )

    ancestors = []
    below = None
    for level in range(1, levels + 1):
        copies = 2 ** (level - 1)
        count = subtree // copies
        if count == 4:
            theirs_coefs = swapped(jnp.concatenate([first, probe_coef], axis=1), copies)
            away = outward(probe_coef, 2 * copies)
            term_first, term_last = call(
                functools.partial(term_kernel, level), [square, square_last],
                couplings, probe_coef, away, last, slots=node_slot, specs=[VMEM, VMEM, VMEM, ANY],
            )
            first = first - swapped(term_first, 2 * copies)
            theirs_first = theirs_coefs[:, :columns] - swapped(term_first, 3 * copies)
            theirs_probe = theirs_coefs[:, columns:]
            term_last = swapped(term_last, 2 * copies)
        else:
            correct = functools.partial(corrected_kernel, level, count == 2)
            if count == 2:
                fields = [tree_swapped(probe_coef, odd) for odd in (0, 1)]
                first, term_last, theirs_half = call(
                    correct, [square, square_last, half.shape],
                    couplings, *fields, first, swapped(half, copies), slots=node_slot,
                    specs=[VMEM, VMEM, VMEM, VMEM, ANY], out_specs=[VMEM, VMEM, ANY],
                    input_output_aliases={5: 2},
                )
                theirs_passed = swapped(theirs_half, 1)
            else:
                theirs_probe = swapped(probe_coef, copies)
                even = (lax.axis_index("leaf") >> level - 1) & 1 == 0
                fields = [flat_shift(probe_coef, by) for by in (2 * copies, -2 * copies)]
                fields = [jnp.where(even, *fields), jnp.where(even, *fields[::-1])]
                first, term_last = call(
                    correct, [square, square_last], couplings, *fields, first, slots=node_slot
                )
            theirs_first = swapped(first, copies)
        if below is None:
            last = last - term_last
        else:
            (last,) = call(node_last_kernel, [square_last], *below, term_last)
        theirs_last = swapped(last, copies)
        mine = first, last, probe_coef
        (inverse,) = call(
            factor_kernel, [square], first, theirs_first, flops=8 * work if count == 4 else 0, **scratch
        )
        if level < levels:
            ancestors += call(
                functools.partial(basis_kernel, level), [(1, 1, 2 * columns, columns)],
                inverse, first, theirs_first,
            )
            below = inverse, first, last, theirs_first, theirs_last
            first, probe_coef, half = call(
                node_kernel, [square, (columns, width), (columns, width // 2)],
                inverse, first, probe_coef, theirs_first, theirs_probe, last,
                specs=[VMEM] * 5 + [ANY],
            )
    transfer_bases, top_samples, top_probes = call(
        functools.partial(top_kernel, levels),
        [(1, levels, 2 * columns, columns), (1, columns, width), (1, columns, width)],
        inverse, *mine, theirs_first, theirs_last, theirs_half, theirs_passed, *ancestors,
    )
    return (leaf_basis, transfer_bases, top_samples, top_probes)


def solution(mesh):
    in_specs = (
        P(("clusters", "leaf"), None),
        P(("clusters", "leaf"), None),
        P(("clusters", "leaf"), None, None),
        P("clusters", None, None, None, None),
        P("clusters", None),
    )
    out_specs = (
        P(("clusters", "leaf"), None),
        P(("clusters", "leaf"), None, None, None),
        P("clusters", None, None),
        P("clusters", None, None),
    )
    return jax.shard_map(body, mesh=mesh, in_specs=in_specs, out_specs=out_specs, check_vma=False)
```

```python
import functools

import jax
import jax.numpy as jnp
from jax import lax
from jax.experimental import pallas as pl
from jax.experimental.pallas import tpu as pltpu
from jax.sharding import PartitionSpec as P

HIGHEST = lax.Precision.HIGHEST
ROWS = 8
GROUP = 4
BOTH = ("leaf", "clusters")


def dot(a, b, ca=1, cb=0):
    return lax.dot_general(
        a, b, (((ca,), (cb,)), ((), ())), precision=HIGHEST, preferred_element_type=jnp.float32
    )


def across_lanes(tile, lane):
    return jnp.broadcast_to(tile[:, lane : lane + 1], tile.shape)


def row_of(ref, row):
    return jnp.broadcast_to(ref[pl.ds(row, 1), :], (ROWS, ref.shape[1]))


def inverse_factor(gram, scratch):
    size = gram.shape[0]
    blocks = size // ROWS
    sub = lax.broadcasted_iota(jnp.int32, (ROWS, size), 0)
    lane = lax.broadcasted_iota(jnp.int32, (ROWS, size), 1)
    rows = [gram[ROWS * i : ROWS * (i + 1), :] for i in range(blocks)]
    scaled = [None] * blocks
    used = 0

    def pair_of(k, j):
        return (lane == ROWS * k + j) | (lane == ROWS * k + j + 1)

    def columns_of(tile, k):
        return [across_lanes(tile, ROWS * k + n) for n in range(ROWS)]

    def factors(cols, j, step):
        a, b, c, inverse = step[:4]
        u, v = cols[j], cols[j + 1]
        return (u * c - v * b) * inverse, (v * a - u * b) * inverse

    def eliminated(tile, cols, j, f, g, step):
        row, next_row, col_rows = step[4:]
        for n, (x, y) in enumerate(col_rows, j + 2):
            cols[n] = cols[n] - (f * x + g * y)
        return tile - (f * row + g * next_row)

    def diagonal(k):
        nonlocal used
        tile, cols, steps = rows[k], columns_of(rows[k], k), []
        pivots = jnp.ones((ROWS, size), jnp.float32)
        for j in range(0, ROWS, 2):
            tile = jnp.where(pair_of(k, j), jnp.where(lane == sub + ROWS * k, 1.0, 0.0), tile)
            held = scratch.at[pl.ds(used, ROWS * (ROWS - j + 1)), :]
            used += ROWS * (ROWS - j + 1)
            for n in range(j, ROWS):
                held[pl.ds(ROWS * (n - j + 1), ROWS), :] = cols[n]
            held[pl.ds(0, ROWS), :] = tile
            a = row_of(held, ROWS + j)
            b = row_of(held, ROWS + j + 1)
            c = row_of(held, 2 * ROWS + j + 1)
            det = a * c - b * b
            inverse = pltpu.reciprocal(det, approx=True)
            inverse_a = pltpu.reciprocal(a, approx=True)
            pivots = jnp.where(sub == j, a, jnp.where(sub == j + 1, det * inverse_a, pivots))
            col_rows = [
                (row_of(held, ROWS * (n - j + 1) + j), row_of(held, ROWS * (n - j + 1) + j + 1))
                for n in range(j + 2, ROWS)
            ]
            step = a, b, c, inverse, row_of(held, j), row_of(held, j + 1), col_rows
            steps.append(step)
            f, g = factors(cols, j, step)
            f = jnp.where(sub > j + 1, f, jnp.where(sub == j + 1, b * inverse_a, 0.0))
            g = jnp.where(sub > j + 1, g, 0.0)
            tile = eliminated(tile, cols, j, f, g, step)
        rows[k] = tile
        return steps, pivots

    def below(i, k, steps):
        tile, cols = rows[i], columns_of(rows[i], k)
        for j, step in zip(range(0, ROWS, 2), steps):
            f, g = factors(cols, j, step)
            tile = eliminated(jnp.where(pair_of(k, j), 0.0, tile), cols, j, f, g, step)
        rows[i] = tile

    waiting = None
    for first in range(0, blocks, GROUP):
        last = first + GROUP
        ahead = min(last + 1, blocks)
        for k in range(first, last):
            steps, pivots = diagonal(k)
            if waiting is not None:
                done, start, stop = waiting
                change = dot(done.T[ROWS * (stop + 1) :, :], done)
                old = (lane >= ROWS * start) & (lane < ROWS * stop)
                for i in range(stop + 1, blocks):
                    piece = change[ROWS * (i - stop - 1) : ROWS * (i - stop), :]
                    rows[i] = jnp.where(old, 0.0, rows[i]) - piece
                waiting = None
            for i in range(k + 1, ahead):
                below(i, k, steps)
            kept = (lane <= sub + ROWS * k) | (lane >= ROWS * last)
            scaled[k] = jnp.where(kept, rows[k] * lax.rsqrt(pivots), 0.0)
        if ahead < blocks:
            waiting = jnp.concatenate(scaled[first:last], axis=0), first, last
    return jnp.concatenate(
        [jnp.where(lane <= sub + ROWS * k, scaled[k], 0.0) for k in range(blocks)], axis=0
    )


def scratch_rows(size):
    return size // ROWS * sum(ROWS * (ROWS - j + 1) for j in range(0, ROWS, 2))


def near_half(view, which, rows, chunks=None):
    chunks = rows // 128 if chunks is None else chunks
    return jnp.concatenate(
        [view[pl.ds(2 * c + which, rows, stride=2 * chunks), :] for c in range(chunks)], axis=1
    )


def handed_kernel(near, probes, handed):
    handed[...] = dot(probes[:, : handed.shape[1]].T, near_half(near, 1, probes.shape[0])).T


def rest_kernel(near, probes, samples, rest, handed_last):
    rows, columns = handed_last.shape
    rest[...] = samples[...] - dot(near_half(near, 0, rows), probes[...])
    handed_last[...] = dot(probes[:, probes.shape[1] - columns :].T, near_half(near, 1, rows)).T


def following_kernel(near, rest, following, _h, first, last, _hout):
    columns = first.shape[1]
    block = rest[...] - dot(near_half(near, 1, rest.shape[0]), following[...])
    first[...] = block[:, :columns]
    last[...] = block[:, columns:]


def leaf_kernel(rest, handed, probes, far, inverse, sample_coef, probe_coef, scratch):
    columns = far.shape[1]
    block = rest[...] - handed[...]
    far[...] = block
    gram = dot(block, block, 0, 0)
    cross = dot(block, probes[...], 0, 0)
    factor = inverse_factor(gram, scratch)
    inverse[...] = factor
    coef = dot(factor, jnp.concatenate([gram, cross], axis=1))
    sample_coef[...] = coef[:, :columns]
    probe_coef[...] = coef[:, columns:]


def leaf_last_kernel(rest, handed, far, inverse, basis, sample_coef):
    basis[...] = dot(far[...], inverse[...], 1, 1)
    sample_coef[...] = dot(basis[...], rest[...] - handed[...], 0, 0)


def coupling_of(slots, couplings, level, node):
    subtree = lax.axis_size("leaf")
    index = subtree - (subtree >> level - 1) + (node >> 1)
    return couplings[0, slots[0, index], node & 1]


def member_node(level):
    return lax.axis_index("leaf") >> level - 1


def term_kernel(level, slots, couplings, mine, away, _last, first, last):
    node = member_node(level)
    block = coupling_of(slots, couplings, level, node ^ 2)
    outer = (node == 0) | (node == 3)
    main = jnp.where(outer, mine[...], away[...])
    other = jnp.where(outer, away[...], mine[...])
    term = dot(jnp.concatenate([block, block.T], axis=1), jnp.concatenate([main, other], axis=0))
    first[...] = term[:, : first.shape[1]]
    last[...] = term[:, first.shape[1] :]


def corrected_kernel(level, trees, slots, couplings, one, two, first, out_first, out_last):
    columns = first.shape[1]
    node = member_node(level)
    block = coupling_of(slots, couplings, level, node)
    main, other = one[...], two[...]
    if trees:
        straight = (lax.axis_index("clusters") ^ node) & 1 == 1
        main, other = jnp.where(straight, main, other), jnp.where(straight, other, main)
    term = dot(jnp.concatenate([block, block.T], axis=1), jnp.concatenate([main, other], axis=0))
    out_first[...] = first[...] - term[:, :columns]
    out_last[...] = term[:, columns:]


def factor_kernel(mine, theirs, inverse, scratch):
    both = jnp.concatenate([mine[...], theirs[...]], axis=0)
    gram = dot(both, both, 0, 0)
    inverse[...] = inverse_factor(gram, scratch)


def write_basis(level, at, mine, theirs, inverse, bases):
    size = mine.shape[0]
    own = (lax.axis_index("leaf") >> level - 1) & 1
    block = dot(jnp.concatenate([mine, theirs], axis=0), inverse, 1, 1)
    bases[0, at, pl.ds(pl.multiple_of(own * size, size), size), :] = block[:size]
    bases[0, at, pl.ds(pl.multiple_of((1 - own) * size, size), size), :] = block[size:]


def basis_kernel(level, inverse, mine, theirs, basis):
    write_basis(level, 0, mine[...], theirs[...], inverse[...], basis)


def level_coefs(inverse, mine, theirs):
    own = jnp.concatenate(mine, axis=1)
    sibling = jnp.concatenate(theirs, axis=1)
    size = inverse.shape[0]
    both = jnp.concatenate([own, sibling], axis=0)
    return dot(inverse, dot(both[:, :size], both, 0, 0))


def node_kernel(inverse, mine, mine_probes, theirs, theirs_probes, _last, first, probe_coef, half):
    columns = first.shape[1]
    coef = level_coefs(inverse[...], (mine[...], mine_probes[...]), (theirs[...], theirs_probes[...]))
    first[...] = coef[:, :columns]
    probe_coef[...] = coef[:, columns:]
    width = half.shape[1]
    upper = lax.axis_index("leaf") & 1 == 1
    half[...] = jnp.where(upper, coef[:, columns + width :], coef[:, columns : columns + width])


def node_last_kernel(inverse, mine, mine_last, theirs, theirs_last, term, *refs):
    mine, theirs = mine[...], theirs[...]
    both = dot(mine, mine_last[...], 0, 0) + dot(theirs, theirs_last[...], 0, 0)
    last = refs[0] if len(refs) == 1 else refs[1]
    last[...] = dot(inverse[...], both) - term[...]


def top_kernel(level, inverse, *refs):
    factor = inverse[...]
    earlier, (bases, samples, probe_coef) = refs[7:-3], refs[-3:]
    mine, theirs, (half, passed) = [r[...] for r in refs[:3]], [r[...] for r in refs[3:5]], refs[5:7]
    upper = lax.axis_index("leaf") & 1 == 1
    theirs.append(jnp.where(upper, passed[...], half[...]))
    theirs.append(jnp.where(upper, half[...], passed[...]))
    coef = level_coefs(factor, mine, theirs)
    width = samples.shape[2]
    samples[0] = coef[:, :width]
    probe_coef[0] = coef[:, width:]
    for at, done in enumerate(earlier):
        bases[0, at] = done[0, 0]
    write_basis(level, len(earlier), mine[0], theirs[0], factor, bases)


VMEM = pl.BlockSpec(memory_space=pltpu.VMEM)
SMEM = pl.BlockSpec(memory_space=pltpu.SMEM)
ANY = pl.BlockSpec(memory_space=pl.ANY)


def call(kernel, shapes, *operands, slots=None, flops=0, specs=None, out_specs=None, vmem=32, **options):
    outs = [jax.ShapeDtypeStruct(shape, jnp.float32) for shape in shapes]
    specs = [VMEM] * len(operands) if specs is None else specs
    out_specs = [VMEM] * len(outs) if out_specs is None else out_specs
    if slots is not None:
        operands = (slots,) + operands
        specs = [SMEM] + specs
    moved = 4 * (sum(o.size for o in operands) + sum(o.size for o in outs))
    return pl.pallas_call(
        kernel,
        out_shape=outs,
        in_specs=specs,
        out_specs=out_specs,
        compiler_params=pltpu.CompilerParams(vmem_limit_bytes=vmem * 2**20),
        cost_estimate=pl.CostEstimate(flops=flops, bytes_accessed=moved, transcendentals=0),
        **options,
    )(*operands)


def permuted(value, target):
    trees, subtree = lax.axis_size("clusters"), lax.axis_size("leaf")
    pairs = []
    for member in range(subtree):
        for tree in range(trees):
            to_tree, to_member = target(tree, member)
            if 0 <= to_tree < trees:
                pairs.append((member * trees + tree, to_member * trees + to_tree))
    return lax.ppermute(value, BOTH, pairs)


def flat_shift(value, by):
    subtree = lax.axis_size("leaf")
    return permuted(value, lambda tree, member: divmod(tree * subtree + member + by, subtree))


def swapped(value, mask):
    return permuted(value, lambda tree, member: (tree, member ^ mask))


def outward(value, half):
    return permuted(value, lambda tree, member: (tree - 1 if member < half else tree + 1, member))


def tree_swapped(value, odd):
    return permuted(value, lambda tree, member: (tree + 1 if tree & 1 == odd else tree - 1, member))


def body(samples, probes, near_blocks, couplings, node_slot):
    rows, width = probes.shape
    columns = couplings.shape[-1]
    subtree = lax.axis_size("leaf")
    levels = subtree.bit_length() - 1
    chunks = rows // 128
    near = near_blocks.reshape(rows, 2, chunks, 128).transpose(0, 2, 1, 3).reshape(-1, 128)
    work = 12 * rows * rows * width
    tall, tall_last = (rows, columns), (rows, width - columns)
    square, square_last = (columns, columns), (columns, width - columns)

    following = flat_shift(probes, -1)
    (handed,) = call(handed_kernel, [tall], near, probes, flops=work)
    handed = flat_shift(handed, 1)
    rest, handed_last = call(
        rest_kernel, [(rows, width), tall_last], near, probes, samples, flops=work
    )
    rest_first, rest_last, handed_last = call(
        following_kernel, [tall, tall_last, tall_last], near, rest, following, handed_last, flops=work,
        specs=[VMEM, VMEM, VMEM, ANY], out_specs=[VMEM, VMEM, ANY], input_output_aliases={3: 2},
    )
    handed_last = flat_shift(handed_last, 1)
    scratch = dict(scratch_shapes=[pltpu.VMEM((scratch_rows(columns), columns), jnp.float32)])
    far, inverse, first, probe_coef = call(
        leaf_kernel, [tall, square, square, (columns, width)], rest_first, handed, probes,
        flops=work, **scratch,
    )
    leaf_basis, last = call(
        leaf_last_kernel, [tall, square_last], rest_last, handed_last, far, inverse, flops=work
    )

    ancestors = []
    below = None
    for level in range(1, levels + 1):
        copies = 2 ** (level - 1)
        count = subtree // copies
        if count == 4:
            theirs_coefs = swapped(jnp.concatenate([first, probe_coef], axis=1), copies)
            away = outward(probe_coef, 2 * copies)
            term_first, term_last = call(
                functools.partial(term_kernel, level), [square, square_last],
                couplings, probe_coef, away, last, slots=node_slot, specs=[VMEM, VMEM, VMEM, ANY],
            )
            first = first - swapped(term_first, 2 * copies)
            theirs_first = theirs_coefs[:, :columns] - swapped(term_first, 3 * copies)
            theirs_probe = theirs_coefs[:, columns:]
            first, theirs_first, term_last = lax.optimization_barrier((first, theirs_first, term_last))
            term_last = swapped(term_last, 2 * copies)
        else:
            correct = functools.partial(corrected_kernel, level, count == 2)
            if count == 2:
                fields = [tree_swapped(probe_coef, odd) for odd in (0, 1)]
                theirs_half = swapped(half, copies)
            else:
                theirs_probe = swapped(probe_coef, copies)
                even = (lax.axis_index("leaf") >> level - 1) & 1 == 0
                fields = [flat_shift(probe_coef, by) for by in (2 * copies, -2 * copies)]
                fields = [jnp.where(even, *fields), jnp.where(even, *fields[::-1])]
            first, term_last = call(
                correct, [square, square_last], couplings, *fields, first, slots=node_slot
            )
            theirs_first = swapped(first, copies)
        if below is None:
            last = last - term_last
        else:
            if level < levels:
                (last,) = call(node_last_kernel, [square_last], *below, term_last)
            else:
                last, theirs_half = call(
                    node_last_kernel, [square_last, half.shape], *below, term_last, theirs_half,
                    specs=[VMEM] * 6 + [ANY], out_specs=[VMEM, ANY], input_output_aliases={6: 1},
                )
                theirs_passed = swapped(theirs_half, 1)
        theirs_last = swapped(last, copies)
        mine = first, last, probe_coef
        (inverse,) = call(
            factor_kernel, [square], first, theirs_first, flops=8 * work if count == 4 else 0, **scratch
        )
        if level < levels:
            ancestors += call(
                functools.partial(basis_kernel, level), [(1, 1, 2 * columns, columns)],
                inverse, first, theirs_first,
            )
            below = inverse, first, last, theirs_first, theirs_last
            first, probe_coef, half = call(
                node_kernel, [square, (columns, width), (columns, width // 2)],
                inverse, first, probe_coef, theirs_first, theirs_probe, last,
                specs=[VMEM] * 5 + [ANY],
            )
    transfer_bases, top_samples, top_probes = call(
        functools.partial(top_kernel, levels),
        [(1, levels, 2 * columns, columns), (1, columns, width), (1, columns, width)],
        inverse, *mine, theirs_first, theirs_last, theirs_half, theirs_passed, *ancestors,
    )
    return (leaf_basis, transfer_bases, top_samples, top_probes)


def solution(mesh):
    in_specs = (
        P(("clusters", "leaf"), None),
        P(("clusters", "leaf"), None),
        P(("clusters", "leaf"), None, None),
        P("clusters", None, None, None, None),
        P("clusters", None),
    )
    out_specs = (
        P(("clusters", "leaf"), None),
        P(("clusters", "leaf"), None, None, None),
        P("clusters", None, None),
        P("clusters", None, None),
    )
    return jax.shard_map(body, mesh=mesh, in_specs=in_specs, out_specs=out_specs, check_vma=False)
```

```python
import functools

import jax
import jax.numpy as jnp
from jax import lax
from jax.experimental import pallas as pl
from jax.experimental.pallas import tpu as pltpu
from jax.sharding import PartitionSpec as P

HIGHEST = lax.Precision.HIGHEST
ROWS = 8
GROUP = 4
BOTH = ("leaf", "clusters")


def dot(a, b, ca=1, cb=0):
    return lax.dot_general(
        a, b, (((ca,), (cb,)), ((), ())), precision=HIGHEST, preferred_element_type=jnp.float32
    )


def across_lanes(tile, lane):
    return jnp.broadcast_to(tile[:, lane : lane + 1], tile.shape)


def row_of(ref, row):
    return jnp.broadcast_to(ref[pl.ds(row, 1), :], (ROWS, ref.shape[1]))


def inverse_factor(gram, scratch):
    size = gram.shape[0]
    blocks = size // ROWS
    sub = lax.broadcasted_iota(jnp.int32, (ROWS, size), 0)
    lane = lax.broadcasted_iota(jnp.int32, (ROWS, size), 1)
    rows = [gram[ROWS * i : ROWS * (i + 1), :] for i in range(blocks)]
    scaled = [None] * blocks
    used = 0

    def pair_of(k, j):
        return (lane == ROWS * k + j) | (lane == ROWS * k + j + 1)

    def columns_of(tile, k):
        return [across_lanes(tile, ROWS * k + n) for n in range(ROWS)]

    def factors(u, v, step):
        a, b, c, inverse = step[:4]
        return (u * c - v * b) * inverse, (v * a - u * b) * inverse

    def diagonal(k):
        nonlocal used
        tile = rows[k]
        held = scratch.at[pl.ds(used, ROWS * ROWS), :]
        used += ROWS * ROWS
        for n, col in enumerate(columns_of(tile, k)):
            held[pl.ds(ROWS * n, ROWS), :] = col
        block = {(n, m): row_of(held, ROWS * m + n) for n in range(ROWS) for m in range(n + 1)}
        steps = []
        pivots = jnp.ones((ROWS, size), jnp.float32)
        for j in range(0, ROWS, 2):
            tile = jnp.where(pair_of(k, j), jnp.where(lane == sub + ROWS * k, 1.0, 0.0), tile)
            held = scratch.at[pl.ds(used, ROWS), :]
            used += ROWS
            held[...] = tile
            row, next_row = row_of(held, j), row_of(held, j + 1)
            a, b, c = block[j, j], block[j + 1, j], block[j + 1, j + 1]
            det = a * c - b * b
            inverse = pltpu.reciprocal(det, approx=True)
            inverse_a = pltpu.reciprocal(a, approx=True)
            pivots = jnp.where(sub == j, a, jnp.where(sub == j + 1, det * inverse_a, pivots))
            col_rows = [(block[n, j], block[n, j + 1]) for n in range(j + 2, ROWS)]
            step = a, b, c, inverse, row, next_row, col_rows
            steps.append(step)
            f, g = jnp.where(sub == j + 1, b * inverse_a, 0.0), jnp.zeros((ROWS, size), jnp.float32)
            for n in range(j + 2, ROWS):
                f_n, g_n = factors(block[n, j], block[n, j + 1], step)
                f, g = jnp.where(sub == n, f_n, f), jnp.where(sub == n, g_n, g)
                for m in range(j + 2, n + 1):
                    block[n, m] = block[n, m] - (f_n * block[m, j] + g_n * block[m, j + 1])
            tile = tile - (f * row + g * next_row)
        rows[k] = tile
        return steps, pivots

    def below(i, k, steps):
        tile, cols = rows[i], columns_of(rows[i], k)
        for j, step in zip(range(0, ROWS, 2), steps):
            row, next_row, col_rows = step[4:]
            f, g = factors(cols[j], cols[j + 1], step)
            for n, (x, y) in enumerate(col_rows, j + 2):
                cols[n] = cols[n] - (f * x + g * y)
            tile = jnp.where(pair_of(k, j), 0.0, tile) - (f * row + g * next_row)
        rows[i] = tile

    waiting = None
    for first in range(0, blocks, GROUP):
        last = first + GROUP
        ahead = min(last + 1, blocks)
        for k in range(first, last):
            steps, pivots = diagonal(k)
            if waiting is not None:
                done, start, stop = waiting
                change = dot(done.T[ROWS * (stop + 1) :, :], done)
                old = (lane >= ROWS * start) & (lane < ROWS * stop)
                for i in range(stop + 1, blocks):
                    piece = change[ROWS * (i - stop - 1) : ROWS * (i - stop), :]
                    rows[i] = jnp.where(old, 0.0, rows[i]) - piece
                waiting = None
            for i in range(k + 1, ahead):
                below(i, k, steps)
            kept = (lane <= sub + ROWS * k) | (lane >= ROWS * last)
            scaled[k] = jnp.where(kept, rows[k] * lax.rsqrt(pivots), 0.0)
        if ahead < blocks:
            waiting = jnp.concatenate(scaled[first:last], axis=0), first, last
    return jnp.concatenate(
        [jnp.where(lane <= sub + ROWS * k, scaled[k], 0.0) for k in range(blocks)], axis=0
    )


def scratch_rows(size):
    return size * (ROWS + ROWS // 2)


def near_half(view, which, rows, chunks=None):
    chunks = rows // 128 if chunks is None else chunks
    return jnp.concatenate(
        [view[pl.ds(2 * c + which, rows, stride=2 * chunks), :] for c in range(chunks)], axis=1
    )


def handed_kernel(near, probes, handed):
    handed[...] = dot(probes[:, : handed.shape[1]].T, near_half(near, 1, probes.shape[0])).T


def rest_kernel(near, probes, samples, rest, handed_last):
    rows, columns = handed_last.shape
    rest[...] = samples[...] - dot(near_half(near, 0, rows), probes[...])
    handed_last[...] = dot(probes[:, probes.shape[1] - columns :].T, near_half(near, 1, rows)).T


def following_kernel(near, rest, following, _h, first, last, _hout):
    columns = first.shape[1]
    block = rest[...] - dot(near_half(near, 1, rest.shape[0]), following[...])
    first[...] = block[:, :columns]
    last[...] = block[:, columns:]


def leaf_kernel(rest, handed, probes, far, inverse, sample_coef, probe_coef, scratch):
    columns = far.shape[1]
    block = rest[...] - handed[...]
    far[...] = block
    gram = dot(block, block, 0, 0)
    cross = dot(block, probes[...], 0, 0)
    factor = inverse_factor(gram, scratch)
    inverse[...] = factor
    coef = dot(factor, jnp.concatenate([gram, cross], axis=1))
    sample_coef[...] = coef[:, :columns]
    probe_coef[...] = coef[:, columns:]


def leaf_last_kernel(rest, handed, far, inverse, basis, sample_coef):
    basis[...] = dot(far[...], inverse[...], 1, 1)
    sample_coef[...] = dot(basis[...], rest[...] - handed[...], 0, 0)


def coupling_of(slots, couplings, level, node):
    subtree = lax.axis_size("leaf")
    index = subtree - (subtree >> level - 1) + (node >> 1)
    return couplings[0, slots[0, index], node & 1]


def member_node(level):
    return lax.axis_index("leaf") >> level - 1


def term_kernel(level, slots, couplings, mine, away, _last, first, last):
    node = member_node(level)
    block = coupling_of(slots, couplings, level, node ^ 2)
    outer = (node == 0) | (node == 3)
    main = jnp.where(outer, mine[...], away[...])
    other = jnp.where(outer, away[...], mine[...])
    term = dot(jnp.concatenate([block, block.T], axis=1), jnp.concatenate([main, other], axis=0))
    first[...] = term[:, : first.shape[1]]
    last[...] = term[:, first.shape[1] :]


def corrected_kernel(level, trees, slots, couplings, one, two, first, out_first, out_last):
    columns = first.shape[1]
    node = member_node(level)
    block = coupling_of(slots, couplings, level, node)
    main, other = one[...], two[...]
    if trees:
        straight = (lax.axis_index("clusters") ^ node) & 1 == 1
        main, other = jnp.where(straight, main, other), jnp.where(straight, other, main)
    term = dot(jnp.concatenate([block, block.T], axis=1), jnp.concatenate([main, other], axis=0))
    out_first[...] = first[...] - term[:, :columns]
    out_last[...] = term[:, columns:]


def factor_kernel(mine, theirs, inverse, scratch):
    both = jnp.concatenate([mine[...], theirs[...]], axis=0)
    gram = dot(both, both, 0, 0)
    inverse[...] = inverse_factor(gram, scratch)


def write_basis(level, at, mine, theirs, inverse, bases):
    size = mine.shape[0]
    own = (lax.axis_index("leaf") >> level - 1) & 1
    block = dot(jnp.concatenate([mine, theirs], axis=0), inverse, 1, 1)
    bases[0, at, pl.ds(pl.multiple_of(own * size, size), size), :] = block[:size]
    bases[0, at, pl.ds(pl.multiple_of((1 - own) * size, size), size), :] = block[size:]


def basis_kernel(level, inverse, mine, theirs, basis):
    write_basis(level, 0, mine[...], theirs[...], inverse[...], basis)


def level_coefs(inverse, mine, theirs):
    own = jnp.concatenate(mine, axis=1)
    sibling = jnp.concatenate(theirs, axis=1)
    size = inverse.shape[0]
    both = jnp.concatenate([own, sibling], axis=0)
    return dot(inverse, dot(both[:, :size], both, 0, 0))


def node_kernel(inverse, mine, mine_probes, theirs, theirs_probes, _last, first, probe_coef, half):
    columns = first.shape[1]
    coef = level_coefs(inverse[...], (mine[...], mine_probes[...]), (theirs[...], theirs_probes[...]))
    first[...] = coef[:, :columns]
    probe_coef[...] = coef[:, columns:]
    width = half.shape[1]
    upper = lax.axis_index("leaf") & 1 == 1
    half[...] = jnp.where(upper, coef[:, columns + width :], coef[:, columns : columns + width])


def node_last_kernel(inverse, mine, mine_last, theirs, theirs_last, term, *refs):
    mine, theirs = mine[...], theirs[...]
    both = dot(mine, mine_last[...], 0, 0) + dot(theirs, theirs_last[...], 0, 0)
    last = refs[0] if len(refs) == 1 else refs[1]
    last[...] = dot(inverse[...], both) - term[...]


def top_kernel(level, inverse, *refs):
    factor = inverse[...]
    earlier, (bases, samples, probe_coef) = refs[7:-3], refs[-3:]
    mine, theirs, (half, passed) = [r[...] for r in refs[:3]], [r[...] for r in refs[3:5]], refs[5:7]
    upper = lax.axis_index("leaf") & 1 == 1
    theirs.append(jnp.where(upper, passed[...], half[...]))
    theirs.append(jnp.where(upper, half[...], passed[...]))
    coef = level_coefs(factor, mine, theirs)
    width = samples.shape[2]
    samples[0] = coef[:, :width]
    probe_coef[0] = coef[:, width:]
    for at, done in enumerate(earlier):
        bases[0, at] = done[0, 0]
    write_basis(level, len(earlier), mine[0], theirs[0], factor, bases)


VMEM = pl.BlockSpec(memory_space=pltpu.VMEM)
SMEM = pl.BlockSpec(memory_space=pltpu.SMEM)
ANY = pl.BlockSpec(memory_space=pl.ANY)


def call(kernel, shapes, *operands, slots=None, flops=0, specs=None, out_specs=None, vmem=32, **options):
    outs = [jax.ShapeDtypeStruct(shape, jnp.float32) for shape in shapes]
    specs = [VMEM] * len(operands) if specs is None else specs
    out_specs = [VMEM] * len(outs) if out_specs is None else out_specs
    if slots is not None:
        operands = (slots,) + operands
        specs = [SMEM] + specs
    moved = 4 * (sum(o.size for o in operands) + sum(o.size for o in outs))
    return pl.pallas_call(
        kernel,
        out_shape=outs,
        in_specs=specs,
        out_specs=out_specs,
        compiler_params=pltpu.CompilerParams(vmem_limit_bytes=vmem * 2**20),
        cost_estimate=pl.CostEstimate(flops=flops, bytes_accessed=moved, transcendentals=0),
        **options,
    )(*operands)


def permuted(value, target):
    trees, subtree = lax.axis_size("clusters"), lax.axis_size("leaf")
    pairs = []
    for member in range(subtree):
        for tree in range(trees):
            to_tree, to_member = target(tree, member)
            if 0 <= to_tree < trees:
                pairs.append((member * trees + tree, to_member * trees + to_tree))
    return lax.ppermute(value, BOTH, pairs)


def flat_shift(value, by):
    subtree = lax.axis_size("leaf")
    return permuted(value, lambda tree, member: divmod(tree * subtree + member + by, subtree))


def swapped(value, mask):
    return permuted(value, lambda tree, member: (tree, member ^ mask))


def outward(value, half):
    return permuted(value, lambda tree, member: (tree - 1 if member < half else tree + 1, member))


def tree_swapped(value, odd):
    return permuted(value, lambda tree, member: (tree + 1 if tree & 1 == odd else tree - 1, member))


def body(samples, probes, near_blocks, couplings, node_slot):
    rows, width = probes.shape
    columns = couplings.shape[-1]
    subtree = lax.axis_size("leaf")
    levels = subtree.bit_length() - 1
    chunks = rows // 128
    near = near_blocks.reshape(rows, 2, chunks, 128).transpose(0, 2, 1, 3).reshape(-1, 128)
    work = 12 * rows * rows * width
    tall, tall_last = (rows, columns), (rows, width - columns)
    square, square_last = (columns, columns), (columns, width - columns)

    following = flat_shift(probes, -1)
    (handed,) = call(handed_kernel, [tall], near, probes, flops=work)
    handed = flat_shift(handed, 1)
    rest, handed_last = call(
        rest_kernel, [(rows, width), tall_last], near, probes, samples, flops=work
    )
    rest_first, rest_last, handed_last = call(
        following_kernel, [tall, tall_last, tall_last], near, rest, following, handed_last, flops=work,
        specs=[VMEM, VMEM, VMEM, ANY], out_specs=[VMEM, VMEM, ANY], input_output_aliases={3: 2},
    )
    handed_last = flat_shift(handed_last, 1)
    scratch = dict(scratch_shapes=[pltpu.VMEM((scratch_rows(columns), columns), jnp.float32)])
    far, inverse, first, probe_coef = call(
        leaf_kernel, [tall, square, square, (columns, width)], rest_first, handed, probes,
        flops=work, **scratch,
    )
    leaf_basis, last = call(
        leaf_last_kernel, [tall, square_last], rest_last, handed_last, far, inverse, flops=work
    )

    ancestors = []
    below = None
    for level in range(1, levels + 1):
        copies = 2 ** (level - 1)
        count = subtree // copies
        if count == 4:
            theirs_coefs = swapped(jnp.concatenate([first, probe_coef], axis=1), copies)
            away = outward(probe_coef, 2 * copies)
            term_first, term_last = call(
                functools.partial(term_kernel, level), [square, square_last],
                couplings, probe_coef, away, last, slots=node_slot, specs=[VMEM, VMEM, VMEM, ANY],
            )
            first = first - swapped(term_first, 2 * copies)
            theirs_first = theirs_coefs[:, :columns] - swapped(term_first, 3 * copies)
            theirs_probe = theirs_coefs[:, columns:]
            term_last = swapped(term_last, 2 * copies)
        else:
            correct = functools.partial(corrected_kernel, level, count == 2)
            if count == 2:
                fields = [tree_swapped(probe_coef, odd) for odd in (0, 1)]
                theirs_half = swapped(half, copies)
            else:
                theirs_probe = swapped(probe_coef, copies)
                even = (lax.axis_index("leaf") >> level - 1) & 1 == 0
                fields = [flat_shift(probe_coef, by) for by in (2 * copies, -2 * copies)]
                fields = [jnp.where(even, *fields), jnp.where(even, *fields[::-1])]
            first, term_last = call(
                correct, [square, square_last], couplings, *fields, first, slots=node_slot
            )
            theirs_first = swapped(first, copies)
        if below is None:
            last = last - term_last
        else:
            if level < levels:
                (last,) = call(node_last_kernel, [square_last], *below, term_last)
            else:
                last, theirs_half = call(
                    node_last_kernel, [square_last, half.shape], *below, term_last, theirs_half,
                    specs=[VMEM] * 6 + [ANY], out_specs=[VMEM, ANY], input_output_aliases={6: 1},
                )
                theirs_passed = swapped(theirs_half, 1)
        theirs_last = swapped(last, copies)
        mine = first, last, probe_coef
        (inverse,) = call(
            factor_kernel, [square], first, theirs_first, flops=8 * work if count == 4 else 0, **scratch
        )
        if level < levels:
            ancestors += call(
                functools.partial(basis_kernel, level), [(1, 1, 2 * columns, columns)],
                inverse, first, theirs_first,
            )
            below = inverse, first, last, theirs_first, theirs_last
            first, probe_coef, half = call(
                node_kernel, [square, (columns, width), (columns, width // 2)],
                inverse, first, probe_coef, theirs_first, theirs_probe, last,
                specs=[VMEM] * 5 + [ANY],
            )
    transfer_bases, top_samples, top_probes = call(
        functools.partial(top_kernel, levels),
        [(1, levels, 2 * columns, columns), (1, columns, width), (1, columns, width)],
        inverse, *mine, theirs_first, theirs_last, theirs_half, theirs_passed, *ancestors,
    )
    return (leaf_basis, transfer_bases, top_samples, top_probes)


def solution(mesh):
    in_specs = (
        P(("clusters", "leaf"), None),
        P(("clusters", "leaf"), None),
        P(("clusters", "leaf"), None, None),
        P("clusters", None, None, None, None),
        P("clusters", None),
    )
    out_specs = (
        P(("clusters", "leaf"), None),
        P(("clusters", "leaf"), None, None, None),
        P("clusters", None, None),
        P("clusters", None, None),
    )
    return jax.shard_map(body, mesh=mesh, in_specs=in_specs, out_specs=out_specs, check_vma=False)
```

```python
import functools

import jax
import jax.numpy as jnp
from jax import lax
from jax.experimental import pallas as pl
from jax.experimental.pallas import tpu as pltpu
from jax.sharding import PartitionSpec as P

HIGHEST = lax.Precision.HIGHEST
ROWS = 8
GROUP = 4
BOTH = ("leaf", "clusters")


def dot(a, b, ca=1, cb=0):
    return lax.dot_general(
        a, b, (((ca,), (cb,)), ((), ())), precision=HIGHEST, preferred_element_type=jnp.float32
    )


def across_lanes(tile, lane):
    return jnp.broadcast_to(tile[:, lane : lane + 1], tile.shape)


def row_of(ref, row):
    return jnp.broadcast_to(ref[pl.ds(row, 1), :], (ROWS, ref.shape[1]))


def inverse_factor(gram, scratch):
    size = gram.shape[0]
    blocks = size // ROWS
    sub = lax.broadcasted_iota(jnp.int32, (ROWS, size), 0)
    lane = lax.broadcasted_iota(jnp.int32, (ROWS, size), 1)
    rows = [gram[ROWS * i : ROWS * (i + 1), :] for i in range(blocks)]
    scaled = [None] * blocks
    used = 0

    def pair_of(k, j):
        return (lane == ROWS * k + j) | (lane == ROWS * k + j + 1)

    def columns_of(tile, k):
        return [across_lanes(tile, ROWS * k + n) for n in range(ROWS)]

    def factors(u, v, step):
        a, b, c, inverse = step[:4]
        return (u * c - v * b) * inverse, (v * a - u * b) * inverse

    def diagonal(k):
        nonlocal used
        tile = rows[k]
        held = scratch.at[pl.ds(used, ROWS * ROWS), :]
        used += ROWS * ROWS
        for n, col in enumerate(columns_of(tile, k)):
            held[pl.ds(ROWS * n, ROWS), :] = col
        block = {(n, m): row_of(held, ROWS * m + n) for n in range(ROWS) for m in range(n + 1)}
        steps = []
        pivots = jnp.ones((ROWS, size), jnp.float32)
        for j in range(0, ROWS, 2):
            tile = jnp.where(pair_of(k, j), jnp.where(lane == sub + ROWS * k, 1.0, 0.0), tile)
            held = scratch.at[pl.ds(used, ROWS), :]
            used += ROWS
            held[...] = tile
            row, next_row = row_of(held, j), row_of(held, j + 1)
            a, b, c = block[j, j], block[j + 1, j], block[j + 1, j + 1]
            det = a * c - b * b
            inverse = pltpu.reciprocal(det, approx=True)
            inverse_a = pltpu.reciprocal(a, approx=True)
            pivots = jnp.where(sub == j, a, jnp.where(sub == j + 1, det * inverse_a, pivots))
            col_rows = [(block[n, j], block[n, j + 1]) for n in range(j + 2, ROWS)]
            step = a, b, c, inverse, row, next_row, col_rows
            steps.append(step)
            f, g = jnp.where(sub == j + 1, b * inverse_a, 0.0), jnp.zeros((ROWS, size), jnp.float32)
            for n in range(j + 2, ROWS):
                f_n, g_n = factors(block[n, j], block[n, j + 1], step)
                f, g = jnp.where(sub == n, f_n, f), jnp.where(sub == n, g_n, g)
                for m in range(j + 2, n + 1):
                    block[n, m] = block[n, m] - (f_n * block[m, j] + g_n * block[m, j + 1])
            tile = tile - (f * row + g * next_row)
        rows[k] = tile
        return steps, pivots

    def below(i, k, steps):
        tile, cols = rows[i], columns_of(rows[i], k)
        for j, step in zip(range(0, ROWS, 2), steps):
            row, next_row, col_rows = step[4:]
            f, g = factors(cols[j], cols[j + 1], step)
            for n, (x, y) in enumerate(col_rows, j + 2):
                cols[n] = cols[n] - (f * x + g * y)
            tile = jnp.where(pair_of(k, j), 0.0, tile) - (f * row + g * next_row)
        rows[i] = tile

    waiting = None
    for first in range(0, blocks, GROUP):
        last = first + GROUP
        ahead = min(last + 1, blocks)
        for k in range(first, last):
            steps, pivots = diagonal(k)
            if waiting is not None:
                done, start, stop = waiting
                change = dot(done.T[ROWS * (stop + 1) :, :], done)
                old = (lane >= ROWS * start) & (lane < ROWS * stop)
                for i in range(stop + 1, blocks):
                    piece = change[ROWS * (i - stop - 1) : ROWS * (i - stop), :]
                    rows[i] = jnp.where(old, 0.0, rows[i]) - piece
                waiting = None
            for i in range(k + 1, ahead):
                below(i, k, steps)
            kept = (lane <= sub + ROWS * k) | (lane >= ROWS * last)
            scaled[k] = jnp.where(kept, rows[k] * lax.rsqrt(pivots), 0.0)
        if ahead < blocks:
            waiting = jnp.concatenate(scaled[first:last], axis=0), first, last
    return jnp.concatenate(
        [jnp.where(lane <= sub + ROWS * k, scaled[k], 0.0) for k in range(blocks)], axis=0
    )


def scratch_rows(size):
    return size * (ROWS + ROWS // 2)


def near_half(view, which, rows, chunks=None):
    chunks = rows // 128 if chunks is None else chunks
    return jnp.concatenate(
        [view[pl.ds(2 * c + which, rows, stride=2 * chunks), :] for c in range(chunks)], axis=1
    )


def handed_kernel(near, probes, handed):
    handed[...] = dot(probes[:, : handed.shape[1]].T, near_half(near, 1, probes.shape[0])).T


def rest_kernel(near, probes, samples, rest, handed_last):
    rows, columns = handed_last.shape
    rest[...] = samples[...] - dot(near_half(near, 0, rows), probes[...])
    handed_last[...] = dot(probes[:, probes.shape[1] - columns :].T, near_half(near, 1, rows)).T


def following_kernel(near, rest, following, _h, first, last, _hout):
    columns = first.shape[1]
    block = rest[...] - dot(near_half(near, 1, rest.shape[0]), following[...])
    first[...] = block[:, :columns]
    last[...] = block[:, columns:]


def leaf_kernel(rest, handed, probes, far, inverse, sample_coef, probe_coef, scratch):
    columns = far.shape[1]
    block = rest[...] - handed[...]
    far[...] = block
    gram = dot(block, block, 0, 0)
    cross = dot(block, probes[...], 0, 0)
    factor = inverse_factor(gram, scratch)
    inverse[...] = factor
    coef = dot(factor, jnp.concatenate([gram, cross], axis=1))
    sample_coef[...] = coef[:, :columns]
    probe_coef[...] = coef[:, columns:]


def leaf_last_kernel(rest, handed, far, inverse, basis, sample_coef):
    basis[...] = dot(far[...], inverse[...], 1, 1)
    sample_coef[...] = dot(basis[...], rest[...] - handed[...], 0, 0)


def coupling_of(slots, couplings, level, node):
    subtree = lax.axis_size("leaf")
    index = subtree - (subtree >> level - 1) + (node >> 1)
    return couplings[0, slots[0, index], node & 1]


def member_node(level):
    return lax.axis_index("leaf") >> level - 1


def term_kernel(level, at, slots, couplings, mine, away, out):
    node = member_node(level)
    block = coupling_of(slots, couplings, level, node ^ 2)
    outer = (node == 0) | (node == 3)
    cols = slice(at, at + out.shape[1])
    main = jnp.where(outer, mine[:, cols], away[:, cols])
    other = jnp.where(outer, away[:, cols], mine[:, cols])
    out[...] = dot(jnp.concatenate([block, block.T], axis=1), jnp.concatenate([main, other], axis=0))


def corrected_kernel(level, trees, slots, couplings, one, two, first, out_first, out_last):
    columns = first.shape[1]
    node = member_node(level)
    block = coupling_of(slots, couplings, level, node)
    main, other = one[...], two[...]
    if trees:
        straight = (lax.axis_index("clusters") ^ node) & 1 == 1
        main, other = jnp.where(straight, main, other), jnp.where(straight, other, main)
    term = dot(jnp.concatenate([block, block.T], axis=1), jnp.concatenate([main, other], axis=0))
    out_first[...] = first[...] - term[:, :columns]
    out_last[...] = term[:, columns:]


def factor_kernel(mine, theirs, inverse, scratch):
    both = jnp.concatenate([mine[...], theirs[...]], axis=0)
    gram = dot(both, both, 0, 0)
    inverse[...] = inverse_factor(gram, scratch)


def write_basis(level, at, mine, theirs, inverse, bases):
    size = mine.shape[0]
    own = (lax.axis_index("leaf") >> level - 1) & 1
    block = dot(jnp.concatenate([mine, theirs], axis=0), inverse, 1, 1)
    bases[0, at, pl.ds(pl.multiple_of(own * size, size), size), :] = block[:size]
    bases[0, at, pl.ds(pl.multiple_of((1 - own) * size, size), size), :] = block[size:]


def basis_kernel(level, inverse, mine, theirs, basis):
    write_basis(level, 0, mine[...], theirs[...], inverse[...], basis)


def level_coefs(inverse, mine, theirs):
    own = jnp.concatenate(mine, axis=1)
    sibling = jnp.concatenate(theirs, axis=1)
    size = inverse.shape[0]
    both = jnp.concatenate([own, sibling], axis=0)
    return dot(inverse, dot(both[:, :size], both, 0, 0))


def node_kernel(inverse, mine, mine_probes, theirs, theirs_probes, _last, first, probe_coef, half):
    columns = first.shape[1]
    coef = level_coefs(inverse[...], (mine[...], mine_probes[...]), (theirs[...], theirs_probes[...]))
    first[...] = coef[:, :columns]
    probe_coef[...] = coef[:, columns:]
    width = half.shape[1]
    upper = lax.axis_index("leaf") & 1 == 1
    half[...] = jnp.where(upper, coef[:, columns + width :], coef[:, columns : columns + width])


def node_last_kernel(inverse, mine, mine_last, theirs, theirs_last, term, *refs):
    mine, theirs = mine[...], theirs[...]
    both = dot(mine, mine_last[...], 0, 0) + dot(theirs, theirs_last[...], 0, 0)
    last = refs[0] if len(refs) == 1 else refs[1]
    last[...] = dot(inverse[...], both) - term[...]


def top_kernel(level, inverse, *refs):
    factor = inverse[...]
    earlier, (bases, samples, probe_coef) = refs[7:-3], refs[-3:]
    mine, theirs, (half, passed) = [r[...] for r in refs[:3]], [r[...] for r in refs[3:5]], refs[5:7]
    upper = lax.axis_index("leaf") & 1 == 1
    theirs.append(jnp.where(upper, passed[...], half[...]))
    theirs.append(jnp.where(upper, half[...], passed[...]))
    coef = level_coefs(factor, mine, theirs)
    width = samples.shape[2]
    samples[0] = coef[:, :width]
    probe_coef[0] = coef[:, width:]
    for at, done in enumerate(earlier):
        bases[0, at] = done[0, 0]
    write_basis(level, len(earlier), mine[0], theirs[0], factor, bases)


VMEM = pl.BlockSpec(memory_space=pltpu.VMEM)
SMEM = pl.BlockSpec(memory_space=pltpu.SMEM)
ANY = pl.BlockSpec(memory_space=pl.ANY)


def call(kernel, shapes, *operands, slots=None, flops=0, specs=None, out_specs=None, vmem=32, **options):
    outs = [jax.ShapeDtypeStruct(shape, jnp.float32) for shape in shapes]
    specs = [VMEM] * len(operands) if specs is None else specs
    out_specs = [VMEM] * len(outs) if out_specs is None else out_specs
    if slots is not None:
        operands = (slots,) + operands
        specs = [SMEM] + specs
    moved = 4 * (sum(o.size for o in operands) + sum(o.size for o in outs))
    return pl.pallas_call(
        kernel,
        out_shape=outs,
        in_specs=specs,
        out_specs=out_specs,
        compiler_params=pltpu.CompilerParams(vmem_limit_bytes=vmem * 2**20),
        cost_estimate=pl.CostEstimate(flops=flops, bytes_accessed=moved, transcendentals=0),
        **options,
    )(*operands)


def permuted(value, target):
    trees, subtree = lax.axis_size("clusters"), lax.axis_size("leaf")
    pairs = []
    for member in range(subtree):
        for tree in range(trees):
            to_tree, to_member = target(tree, member)
            if 0 <= to_tree < trees:
                pairs.append((member * trees + tree, to_member * trees + to_tree))
    return lax.ppermute(value, BOTH, pairs)


def flat_shift(value, by):
    subtree = lax.axis_size("leaf")
    return permuted(value, lambda tree, member: divmod(tree * subtree + member + by, subtree))


def swapped(value, mask):
    return permuted(value, lambda tree, member: (tree, member ^ mask))


def outward(value, half):
    return permuted(value, lambda tree, member: (tree - 1 if member < half else tree + 1, member))


def tree_swapped(value, odd):
    return permuted(value, lambda tree, member: (tree + 1 if tree & 1 == odd else tree - 1, member))


def body(samples, probes, near_blocks, couplings, node_slot):
    rows, width = probes.shape
    columns = couplings.shape[-1]
    subtree = lax.axis_size("leaf")
    levels = subtree.bit_length() - 1
    chunks = rows // 128
    near = near_blocks.reshape(rows, 2, chunks, 128).transpose(0, 2, 1, 3).reshape(-1, 128)
    work = 12 * rows * rows * width
    tall, tall_last = (rows, columns), (rows, width - columns)
    square, square_last = (columns, columns), (columns, width - columns)

    following = flat_shift(probes, -1)
    (handed,) = call(handed_kernel, [tall], near, probes, flops=work)
    handed = flat_shift(handed, 1)
    rest, handed_last = call(
        rest_kernel, [(rows, width), tall_last], near, probes, samples, flops=work
    )
    rest_first, rest_last, handed_last = call(
        following_kernel, [tall, tall_last, tall_last], near, rest, following, handed_last, flops=work,
        specs=[VMEM, VMEM, VMEM, ANY], out_specs=[VMEM, VMEM, ANY], input_output_aliases={3: 2},
    )
    handed_last = flat_shift(handed_last, 1)
    scratch = dict(scratch_shapes=[pltpu.VMEM((scratch_rows(columns), columns), jnp.float32)])
    far, inverse, first, probe_coef = call(
        leaf_kernel, [tall, square, square, (columns, width)], rest_first, handed, probes,
        flops=work, **scratch,
    )
    if subtree != 4:
        leaf_basis, last = call(
            leaf_last_kernel, [tall, square_last], rest_last, handed_last, far, inverse, flops=work
        )

    ancestors = []
    below = None
    for level in range(1, levels + 1):
        copies = 2 ** (level - 1)
        count = subtree // copies
        if count == 4:
            theirs_coefs = swapped(jnp.concatenate([first, probe_coef], axis=1), copies)
            away = outward(probe_coef, 2 * copies)
            if level == 1:
                away, handed_last = lax.optimization_barrier((away, handed_last))
            (term_first,) = call(
                functools.partial(term_kernel, level, 0), [square], couplings, probe_coef, away,
                slots=node_slot,
            )
            (term_last,) = call(
                functools.partial(term_kernel, level, columns), [square_last],
                couplings, probe_coef, away, slots=node_slot,
            )
            if level == 1:
                leaf_basis, last = call(
                    leaf_last_kernel, [tall, square_last], rest_last, handed_last, far, inverse,
                    flops=work,
                )
            term_first, term_twin = swapped(term_first, 2 * copies), swapped(term_first, 3 * copies)
            term_first, term_twin, theirs_coefs, last = lax.optimization_barrier(
                (term_first, term_twin, theirs_coefs, last)
            )
            first = first - term_first
            theirs_first = theirs_coefs[:, :columns] - term_twin
            theirs_probe = theirs_coefs[:, columns:]
            term_last = swapped(term_last, 2 * copies)
        else:
            correct = functools.partial(corrected_kernel, level, count == 2)
            if count == 2:
                fields = [tree_swapped(probe_coef, odd) for odd in (0, 1)]
                *fields, ancestors[-1] = lax.optimization_barrier((*fields, ancestors[-1]))
                theirs_half = swapped(half, copies)
            else:
                theirs_probe = swapped(probe_coef, copies)
                even = (lax.axis_index("leaf") >> level - 1) & 1 == 0
                fields = [flat_shift(probe_coef, by) for by in (2 * copies, -2 * copies)]
                fields = [jnp.where(even, *fields), jnp.where(even, *fields[::-1])]
            first, term_last = call(
                correct, [square, square_last], couplings, *fields, first, slots=node_slot
            )
            theirs_first = swapped(first, copies)
        if below is None:
            last = last - term_last
        else:
            if level < levels:
                (last,) = call(node_last_kernel, [square_last], *below, term_last)
            else:
                last, theirs_half = call(
                    node_last_kernel, [square_last, half.shape], *below, term_last, theirs_half,
                    specs=[VMEM] * 6 + [ANY], out_specs=[VMEM, ANY], input_output_aliases={6: 1},
                )
                theirs_passed = swapped(theirs_half, 1)
        theirs_last = swapped(last, copies)
        mine = first, last, probe_coef
        (inverse,) = call(
            factor_kernel, [square], first, theirs_first, flops=8 * work if count == 4 else 0, **scratch
        )
        if level < levels:
            ancestors += call(
                functools.partial(basis_kernel, level), [(1, 1, 2 * columns, columns)],
                inverse, first, theirs_first,
            )
            below = inverse, first, last, theirs_first, theirs_last
            first, probe_coef, half = call(
                node_kernel, [square, (columns, width), (columns, width // 2)],
                inverse, first, probe_coef, theirs_first, theirs_probe, last,
                specs=[VMEM] * 5 + [ANY],
            )
    transfer_bases, top_samples, top_probes = call(
        functools.partial(top_kernel, levels),
        [(1, levels, 2 * columns, columns), (1, columns, width), (1, columns, width)],
        inverse, *mine, theirs_first, theirs_last, theirs_half, theirs_passed, *ancestors,
    )
    return (leaf_basis, transfer_bases, top_samples, top_probes)


def solution(mesh):
    in_specs = (
        P(("clusters", "leaf"), None),
        P(("clusters", "leaf"), None),
        P(("clusters", "leaf"), None, None),
        P("clusters", None, None, None, None),
        P("clusters", None),
    )
    out_specs = (
        P(("clusters", "leaf"), None),
        P(("clusters", "leaf"), None, None, None),
        P("clusters", None, None),
        P("clusters", None, None),
    )
    return jax.shard_map(body, mesh=mesh, in_specs=in_specs, out_specs=out_specs, check_vma=False)
```

```python
import functools

import jax
import jax.numpy as jnp
from jax import lax
from jax.experimental import pallas as pl
from jax.experimental.pallas import tpu as pltpu
from jax.sharding import PartitionSpec as P

HIGHEST = lax.Precision.HIGHEST
ROWS = 8
GROUP = 4
BOTH = ("leaf", "clusters")


def dot(a, b, ca=1, cb=0):
    return lax.dot_general(
        a, b, (((ca,), (cb,)), ((), ())), precision=HIGHEST, preferred_element_type=jnp.float32
    )


def across_lanes(tile, lane):
    return jnp.broadcast_to(tile[:, lane : lane + 1], tile.shape)


def row_of(ref, row):
    return jnp.broadcast_to(ref[pl.ds(row, 1), :], (ROWS, ref.shape[1]))


def inverse_factor(gram, scratch):
    size = gram.shape[0]
    blocks = size // ROWS
    sub = lax.broadcasted_iota(jnp.int32, (ROWS, size), 0)
    lane = lax.broadcasted_iota(jnp.int32, (ROWS, size), 1)
    rows = [gram[ROWS * i : ROWS * (i + 1), :] for i in range(blocks)]
    scaled = [None] * blocks
    used = 0

    def pair_of(k, j):
        return (lane == ROWS * k + j) | (lane == ROWS * k + j + 1)

    def columns_of(tile, k):
        return [across_lanes(tile, ROWS * k + n) for n in range(ROWS)]

    def factors(u, v, step):
        a, b, c, inverse = step[:4]
        return (u * c - v * b) * inverse, (v * a - u * b) * inverse

    def diagonal(k):
        nonlocal used
        tile = rows[k]
        held = scratch.at[pl.ds(used, ROWS * ROWS), :]
        used += ROWS * ROWS
        for n, col in enumerate(columns_of(tile, k)):
            held[pl.ds(ROWS * n, ROWS), :] = col
        block = {(n, m): row_of(held, ROWS * m + n) for n in range(ROWS) for m in range(n + 1)}
        steps = []
        pivots = jnp.ones((ROWS, size), jnp.float32)
        for j in range(0, ROWS, 2):
            tile = jnp.where(pair_of(k, j), jnp.where(lane == sub + ROWS * k, 1.0, 0.0), tile)
            held = scratch.at[pl.ds(used, ROWS), :]
            used += ROWS
            held[...] = tile
            row, next_row = row_of(held, j), row_of(held, j + 1)
            a, b, c = block[j, j], block[j + 1, j], block[j + 1, j + 1]
            det = a * c - b * b
            inverse = pltpu.reciprocal(det, approx=True)
            inverse_a = pltpu.reciprocal(a, approx=True)
            pivots = jnp.where(sub == j, a, jnp.where(sub == j + 1, det * inverse_a, pivots))
            col_rows = [(block[n, j], block[n, j + 1]) for n in range(j + 2, ROWS)]
            step = a, b, c, inverse, row, next_row, col_rows
            steps.append(step)
            f, g = jnp.where(sub == j + 1, b * inverse_a, 0.0), jnp.zeros((ROWS, size), jnp.float32)
            for n in range(j + 2, ROWS):
                f_n, g_n = factors(block[n, j], block[n, j + 1], step)
                f, g = jnp.where(sub == n, f_n, f), jnp.where(sub == n, g_n, g)
                for m in range(j + 2, n + 1):
                    block[n, m] = block[n, m] - (f_n * block[m, j] + g_n * block[m, j + 1])
            tile = tile - (f * row + g * next_row)
        rows[k] = tile
        return steps, pivots

    def below(i, k, steps):
        tile, cols = rows[i], columns_of(rows[i], k)
        for j, step in zip(range(0, ROWS, 2), steps):
            row, next_row, col_rows = step[4:]
            f, g = factors(cols[j], cols[j + 1], step)
            for n, (x, y) in enumerate(col_rows, j + 2):
                cols[n] = cols[n] - (f * x + g * y)
            tile = jnp.where(pair_of(k, j), 0.0, tile) - (f * row + g * next_row)
        rows[i] = tile

    waiting = None
    for first in range(0, blocks, GROUP):
        last = first + GROUP
        ahead = min(last + 1, blocks)
        for k in range(first, last):
            steps, pivots = diagonal(k)
            if waiting is not None:
                done, start, stop = waiting
                change = dot(done.T[ROWS * (stop + 1) :, :], done)
                old = (lane >= ROWS * start) & (lane < ROWS * stop)
                for i in range(stop + 1, blocks):
                    piece = change[ROWS * (i - stop - 1) : ROWS * (i - stop), :]
                    rows[i] = jnp.where(old, 0.0, rows[i]) - piece
                waiting = None
            for i in range(k + 1, ahead):
                below(i, k, steps)
            kept = (lane <= sub + ROWS * k) | (lane >= ROWS * last)
            scaled[k] = jnp.where(kept, rows[k] * lax.rsqrt(pivots), 0.0)
        if ahead < blocks:
            waiting = jnp.concatenate(scaled[first:last], axis=0), first, last
    return jnp.concatenate(
        [jnp.where(lane <= sub + ROWS * k, scaled[k], 0.0) for k in range(blocks)], axis=0
    )


def scratch_rows(size):
    return size * (ROWS + ROWS // 2)


def near_half(view, which, rows, chunks=None):
    chunks = rows // 128 if chunks is None else chunks
    return jnp.concatenate(
        [view[pl.ds(2 * c + which, rows, stride=2 * chunks), :] for c in range(chunks)], axis=1
    )


def handed_kernel(near, probes, handed):
    handed[...] = dot(probes[:, : handed.shape[1]].T, near_half(near, 1, probes.shape[0])).T


def rest_kernel(near, probes, samples, rest, handed_last):
    rows, columns = handed_last.shape
    rest[...] = samples[...] - dot(near_half(near, 0, rows), probes[...])
    handed_last[...] = dot(probes[:, probes.shape[1] - columns :].T, near_half(near, 1, rows)).T


def following_kernel(near, rest, following, _h, first, last, _hout):
    columns = first.shape[1]
    block = rest[...] - dot(near_half(near, 1, rest.shape[0]), following[...])
    first[...] = block[:, :columns]
    last[...] = block[:, columns:]


def leaf_kernel(rest, handed, probes, far, inverse, sample_coef, probe_coef, scratch):
    columns = far.shape[1]
    block = rest[...] - handed[...]
    far[...] = block
    products = dot(block, jnp.concatenate([block, probes[...]], axis=1), 0, 0)
    factor = inverse_factor(products[:, :columns], scratch)
    inverse[...] = factor
    coef = dot(factor, products)
    probe_coef[...] = coef[:, columns:]
    sample_coef[...] = coef[:, :columns]


def leaf_last_kernel(rest, handed, far, inverse, basis, sample_coef):
    basis[...] = dot(far[...], inverse[...], 1, 1)
    sample_coef[...] = dot(basis[...], rest[...] - handed[...], 0, 0)


def coupling_of(slots, couplings, level, node):
    subtree = lax.axis_size("leaf")
    index = subtree - (subtree >> level - 1) + (node >> 1)
    return couplings[0, slots[0, index], node & 1]


def member_node(level):
    return lax.axis_index("leaf") >> level - 1


def term_kernel(level, at, slots, couplings, mine, away, out):
    node = member_node(level)
    block = coupling_of(slots, couplings, level, node ^ 2)
    outer = (node == 0) | (node == 3)
    cols = slice(at, at + out.shape[1])
    main = jnp.where(outer, mine[:, cols], away[:, cols])
    other = jnp.where(outer, away[:, cols], mine[:, cols])
    out[...] = dot(jnp.concatenate([block, block.T], axis=1), jnp.concatenate([main, other], axis=0))


def corrected_kernel(level, trees, slots, couplings, one, two, first, out_first, out_last):
    columns = first.shape[1]
    node = member_node(level)
    block = coupling_of(slots, couplings, level, node)
    main, other = one[...], two[...]
    if trees:
        straight = (lax.axis_index("clusters") ^ node) & 1 == 1
        main, other = jnp.where(straight, main, other), jnp.where(straight, other, main)
    term = dot(jnp.concatenate([block, block.T], axis=1), jnp.concatenate([main, other], axis=0))
    out_first[...] = first[...] - term[:, :columns]
    out_last[...] = term[:, columns:]


def factor_kernel(mine, theirs, inverse, scratch):
    both = jnp.concatenate([mine[...], theirs[...]], axis=0)
    gram = dot(both, both, 0, 0)
    inverse[...] = inverse_factor(gram, scratch)


def basis_of(level, mine, theirs, inverse, out):
    size = mine.shape[0]
    own = (lax.axis_index("leaf") >> level - 1) & 1
    block = dot(jnp.concatenate([mine, theirs], axis=0), inverse, 1, 1)
    out[pl.ds(pl.multiple_of(own * size, size), size), :] = block[:size]
    out[pl.ds(pl.multiple_of((1 - own) * size, size), size), :] = block[size:]


def basis_kernel(level, inverse, mine, theirs, basis):
    basis_of(level, mine[...], theirs[...], inverse[...], basis)


def level_products(inverse, size, own, sibling):
    own, sibling = jnp.concatenate(own, axis=1), jnp.concatenate(sibling, axis=1)
    both = jnp.concatenate([own, sibling], axis=0)
    return dot(inverse, dot(both[:, :size], both, 0, 0))


def node_first_kernel(inverse, mine, theirs, first):
    both = jnp.concatenate([mine[...], theirs[...]], axis=0)
    first[...] = dot(inverse[...], dot(both, both, 0, 0))


def node_kernel(inverse, mine, theirs, mine_probes, theirs_probes, _last, probe_coef, half):
    nodes = jnp.concatenate([mine[...], theirs[...]], axis=0)
    probes = jnp.concatenate([mine_probes[...], theirs_probes[...]], axis=0)
    coef = dot(inverse[...], dot(nodes, probes, 0, 0))
    probe_coef[...] = coef
    width = half.shape[1]
    upper = lax.axis_index("leaf") & 1 == 1
    half[...] = jnp.where(upper, coef[:, width:], coef[:, :width])


def node_last_kernel(inverse, mine, mine_last, theirs, theirs_last, term, *refs):
    nodes = jnp.concatenate([mine[...], theirs[...]], axis=0)
    both = jnp.concatenate([mine_last[...], theirs_last[...]], axis=0)
    last = refs[0] if len(refs) == 1 else refs[1]
    last[...] = dot(inverse[...], dot(nodes, both, 0, 0)) - term[...]


def top_kernel(level, inverse, *refs):
    mine, theirs, (half, passed) = refs[:3], refs[3:5], refs[5:7]
    earlier, (bases, samples, probe_coef, basis, coefs, done) = refs[7:-6], refs[-6:]
    copies = [
        pltpu.make_async_copy(one, bases.at[0, at], done.at[at]) for at, one in enumerate(earlier)
    ]
    for copy in copies:
        copy.start()
    factor = inverse[...]
    mine, theirs = [ref[...] for ref in mine], [ref[...] for ref in theirs]
    basis_of(level, mine[0], theirs[0], factor, basis)
    at = len(earlier)
    copies.append(pltpu.make_async_copy(basis, bases.at[0, at], done.at[at]))
    copies[-1].start()
    upper = lax.axis_index("leaf") & 1 == 1
    theirs.append(jnp.where(upper, passed[...], half[...]))
    theirs.append(jnp.where(upper, half[...], passed[...]))
    coef = level_products(factor, factor.shape[0], mine, theirs)
    width = samples.shape[2]
    coefs[0] = coef[:, :width]
    coefs[1] = coef[:, width:]
    for at, out in enumerate((samples, probe_coef)):
        copies.append(pltpu.make_async_copy(coefs.at[at], out.at[0], done.at[level + at]))
        copies[-1].start()
    for copy in copies:
        copy.wait()


VMEM = pl.BlockSpec(memory_space=pltpu.VMEM)
SMEM = pl.BlockSpec(memory_space=pltpu.SMEM)
ANY = pl.BlockSpec(memory_space=pl.ANY)


def call(kernel, shapes, *operands, slots=None, flops=0, specs=None, out_specs=None, vmem=32, **options):
    outs = [jax.ShapeDtypeStruct(shape, jnp.float32) for shape in shapes]
    specs = [VMEM] * len(operands) if specs is None else specs
    out_specs = [VMEM] * len(outs) if out_specs is None else out_specs
    if slots is not None:
        operands = (slots,) + operands
        specs = [SMEM] + specs
    moved = 4 * (sum(o.size for o in operands) + sum(o.size for o in outs))
    return pl.pallas_call(
        kernel,
        out_shape=outs,
        in_specs=specs,
        out_specs=out_specs,
        compiler_params=pltpu.CompilerParams(vmem_limit_bytes=vmem * 2**20),
        cost_estimate=pl.CostEstimate(flops=flops, bytes_accessed=moved, transcendentals=0),
        **options,
    )(*operands)


def permuted(value, target):
    trees, subtree = lax.axis_size("clusters"), lax.axis_size("leaf")
    pairs = []
    for member in range(subtree):
        for tree in range(trees):
            to_tree, to_member = target(tree, member)
            if 0 <= to_tree < trees:
                pairs.append((member * trees + tree, to_member * trees + to_tree))
    return lax.ppermute(value, BOTH, pairs)


def flat_shift(value, by):
    subtree = lax.axis_size("leaf")
    return permuted(value, lambda tree, member: divmod(tree * subtree + member + by, subtree))


def swapped(value, mask):
    return permuted(value, lambda tree, member: (tree, member ^ mask))


def outward(value, half):
    return permuted(value, lambda tree, member: (tree - 1 if member < half else tree + 1, member))


def tree_swapped(value, odd):
    return permuted(value, lambda tree, member: (tree + 1 if tree & 1 == odd else tree - 1, member))


def body(samples, probes, near_blocks, couplings, node_slot):
    rows, width = probes.shape
    columns = couplings.shape[-1]
    subtree = lax.axis_size("leaf")
    levels = subtree.bit_length() - 1
    chunks = rows // 128
    near = near_blocks.reshape(rows, 2, chunks, 128).transpose(0, 2, 1, 3).reshape(-1, 128)
    work = 12 * rows * rows * width
    tall, tall_last = (rows, columns), (rows, width - columns)
    square, square_last = (columns, columns), (columns, width - columns)

    following = flat_shift(probes, -1)
    (handed,) = call(handed_kernel, [tall], near, probes, flops=work)
    handed = flat_shift(handed, 1)
    rest, handed_last = call(
        rest_kernel, [(rows, width), tall_last], near, probes, samples, flops=work
    )
    rest_first, rest_last, handed_last = call(
        following_kernel, [tall, tall_last, tall_last], near, rest, following, handed_last, flops=work,
        specs=[VMEM, VMEM, VMEM, ANY], out_specs=[VMEM, VMEM, ANY], input_output_aliases={3: 2},
    )
    handed_last = flat_shift(handed_last, 1)
    scratch = dict(scratch_shapes=[pltpu.VMEM((scratch_rows(columns), columns), jnp.float32)])
    far, inverse, first, probe_coef = call(
        leaf_kernel, [tall, square, square, (columns, width)], rest_first, handed, probes,
        flops=work, **scratch,
    )
    if subtree != 4:
        leaf_basis, last = call(
            leaf_last_kernel, [tall, square_last], rest_last, handed_last, far, inverse, flops=work
        )

    ancestors = []
    below = None
    for level in range(1, levels + 1):
        copies = 2 ** (level - 1)
        count = subtree // copies
        if count == 4:
            theirs_coefs = swapped(jnp.concatenate([first, probe_coef], axis=1), copies)
            away = outward(probe_coef, 2 * copies)
            if level == 1:
                away, handed_last = lax.optimization_barrier((away, handed_last))
            (term_first,) = call(
                functools.partial(term_kernel, level, 0), [square], couplings, probe_coef, away,
                slots=node_slot,
            )
            if level == 1:
                leaf_basis, last = call(
                    leaf_last_kernel, [tall, square_last], rest_last, handed_last, far, inverse,
                    flops=work,
                )
            away, last = lax.optimization_barrier((away, last))
            (term_last,) = call(
                functools.partial(term_kernel, level, columns), [square_last],
                couplings, probe_coef, away, slots=node_slot,
            )
            term_first, term_twin = swapped(term_first, 2 * copies), swapped(term_first, 3 * copies)
            term_first, term_twin, theirs_coefs, last = lax.optimization_barrier(
                (term_first, term_twin, theirs_coefs, last)
            )
            first = first - term_first
            theirs_first = theirs_coefs[:, :columns] - term_twin
            theirs_probe = theirs_coefs[:, columns:]
            term_last = swapped(term_last, 2 * copies)
        else:
            correct = functools.partial(corrected_kernel, level, count == 2)
            if count == 2:
                fields = [tree_swapped(probe_coef, odd) for odd in (0, 1)]
                *fields, ancestors[-1] = lax.optimization_barrier((*fields, ancestors[-1]))
                theirs_half = swapped(half, copies)
            else:
                theirs_probe = swapped(probe_coef, copies)
                even = (lax.axis_index("leaf") >> level - 1) & 1 == 0
                fields = [flat_shift(probe_coef, by) for by in (2 * copies, -2 * copies)]
                fields = [jnp.where(even, *fields), jnp.where(even, *fields[::-1])]
            first, term_last = call(
                correct, [square, square_last], couplings, *fields, first, slots=node_slot
            )
            theirs_first = swapped(first, copies)
        if below is None:
            last = last - term_last
        else:
            if level < levels:
                (last,) = call(node_last_kernel, [square_last], *below, term_last)
            else:
                last, theirs_half = call(
                    node_last_kernel, [square_last, half.shape], *below, term_last, theirs_half,
                    specs=[VMEM] * 6 + [ANY], out_specs=[VMEM, ANY], input_output_aliases={6: 1},
                )
                theirs_passed = swapped(theirs_half, 1)
        theirs_last = swapped(last, copies)
        (inverse,) = call(
            factor_kernel, [square], first, theirs_first, flops=8 * work if count == 4 else 0, **scratch
        )
        if level < levels:
            ancestors += call(
                functools.partial(basis_kernel, level), [(2 * columns, columns)],
                inverse, first, theirs_first,
            )
            below = inverse, first, last, theirs_first, theirs_last
            probe_coef, half = call(
                node_kernel, [(columns, width), (columns, width // 2)],
                inverse, first, theirs_first, probe_coef, theirs_probe, last,
                specs=[VMEM] * 5 + [ANY],
            )
            (first,) = call(node_first_kernel, [square], inverse, first, theirs_first)
    transfer_bases, top_samples, top_probes = call(
        functools.partial(top_kernel, levels),
        [(1, levels, 2 * columns, columns), (1, columns, width), (1, columns, width)],
        inverse, first, last, probe_coef, theirs_first, theirs_last, theirs_half, theirs_passed,
        *ancestors, out_specs=[ANY] * 3,
        scratch_shapes=[
            pltpu.VMEM((2 * columns, columns), jnp.float32),
            pltpu.VMEM((2, columns, width), jnp.float32),
            pltpu.SemaphoreType.DMA((levels + 2,)),
        ],
    )
    return (leaf_basis, transfer_bases, top_samples, top_probes)


def solution(mesh):
    in_specs = (
        P(("clusters", "leaf"), None),
        P(("clusters", "leaf"), None),
        P(("clusters", "leaf"), None, None),
        P("clusters", None, None, None, None),
        P("clusters", None),
    )
    out_specs = (
        P(("clusters", "leaf"), None),
        P(("clusters", "leaf"), None, None, None),
        P("clusters", None, None),
        P("clusters", None, None),
    )
    return jax.shard_map(body, mesh=mesh, in_specs=in_specs, out_specs=out_specs, check_vma=False)
```

```python
import functools

import jax
import jax.numpy as jnp
from jax import lax
from jax.experimental import pallas as pl
from jax.experimental.pallas import tpu as pltpu
from jax.sharding import PartitionSpec as P

HIGHEST = lax.Precision.HIGHEST
ROWS = 8
GROUP = 4
BOTH = ("leaf", "clusters")


def dot(a, b, ca=1, cb=0):
    return lax.dot_general(
        a, b, (((ca,), (cb,)), ((), ())), precision=HIGHEST, preferred_element_type=jnp.float32
    )


def across_lanes(tile, lane):
    return jnp.broadcast_to(tile[:, lane : lane + 1], tile.shape)


def row_of(ref, row):
    return jnp.broadcast_to(ref[pl.ds(row, 1), :], (ROWS, ref.shape[1]))


def inverse_factor(gram, scratch):
    size = gram.shape[0]
    blocks = size // ROWS
    sub = lax.broadcasted_iota(jnp.int32, (ROWS, size), 0)
    lane = lax.broadcasted_iota(jnp.int32, (ROWS, size), 1)
    rows = [gram[ROWS * i : ROWS * (i + 1), :] for i in range(blocks)]
    scaled = [None] * blocks
    used = 0

    def pair_of(k, j):
        return (lane == ROWS * k + j) | (lane == ROWS * k + j + 1)

    def columns_of(tile, k):
        return [across_lanes(tile, ROWS * k + n) for n in range(ROWS)]

    def factors(u, v, step):
        a, b, c, inverse = step[:4]
        return (u * c - v * b) * inverse, (v * a - u * b) * inverse

    def diagonal(k):
        nonlocal used
        tile = rows[k]
        held = scratch.at[pl.ds(used, ROWS * ROWS), :]
        used += ROWS * ROWS
        for n, col in enumerate(columns_of(tile, k)):
            held[pl.ds(ROWS * n, ROWS), :] = col
        block = {(n, m): row_of(held, ROWS * m + n) for n in range(ROWS) for m in range(n + 1)}
        steps = []
        pivots = jnp.ones((ROWS, size), jnp.float32)
        for j in range(0, ROWS, 2):
            tile = jnp.where(pair_of(k, j), jnp.where(lane == sub + ROWS * k, 1.0, 0.0), tile)
            held = scratch.at[pl.ds(used, ROWS), :]
            used += ROWS
            held[...] = tile
            row, next_row = row_of(held, j), row_of(held, j + 1)
            a, b, c = block[j, j], block[j + 1, j], block[j + 1, j + 1]
            det = a * c - b * b
            inverse = pltpu.reciprocal(det, approx=True)
            inverse_a = pltpu.reciprocal(a, approx=True)
            pivots = jnp.where(sub == j, a, jnp.where(sub == j + 1, det * inverse_a, pivots))
            col_rows = [(block[n, j], block[n, j + 1]) for n in range(j + 2, ROWS)]
            step = a, b, c, inverse, row, next_row, col_rows
            steps.append(step)
            f, g = jnp.where(sub == j + 1, b * inverse_a, 0.0), jnp.zeros((ROWS, size), jnp.float32)
            for n in range(j + 2, ROWS):
                f_n, g_n = factors(block[n, j], block[n, j + 1], step)
                f, g = jnp.where(sub == n, f_n, f), jnp.where(sub == n, g_n, g)
                for m in range(j + 2, n + 1):
                    block[n, m] = block[n, m] - (f_n * block[m, j] + g_n * block[m, j + 1])
            tile = tile - (f * row + g * next_row)
        rows[k] = tile
        return steps, pivots

    def below(i, k, steps):
        tile, cols = rows[i], columns_of(rows[i], k)
        for j, step in zip(range(0, ROWS, 2), steps):
            row, next_row, col_rows = step[4:]
            f, g = factors(cols[j], cols[j + 1], step)
            for n, (x, y) in enumerate(col_rows, j + 2):
                cols[n] = cols[n] - (f * x + g * y)
            tile = jnp.where(pair_of(k, j), 0.0, tile) - (f * row + g * next_row)
        rows[i] = tile

    waiting = None
    for first in range(0, blocks, GROUP):
        last = first + GROUP
        ahead = min(last + 1, blocks)
        for k in range(first, last):
            steps, pivots = diagonal(k)
            if waiting is not None:
                done, start, stop = waiting
                change = dot(done.T[ROWS * (stop + 1) :, :], done)
                old = (lane >= ROWS * start) & (lane < ROWS * stop)
                for i in range(stop + 1, blocks):
                    piece = change[ROWS * (i - stop - 1) : ROWS * (i - stop), :]
                    rows[i] = jnp.where(old, 0.0, rows[i]) - piece
                waiting = None
            for i in range(k + 1, ahead):
                below(i, k, steps)
            kept = (lane <= sub + ROWS * k) | (lane >= ROWS * last)
            scaled[k] = jnp.where(kept, rows[k] * lax.rsqrt(pivots), 0.0)
        if ahead < blocks:
            waiting = jnp.concatenate(scaled[first:last], axis=0), first, last
    return jnp.concatenate(
        [jnp.where(lane <= sub + ROWS * k, scaled[k], 0.0) for k in range(blocks)], axis=0
    )


def scratch_rows(size):
    return size * (ROWS + ROWS // 2)


def near_half(view, which, rows, chunks=None):
    chunks = rows // 128 if chunks is None else chunks
    return jnp.concatenate(
        [view[pl.ds(2 * c + which, rows, stride=2 * chunks), :] for c in range(chunks)], axis=1
    )


def handed_kernel(near, probes, handed):
    handed[...] = dot(probes[:, : handed.shape[1]].T, near_half(near, 1, probes.shape[0])).T


def rest_kernel(near, probes, samples, rest, handed_last):
    rows, columns = handed_last.shape
    rest[...] = samples[...] - dot(near_half(near, 0, rows), probes[...])
    handed_last[...] = dot(probes[:, probes.shape[1] - columns :].T, near_half(near, 1, rows)).T


def following_kernel(near, rest, following, _h, first, last, _hout):
    columns = first.shape[1]
    block = rest[...] - dot(near_half(near, 1, rest.shape[0]), following[...])
    first[...] = block[:, :columns]
    last[...] = block[:, columns:]


def leaf_kernel(rest, handed, probes, far, inverse, sample_coef, probe_coef, scratch):
    columns = far.shape[1]
    block = rest[...] - handed[...]
    far[...] = block
    products = dot(block, jnp.concatenate([block, probes[...]], axis=1), 0, 0)
    factor = inverse_factor(products[:, :columns], scratch)
    inverse[...] = factor
    coef = dot(factor, products)
    probe_coef[...] = coef[:, columns:]
    sample_coef[...] = coef[:, :columns]


def leaf_last_kernel(rest, handed, far, inverse, basis, sample_coef):
    basis[...] = dot(far[...], inverse[...], 1, 1)
    sample_coef[...] = dot(basis[...], rest[...] - handed[...], 0, 0)


def coupling_of(slots, couplings, level, node):
    subtree = lax.axis_size("leaf")
    index = subtree - (subtree >> level - 1) + (node >> 1)
    return couplings[0, slots[0, index], node & 1]


def member_node(level):
    return lax.axis_index("leaf") >> level - 1


def term_kernel(level, at, slots, couplings, mine, away, out):
    node = member_node(level)
    block = coupling_of(slots, couplings, level, node ^ 2)
    outer = (node == 0) | (node == 3)
    cols = slice(at, at + out.shape[1])
    main = jnp.where(outer, mine[:, cols], away[:, cols])
    other = jnp.where(outer, away[:, cols], mine[:, cols])
    out[...] = dot(jnp.concatenate([block, block.T], axis=1), jnp.concatenate([main, other], axis=0))


def corrected_kernel(level, trees, slots, couplings, one, two, first, out_first, out_last):
    columns = first.shape[1]
    node = member_node(level)
    block = coupling_of(slots, couplings, level, node)
    main, other = one[...], two[...]
    if trees:
        straight = (lax.axis_index("clusters") ^ node) & 1 == 0
        main, other = jnp.where(straight, main, other), jnp.where(straight, other, main)
    term = dot(jnp.concatenate([block, block.T], axis=1), jnp.concatenate([main, other], axis=0))
    out_first[...] = first[...] - term[:, :columns]
    out_last[...] = term[:, columns:]


def factor_kernel(mine, theirs, inverse, scratch):
    both = jnp.concatenate([mine[...], theirs[...]], axis=0)
    gram = dot(both, both, 0, 0)
    inverse[...] = inverse_factor(gram, scratch)


def basis_of(level, mine, theirs, inverse, out):
    size = mine.shape[0]
    own = (lax.axis_index("leaf") >> level - 1) & 1
    block = dot(jnp.concatenate([mine, theirs], axis=0), inverse, 1, 1)
    out[pl.ds(pl.multiple_of(own * size, size), size), :] = block[:size]
    out[pl.ds(pl.multiple_of((1 - own) * size, size), size), :] = block[size:]


def basis_kernel(level, inverse, mine, theirs, basis):
    basis_of(level, mine[...], theirs[...], inverse[...], basis)


def level_products(inverse, size, own, sibling):
    own, sibling = jnp.concatenate(own, axis=1), jnp.concatenate(sibling, axis=1)
    both = jnp.concatenate([own, sibling], axis=0)
    return dot(inverse, dot(both[:, :size], both, 0, 0))


def node_first_kernel(inverse, mine, theirs, first):
    both = jnp.concatenate([mine[...], theirs[...]], axis=0)
    first[...] = dot(inverse[...], dot(both, both, 0, 0))


def node_kernel(inverse, mine, theirs, mine_probes, theirs_probes, _last, probe_coef, half):
    nodes = jnp.concatenate([mine[...], theirs[...]], axis=0)
    probes = jnp.concatenate([mine_probes[...], theirs_probes[...]], axis=0)
    coef = dot(inverse[...], dot(nodes, probes, 0, 0))
    probe_coef[...] = coef
    width = half.shape[1]
    upper = lax.axis_index("leaf") & 1 == 1
    half[...] = jnp.where(upper, coef[:, width:], coef[:, :width])


def node_last_kernel(inverse, mine, mine_last, theirs, theirs_last, term, *refs):
    nodes = jnp.concatenate([mine[...], theirs[...]], axis=0)
    both = jnp.concatenate([mine_last[...], theirs_last[...]], axis=0)
    last = refs[0] if len(refs) == 1 else refs[1]
    last[...] = dot(inverse[...], dot(nodes, both, 0, 0)) - term[...]


def top_kernel(level, inverse, *refs):
    mine, theirs, (half, passed) = refs[:3], refs[3:5], refs[5:7]
    earlier, (bases, samples, probe_coef, basis, coefs, done) = refs[7:-6], refs[-6:]
    copies = [
        pltpu.make_async_copy(one, bases.at[0, at], done.at[at]) for at, one in enumerate(earlier)
    ]
    for copy in copies:
        copy.start()
    factor = inverse[...]
    mine, theirs = [ref[...] for ref in mine], [ref[...] for ref in theirs]
    basis_of(level, mine[0], theirs[0], factor, basis)
    at = len(earlier)
    copies.append(pltpu.make_async_copy(basis, bases.at[0, at], done.at[at]))
    copies[-1].start()
    upper = lax.axis_index("leaf") & 1 == 1
    theirs.append(jnp.where(upper, passed[...], half[...]))
    theirs.append(jnp.where(upper, half[...], passed[...]))
    coef = level_products(factor, factor.shape[0], mine, theirs)
    width = samples.shape[2]
    coefs[0] = coef[:, :width]
    coefs[1] = coef[:, width:]
    for at, out in enumerate((samples, probe_coef)):
        copies.append(pltpu.make_async_copy(coefs.at[at], out.at[0], done.at[level + at]))
        copies[-1].start()
    for copy in copies:
        copy.wait()


VMEM = pl.BlockSpec(memory_space=pltpu.VMEM)
SMEM = pl.BlockSpec(memory_space=pltpu.SMEM)
ANY = pl.BlockSpec(memory_space=pl.ANY)


def call(kernel, shapes, *operands, slots=None, flops=0, specs=None, out_specs=None, vmem=32, **options):
    outs = [jax.ShapeDtypeStruct(shape, jnp.float32) for shape in shapes]
    specs = [VMEM] * len(operands) if specs is None else specs
    out_specs = [VMEM] * len(outs) if out_specs is None else out_specs
    if slots is not None:
        operands = (slots,) + operands
        specs = [SMEM] + specs
    moved = 4 * (sum(o.size for o in operands) + sum(o.size for o in outs))
    return pl.pallas_call(
        kernel,
        out_shape=outs,
        in_specs=specs,
        out_specs=out_specs,
        compiler_params=pltpu.CompilerParams(vmem_limit_bytes=vmem * 2**20),
        cost_estimate=pl.CostEstimate(flops=flops, bytes_accessed=moved, transcendentals=0),
        **options,
    )(*operands)


def permuted(value, target):
    trees, subtree = lax.axis_size("clusters"), lax.axis_size("leaf")
    pairs = []
    for member in range(subtree):
        for tree in range(trees):
            to_tree, to_member = target(tree, member)
            if 0 <= to_tree < trees:
                pairs.append((member * trees + tree, to_member * trees + to_tree))
    return lax.ppermute(value, BOTH, pairs)


def flat_shift(value, by):
    subtree = lax.axis_size("leaf")
    return permuted(value, lambda tree, member: divmod(tree * subtree + member + by, subtree))


def swapped(value, mask):
    return permuted(value, lambda tree, member: (tree, member ^ mask))


def outward(value, half):
    return permuted(value, lambda tree, member: (tree - 1 if member < half else tree + 1, member))


def tree_swapped(value, odd):
    return permuted(value, lambda tree, member: (tree + 1 if tree & 1 == odd else tree - 1, member))


def body(samples, probes, near_blocks, couplings, node_slot):
    rows, width = probes.shape
    columns = couplings.shape[-1]
    subtree = lax.axis_size("leaf")
    levels = subtree.bit_length() - 1
    chunks = rows // 128
    near = near_blocks.reshape(rows, 2, chunks, 128).transpose(0, 2, 1, 3).reshape(-1, 128)
    work = 12 * rows * rows * width
    tall, tall_last = (rows, columns), (rows, width - columns)
    square, square_last = (columns, columns), (columns, width - columns)

    following = flat_shift(probes, -1)
    (handed,) = call(handed_kernel, [tall], near, probes, flops=work)
    handed = flat_shift(handed, 1)
    rest, handed_last = call(
        rest_kernel, [(rows, width), tall_last], near, probes, samples, flops=work
    )
    rest_first, rest_last, handed_last = call(
        following_kernel, [tall, tall_last, tall_last], near, rest, following, handed_last, flops=work,
        specs=[VMEM, VMEM, VMEM, ANY], out_specs=[VMEM, VMEM, ANY], input_output_aliases={3: 2},
    )
    handed_last = flat_shift(handed_last, 1)
    scratch = dict(scratch_shapes=[pltpu.VMEM((scratch_rows(columns), columns), jnp.float32)])
    far, inverse, first, probe_coef = call(
        leaf_kernel, [tall, square, square, (columns, width)], rest_first, handed, probes,
        flops=work, **scratch,
    )
    if subtree != 4:
        leaf_basis, last = call(
            leaf_last_kernel, [tall, square_last], rest_last, handed_last, far, inverse, flops=work
        )

    ancestors = []
    below = None
    for level in range(1, levels + 1):
        copies = 2 ** (level - 1)
        count = subtree // copies
        if count == 4:
            theirs_coefs = swapped(jnp.concatenate([first, probe_coef], axis=1), copies)
            away = outward(probe_coef, 2 * copies)
            if level == 1:
                away, handed_last = lax.optimization_barrier((away, handed_last))
            (term_first,) = call(
                functools.partial(term_kernel, level, 0), [square], couplings, probe_coef, away,
                slots=node_slot,
            )
            if level == 1:
                leaf_basis, last = call(
                    leaf_last_kernel, [tall, square_last], rest_last, handed_last, far, inverse,
                    flops=work,
                )
            away, last = lax.optimization_barrier((away, last))
            (term_last,) = call(
                functools.partial(term_kernel, level, columns), [square_last],
                couplings, probe_coef, away, slots=node_slot,
            )
            term_first, term_twin = swapped(term_first, 2 * copies), swapped(term_first, 3 * copies)
            term_first, term_twin, theirs_coefs, last = lax.optimization_barrier(
                (term_first, term_twin, theirs_coefs, last)
            )
            first = first - term_first
            theirs_first = theirs_coefs[:, :columns] - term_twin
            theirs_probe = theirs_coefs[:, columns:]
            term_last = swapped(term_last, 2 * copies)
        else:
            correct = functools.partial(corrected_kernel, level, count == 2)
            if count == 2:
                fields = [tree_swapped(probe_coef, odd) for odd in (1, 0)]
                *fields, ancestors[-1] = lax.optimization_barrier((*fields, ancestors[-1]))
                theirs_half = swapped(half, copies)
            else:
                theirs_probe = swapped(probe_coef, copies)
                even = (lax.axis_index("leaf") >> level - 1) & 1 == 0
                fields = [flat_shift(probe_coef, by) for by in (2 * copies, -2 * copies)]
                fields = [jnp.where(even, *fields), jnp.where(even, *fields[::-1])]
            first, term_last = call(
                correct, [square, square_last], couplings, *fields, first, slots=node_slot
            )
            theirs_first = swapped(first, copies)
        if below is None:
            last = last - term_last
        else:
            if level < levels:
                (last,) = call(node_last_kernel, [square_last], *below, term_last)
            else:
                last, theirs_half = call(
                    node_last_kernel, [square_last, half.shape], *below, term_last, theirs_half,
                    specs=[VMEM] * 6 + [ANY], out_specs=[VMEM, ANY], input_output_aliases={6: 1},
                )
                theirs_passed = swapped(theirs_half, 1)
        theirs_last = swapped(last, copies)
        (inverse,) = call(
            factor_kernel, [square], first, theirs_first, flops=8 * work if count == 4 else 0, **scratch
        )
        if level < levels:
            ancestors += call(
                functools.partial(basis_kernel, level), [(2 * columns, columns)],
                inverse, first, theirs_first,
            )
            below = inverse, first, last, theirs_first, theirs_last
            probe_coef, half = call(
                node_kernel, [(columns, width), (columns, width // 2)],
                inverse, first, theirs_first, probe_coef, theirs_probe, last,
                specs=[VMEM] * 5 + [ANY],
            )
            (first,) = call(node_first_kernel, [square], inverse, first, theirs_first)
    transfer_bases, top_samples, top_probes = call(
        functools.partial(top_kernel, levels),
        [(1, levels, 2 * columns, columns), (1, columns, width), (1, columns, width)],
        inverse, first, last, probe_coef, theirs_first, theirs_last, theirs_half, theirs_passed,
        *ancestors, out_specs=[ANY] * 3,
        scratch_shapes=[
            pltpu.VMEM((2 * columns, columns), jnp.float32),
            pltpu.VMEM((2, columns, width), jnp.float32),
            pltpu.SemaphoreType.DMA((levels + 2,)),
        ],
    )
    return (leaf_basis, transfer_bases, top_samples, top_probes)


def solution(mesh):
    in_specs = (
        P(("clusters", "leaf"), None),
        P(("clusters", "leaf"), None),
        P(("clusters", "leaf"), None, None),
        P("clusters", None, None, None, None),
        P("clusters", None),
    )
    out_specs = (
        P(("clusters", "leaf"), None),
        P(("clusters", "leaf"), None, None, None),
        P("clusters", None, None),
        P("clusters", None, None),
    )
    return jax.shard_map(body, mesh=mesh, in_specs=in_specs, out_specs=out_specs, check_vma=False)
```

```python
import functools

import jax
import jax.numpy as jnp
from jax import lax
from jax.experimental import pallas as pl
from jax.experimental.pallas import tpu as pltpu
from jax.sharding import PartitionSpec as P

HIGHEST = lax.Precision.HIGHEST
ROWS = 8
GROUP = 4
BOTH = ("leaf", "clusters")


def dot(a, b, ca=1, cb=0):
    return lax.dot_general(
        a, b, (((ca,), (cb,)), ((), ())), precision=HIGHEST, preferred_element_type=jnp.float32
    )


def across_lanes(tile, lane):
    return jnp.broadcast_to(tile[:, lane : lane + 1], tile.shape)


def row_of(ref, row):
    return jnp.broadcast_to(ref[pl.ds(row, 1), :], (ROWS, ref.shape[1]))


def inverse_factor(gram, scratch):
    size = gram.shape[0]
    blocks = size // ROWS
    sub = lax.broadcasted_iota(jnp.int32, (ROWS, size), 0)
    lane = lax.broadcasted_iota(jnp.int32, (ROWS, size), 1)
    rows = [gram[ROWS * i : ROWS * (i + 1), :] for i in range(blocks)]
    scaled = [None] * blocks
    used = 0

    def pair_of(k, j):
        return (lane == ROWS * k + j) | (lane == ROWS * k + j + 1)

    def columns_of(tile, k):
        return [across_lanes(tile, ROWS * k + n) for n in range(ROWS)]

    def factors(u, v, step):
        a, b, c, inverse = step[:4]
        return (u * c - v * b) * inverse, (v * a - u * b) * inverse

    def diagonal(k):
        nonlocal used
        tile = rows[k]
        held = scratch.at[pl.ds(used, ROWS * ROWS), :]
        used += ROWS * ROWS
        for n, col in enumerate(columns_of(tile, k)):
            held[pl.ds(ROWS * n, ROWS), :] = col
        block = {(n, m): row_of(held, ROWS * m + n) for n in range(ROWS) for m in range(n + 1)}
        steps = []
        pivots = jnp.ones((ROWS, size), jnp.float32)
        for j in range(0, ROWS, 2):
            tile = jnp.where(pair_of(k, j), jnp.where(lane == sub + ROWS * k, 1.0, 0.0), tile)
            held = scratch.at[pl.ds(used, ROWS), :]
            used += ROWS
            held[...] = tile
            row, next_row = row_of(held, j), row_of(held, j + 1)
            a, b, c = block[j, j], block[j + 1, j], block[j + 1, j + 1]
            det = a * c - b * b
            inverse = pltpu.reciprocal(det, approx=True)
            inverse_a = pltpu.reciprocal(a, approx=True)
            pivots = jnp.where(sub == j, a, jnp.where(sub == j + 1, det * inverse_a, pivots))
            col_rows = [(block[n, j], block[n, j + 1]) for n in range(j + 2, ROWS)]
            step = a, b, c, inverse, row, next_row, col_rows
            steps.append(step)
            f, g = jnp.where(sub == j + 1, b * inverse_a, 0.0), jnp.zeros((ROWS, size), jnp.float32)
            for n in range(j + 2, ROWS):
                f_n, g_n = factors(block[n, j], block[n, j + 1], step)
                f, g = jnp.where(sub == n, f_n, f), jnp.where(sub == n, g_n, g)
                for m in range(j + 2, n + 1):
                    block[n, m] = block[n, m] - (f_n * block[m, j] + g_n * block[m, j + 1])
            tile = tile - (f * row + g * next_row)
        rows[k] = tile
        return steps, pivots

    def below(i, k, steps):
        tile, cols = rows[i], columns_of(rows[i], k)
        for j, step in zip(range(0, ROWS, 2), steps):
            row, next_row, col_rows = step[4:]
            f, g = factors(cols[j], cols[j + 1], step)
            for n, (x, y) in enumerate(col_rows, j + 2):
                cols[n] = cols[n] - (f * x + g * y)
            tile = jnp.where(pair_of(k, j), 0.0, tile) - (f * row + g * next_row)
        rows[i] = tile

    waiting = None
    for first in range(0, blocks, GROUP):
        last = first + GROUP
        ahead = min(last + 1, blocks)
        for k in range(first, last):
            steps, pivots = diagonal(k)
            if waiting is not None:
                done, start, stop = waiting
                change = dot(done.T[ROWS * (stop + 1) :, :], done)
                old = (lane >= ROWS * start) & (lane < ROWS * stop)
                for i in range(stop + 1, blocks):
                    piece = change[ROWS * (i - stop - 1) : ROWS * (i - stop), :]
                    rows[i] = jnp.where(old, 0.0, rows[i]) - piece
                waiting = None
            for i in range(k + 1, ahead):
                below(i, k, steps)
            kept = (lane <= sub + ROWS * k) | (lane >= ROWS * last)
            scaled[k] = jnp.where(kept, rows[k] * lax.rsqrt(pivots), 0.0)
        if ahead < blocks:
            waiting = jnp.concatenate(scaled[first:last], axis=0), first, last
    return jnp.concatenate(
        [jnp.where(lane <= sub + ROWS * k, scaled[k], 0.0) for k in range(blocks)], axis=0
    )


def scratch_rows(size):
    return size * (ROWS + ROWS // 2)


def near_half(view, which, rows, chunks=None):
    chunks = rows // 128 if chunks is None else chunks
    return jnp.concatenate(
        [view[pl.ds(2 * c + which, rows, stride=2 * chunks), :] for c in range(chunks)], axis=1
    )


def handed_kernel(near, probes, handed):
    handed[...] = dot(probes[:, : handed.shape[1]].T, near_half(near, 1, probes.shape[0])).T


def rest_kernel(near, probes, samples, rest, handed_last):
    rows, columns = handed_last.shape
    rest[...] = samples[...] - dot(near_half(near, 0, rows), probes[...])
    handed_last[...] = dot(probes[:, probes.shape[1] - columns :].T, near_half(near, 1, rows)).T


def following_kernel(near, rest, following, _h, first, last, _hout):
    columns = first.shape[1]
    block = rest[...] - dot(near_half(near, 1, rest.shape[0]), following[...])
    first[...] = block[:, :columns]
    last[...] = block[:, columns:]


def leaf_kernel(rest, handed, probes, far, inverse, sample_coef, probe_coef, scratch):
    columns = far.shape[1]
    block = rest[...] - handed[...]
    far[...] = block
    products = dot(block, jnp.concatenate([block, probes[...]], axis=1), 0, 0)
    factor = inverse_factor(products[:, :columns], scratch)
    inverse[...] = factor
    coef = dot(factor, products)
    probe_coef[...] = coef[:, columns:]
    sample_coef[...] = coef[:, :columns]


def leaf_last_kernel(rest, handed, far, inverse, basis, sample_coef):
    basis[...] = dot(far[...], inverse[...], 1, 1)
    sample_coef[...] = dot(basis[...], rest[...] - handed[...], 0, 0)


def member_node(level):
    return lax.axis_index("leaf") >> level - 1


def pick_kernel(slots, couplings, *blocks):
    subtree = lax.axis_size("leaf")
    for at, out in enumerate(blocks):
        level = at + 1
        node = member_node(level)
        if subtree >> at == 4:
            node = node ^ 2
        index = subtree - (subtree >> at) + (node >> 1)
        block = couplings[0, slots[0, index], node & 1]
        out[...] = jnp.concatenate([block, block.T], axis=1)


def term_kernel(level, at, block, mine, away, out):
    node = member_node(level)
    outer = (node == 0) | (node == 3)
    cols = slice(at, at + out.shape[1])
    main = jnp.where(outer, mine[:, cols], away[:, cols])
    other = jnp.where(outer, away[:, cols], mine[:, cols])
    out[...] = dot(block[...], jnp.concatenate([main, other], axis=0))


def corrected_kernel(level, trees, block, one, two, first, out_first, out_last):
    columns = first.shape[1]
    main, other = one[...], two[...]
    if trees:
        straight = (lax.axis_index("clusters") ^ member_node(level)) & 1 == 0
        main, other = jnp.where(straight, main, other), jnp.where(straight, other, main)
    term = dot(block[...], jnp.concatenate([main, other], axis=0))
    out_first[...] = first[...] - term[:, :columns]
    out_last[...] = term[:, columns:]


def factor_kernel(mine, theirs, inverse, scratch):
    both = jnp.concatenate([mine[...], theirs[...]], axis=0)
    gram = dot(both, both, 0, 0)
    inverse[...] = inverse_factor(gram, scratch)


def basis_of(level, mine, theirs, inverse, out):
    size = mine.shape[0]
    own = (lax.axis_index("leaf") >> level - 1) & 1
    block = dot(jnp.concatenate([mine, theirs], axis=0), inverse, 1, 1)
    out[pl.ds(pl.multiple_of(own * size, size), size), :] = block[:size]
    out[pl.ds(pl.multiple_of((1 - own) * size, size), size), :] = block[size:]


def basis_kernel(level, inverse, mine, theirs, basis):
    basis_of(level, mine[...], theirs[...], inverse[...], basis)


def level_products(inverse, size, own, sibling):
    own, sibling = jnp.concatenate(own, axis=1), jnp.concatenate(sibling, axis=1)
    both = jnp.concatenate([own, sibling], axis=0)
    return dot(inverse, dot(both[:, :size], both, 0, 0))


def node_first_kernel(inverse, mine, theirs, first):
    both = jnp.concatenate([mine[...], theirs[...]], axis=0)
    first[...] = dot(inverse[...], dot(both, both, 0, 0))


def node_kernel(mine, theirs, mine_probes, theirs_probes, inverse, probe_coef, half, scratch):
    nodes = jnp.concatenate([mine[...], theirs[...]], axis=0)
    probes = jnp.concatenate([mine_probes[...], theirs_probes[...]], axis=0)
    cross = dot(nodes, probes, 0, 0)
    factor = inverse_factor(dot(nodes, nodes, 0, 0), scratch)
    inverse[...] = factor
    coef = dot(factor, cross)
    probe_coef[...] = coef
    width = half.shape[1]
    upper = lax.axis_index("leaf") & 1 == 1
    half[...] = jnp.where(upper, coef[:, width:], coef[:, :width])


def node_last_kernel(inverse, mine, mine_last, theirs, theirs_last, term, *refs):
    nodes = jnp.concatenate([mine[...], theirs[...]], axis=0)
    both = jnp.concatenate([mine_last[...], theirs_last[...]], axis=0)
    last = refs[0] if len(refs) == 1 else refs[1]
    last[...] = dot(inverse[...], dot(nodes, both, 0, 0)) - term[...]


def top_kernel(level, inverse, *refs):
    mine, theirs, (half, passed) = refs[:3], refs[3:5], refs[5:7]
    earlier, (bases, samples, probe_coef, basis, coefs, done) = refs[7:-6], refs[-6:]
    copies = [
        pltpu.make_async_copy(one, bases.at[0, at], done.at[at]) for at, one in enumerate(earlier)
    ]
    for copy in copies:
        copy.start()
    factor = inverse[...]
    mine, theirs = [ref[...] for ref in mine], [ref[...] for ref in theirs]
    basis_of(level, mine[0], theirs[0], factor, basis)
    at = len(earlier)
    copies.append(pltpu.make_async_copy(basis, bases.at[0, at], done.at[at]))
    copies[-1].start()
    upper = lax.axis_index("leaf") & 1 == 1
    theirs.append(jnp.where(upper, passed[...], half[...]))
    theirs.append(jnp.where(upper, half[...], passed[...]))
    coef = level_products(factor, factor.shape[0], mine, theirs)
    width = samples.shape[2]
    coefs[0] = coef[:, :width]
    coefs[1] = coef[:, width:]
    for at, out in enumerate((samples, probe_coef)):
        copies.append(pltpu.make_async_copy(coefs.at[at], out.at[0], done.at[level + at]))
        copies[-1].start()
    for copy in copies:
        copy.wait()


VMEM = pl.BlockSpec(memory_space=pltpu.VMEM)
SMEM = pl.BlockSpec(memory_space=pltpu.SMEM)
ANY = pl.BlockSpec(memory_space=pl.ANY)


def call(kernel, shapes, *operands, slots=None, flops=0, specs=None, out_specs=None, vmem=32, **options):
    outs = [jax.ShapeDtypeStruct(shape, jnp.float32) for shape in shapes]
    specs = [VMEM] * len(operands) if specs is None else specs
    out_specs = [VMEM] * len(outs) if out_specs is None else out_specs
    if slots is not None:
        operands = (slots,) + operands
        specs = [SMEM] + specs
    moved = 4 * (sum(o.size for o in operands) + sum(o.size for o in outs))
    return pl.pallas_call(
        kernel,
        out_shape=outs,
        in_specs=specs,
        out_specs=out_specs,
        compiler_params=pltpu.CompilerParams(vmem_limit_bytes=vmem * 2**20),
        cost_estimate=pl.CostEstimate(flops=flops, bytes_accessed=moved, transcendentals=0),
        **options,
    )(*operands)


def permuted(value, target):
    trees, subtree = lax.axis_size("clusters"), lax.axis_size("leaf")
    pairs = []
    for member in range(subtree):
        for tree in range(trees):
            to_tree, to_member = target(tree, member)
            if 0 <= to_tree < trees:
                pairs.append((member * trees + tree, to_member * trees + to_tree))
    return lax.ppermute(value, BOTH, pairs)


def flat_shift(value, by):
    subtree = lax.axis_size("leaf")
    return permuted(value, lambda tree, member: divmod(tree * subtree + member + by, subtree))


def swapped(value, mask):
    return permuted(value, lambda tree, member: (tree, member ^ mask))


def outward(value, half):
    return permuted(value, lambda tree, member: (tree - 1 if member < half else tree + 1, member))


def tree_swapped(value, odd):
    return permuted(value, lambda tree, member: (tree + 1 if tree & 1 == odd else tree - 1, member))


def body(samples, probes, near_blocks, couplings, node_slot):
    rows, width = probes.shape
    columns = couplings.shape[-1]
    subtree = lax.axis_size("leaf")
    levels = subtree.bit_length() - 1
    chunks = rows // 128
    near = near_blocks.reshape(rows, 2, chunks, 128).transpose(0, 2, 1, 3).reshape(-1, 128)
    work = 12 * rows * rows * width
    tall, tall_last = (rows, columns), (rows, width - columns)
    square, square_last = (columns, columns), (columns, width - columns)

    following = flat_shift(probes, -1)
    (handed,) = call(handed_kernel, [tall], near, probes, flops=work)
    handed = flat_shift(handed, 1)
    blocks = call(pick_kernel, [(columns, 2 * columns)] * levels, couplings, slots=node_slot)
    following, *blocks = lax.optimization_barrier((following, *blocks))
    rest, handed_last = call(
        rest_kernel, [(rows, width), tall_last], near, probes, samples, flops=work
    )
    rest_first, rest_last, handed_last = call(
        following_kernel, [tall, tall_last, tall_last], near, rest, following, handed_last, flops=work,
        specs=[VMEM, VMEM, VMEM, ANY], out_specs=[VMEM, VMEM, ANY], input_output_aliases={3: 2},
    )
    handed_last = flat_shift(handed_last, 1)
    scratch = dict(scratch_shapes=[pltpu.VMEM((scratch_rows(columns), columns), jnp.float32)])
    far, inverse, first, probe_coef = call(
        leaf_kernel, [tall, square, square, (columns, width)], rest_first, handed, probes,
        flops=work, **scratch,
    )
    if subtree != 4:
        leaf_basis, last = call(
            leaf_last_kernel, [tall, square_last], rest_last, handed_last, far, inverse, flops=work
        )

    ancestors = []
    below = None
    for level in range(1, levels + 1):
        copies = 2 ** (level - 1)
        count = subtree // copies
        if count == 4:
            theirs_coefs = swapped(jnp.concatenate([first, probe_coef], axis=1), copies)
            away = outward(probe_coef, 2 * copies)
            if level == 1:
                away, handed_last = lax.optimization_barrier((away, handed_last))
            (term_first,) = call(
                functools.partial(term_kernel, level, 0), [square], blocks[level - 1], probe_coef, away
            )
            if level == 1:
                leaf_basis, last = call(
                    leaf_last_kernel, [tall, square_last], rest_last, handed_last, far, inverse,
                    flops=work,
                )
            away, last = lax.optimization_barrier((away, last))
            (term_last,) = call(
                functools.partial(term_kernel, level, columns), [square_last],
                blocks[level - 1], probe_coef, away,
            )
            term_first, term_twin = swapped(term_first, 2 * copies), swapped(term_first, 3 * copies)
            term_first, term_twin, theirs_coefs, last = lax.optimization_barrier(
                (term_first, term_twin, theirs_coefs, last)
            )
            first = first - term_first
            theirs_first = theirs_coefs[:, :columns] - term_twin
            theirs_probe = theirs_coefs[:, columns:]
            term_last = swapped(term_last, 2 * copies)
        else:
            correct = functools.partial(corrected_kernel, level, count == 2)
            if count == 2:
                fields = [tree_swapped(probe_coef, odd) for odd in (1, 0)]
                *fields, ancestors[-1] = lax.optimization_barrier((*fields, ancestors[-1]))
                theirs_half = swapped(half, copies)
            else:
                theirs_probe = swapped(probe_coef, copies)
                even = (lax.axis_index("leaf") >> level - 1) & 1 == 0
                fields = [flat_shift(probe_coef, by) for by in (2 * copies, -2 * copies)]
                fields = [jnp.where(even, *fields), jnp.where(even, *fields[::-1])]
            first, term_last = call(
                correct, [square, square_last], blocks[level - 1], *fields, first
            )
            theirs_first = swapped(first, copies)
        if below is None:
            last = last - term_last
        else:
            if level < levels:
                (last,) = call(node_last_kernel, [square_last], *below, term_last)
            else:
                last, theirs_half = call(
                    node_last_kernel, [square_last, half.shape], *below, term_last, theirs_half,
                    specs=[VMEM] * 6 + [ANY], out_specs=[VMEM, ANY], input_output_aliases={6: 1},
                )
                theirs_passed = swapped(theirs_half, 1)
        theirs_last = swapped(last, copies)
        if level == levels:
            (inverse,) = call(factor_kernel, [square], first, theirs_first, **scratch)
        else:
            inverse, probe_coef, half = call(
                node_kernel, [square, (columns, width), (columns, width // 2)],
                first, theirs_first, probe_coef, theirs_probe, flops=8 * work, **scratch,
            )
            probe_coef, half, last = lax.optimization_barrier((probe_coef, half, last))
            ancestors += call(
                functools.partial(basis_kernel, level), [(2 * columns, columns)],
                inverse, first, theirs_first,
            )
            below = inverse, first, last, theirs_first, theirs_last
            (first,) = call(node_first_kernel, [square], inverse, first, theirs_first)
    transfer_bases, top_samples, top_probes = call(
        functools.partial(top_kernel, levels),
        [(1, levels, 2 * columns, columns), (1, columns, width), (1, columns, width)],
        inverse, first, last, probe_coef, theirs_first, theirs_last, theirs_half, theirs_passed,
        *ancestors, out_specs=[ANY] * 3,
        scratch_shapes=[
            pltpu.VMEM((2 * columns, columns), jnp.float32),
            pltpu.VMEM((2, columns, width), jnp.float32),
            pltpu.SemaphoreType.DMA((levels + 2,)),
        ],
    )
    return (leaf_basis, transfer_bases, top_samples, top_probes)


def solution(mesh):
    in_specs = (
        P(("clusters", "leaf"), None),
        P(("clusters", "leaf"), None),
        P(("clusters", "leaf"), None, None),
        P("clusters", None, None, None, None),
        P("clusters", None),
    )
    out_specs = (
        P(("clusters", "leaf"), None),
        P(("clusters", "leaf"), None, None, None),
        P("clusters", None, None),
        P("clusters", None, None),
    )
    return jax.shard_map(body, mesh=mesh, in_specs=in_specs, out_specs=out_specs, check_vma=False)
```

```python
import functools

import jax
import jax.numpy as jnp
from jax import lax
from jax.experimental import pallas as pl
from jax.experimental.pallas import tpu as pltpu
from jax.sharding import PartitionSpec as P

HIGHEST = lax.Precision.HIGHEST
ROWS = 8
GROUP = 4
BOTH = ("leaf", "clusters")


def dot(a, b, ca=1, cb=0):
    return lax.dot_general(
        a, b, (((ca,), (cb,)), ((), ())), precision=HIGHEST, preferred_element_type=jnp.float32
    )


def across_lanes(tile, lane):
    return jnp.broadcast_to(tile[:, lane : lane + 1], tile.shape)


def row_of(ref, row):
    return jnp.broadcast_to(ref[pl.ds(row, 1), :], (ROWS, ref.shape[1]))


def inverse_factor(gram, scratch):
    size = gram.shape[0]
    blocks = size // ROWS
    sub = lax.broadcasted_iota(jnp.int32, (ROWS, size), 0)
    lane = lax.broadcasted_iota(jnp.int32, (ROWS, size), 1)
    rows = [gram[ROWS * i : ROWS * (i + 1), :] for i in range(blocks)]
    scaled = [None] * blocks
    used = 0

    def pair_of(k, j):
        return (lane == ROWS * k + j) | (lane == ROWS * k + j + 1)

    def columns_of(tile, k):
        return [across_lanes(tile, ROWS * k + n) for n in range(ROWS)]

    def factors(u, v, step):
        a, b, c, inverse = step[:4]
        return (u * c - v * b) * inverse, (v * a - u * b) * inverse

    def diagonal(k):
        nonlocal used
        tile = rows[k]
        held = scratch.at[pl.ds(used, ROWS * ROWS), :]
        used += ROWS * ROWS
        for n, col in enumerate(columns_of(tile, k)):
            held[pl.ds(ROWS * n, ROWS), :] = col
        block = {(n, m): row_of(held, ROWS * m + n) for n in range(ROWS) for m in range(n + 1)}
        steps = []
        pivots = jnp.ones((ROWS, size), jnp.float32)
        for j in range(0, ROWS, 2):
            tile = jnp.where(pair_of(k, j), jnp.where(lane == sub + ROWS * k, 1.0, 0.0), tile)
            held = scratch.at[pl.ds(used, ROWS), :]
            used += ROWS
            held[...] = tile
            row, next_row = row_of(held, j), row_of(held, j + 1)
            a, b, c = block[j, j], block[j + 1, j], block[j + 1, j + 1]
            det = a * c - b * b
            inverse = pltpu.reciprocal(det, approx=True)
            inverse_a = pltpu.reciprocal(a, approx=True)
            pivots = jnp.where(sub == j, a, jnp.where(sub == j + 1, det * inverse_a, pivots))
            col_rows = [(block[n, j], block[n, j + 1]) for n in range(j + 2, ROWS)]
            step = a, b, c, inverse, row, next_row, col_rows
            steps.append(step)
            f, g = jnp.where(sub == j + 1, b * inverse_a, 0.0), jnp.zeros((ROWS, size), jnp.float32)
            for n in range(j + 2, ROWS):
                f_n, g_n = factors(block[n, j], block[n, j + 1], step)
                f, g = jnp.where(sub == n, f_n, f), jnp.where(sub == n, g_n, g)
                for m in range(j + 2, n + 1):
                    block[n, m] = block[n, m] - (f_n * block[m, j] + g_n * block[m, j + 1])
            tile = tile - (f * row + g * next_row)
        rows[k] = tile
        return steps, pivots

    def below(i, k, steps):
        tile, cols = rows[i], columns_of(rows[i], k)
        for j, step in zip(range(0, ROWS, 2), steps):
            row, next_row, col_rows = step[4:]
            f, g = factors(cols[j], cols[j + 1], step)
            for n, (x, y) in enumerate(col_rows, j + 2):
                cols[n] = cols[n] - (f * x + g * y)
            tile = jnp.where(pair_of(k, j), 0.0, tile) - (f * row + g * next_row)
        rows[i] = tile

    waiting = None
    for first in range(0, blocks, GROUP):
        last = first + GROUP
        ahead = min(last + 1, blocks)
        for k in range(first, last):
            steps, pivots = diagonal(k)
            if waiting is not None:
                done, start, stop = waiting
                change = dot(done.T[ROWS * (stop + 1) :, :], done)
                old = (lane >= ROWS * start) & (lane < ROWS * stop)
                for i in range(stop + 1, blocks):
                    piece = change[ROWS * (i - stop - 1) : ROWS * (i - stop), :]
                    rows[i] = jnp.where(old, 0.0, rows[i]) - piece
                waiting = None
            for i in range(k + 1, ahead):
                below(i, k, steps)
            kept = (lane <= sub + ROWS * k) | (lane >= ROWS * last)
            scaled[k] = jnp.where(kept, rows[k] * lax.rsqrt(pivots), 0.0)
        if ahead < blocks:
            waiting = jnp.concatenate(scaled[first:last], axis=0), first, last
    return jnp.concatenate(
        [jnp.where(lane <= sub + ROWS * k, scaled[k], 0.0) for k in range(blocks)], axis=0
    )


def scratch_rows(size):
    return size * (ROWS + ROWS // 2)


def near_half(view, which, rows, chunks=None):
    chunks = rows // 128 if chunks is None else chunks
    return jnp.concatenate(
        [view[pl.ds(2 * c + which, rows, stride=2 * chunks), :] for c in range(chunks)], axis=1
    )


def handed_kernel(near, probes, handed):
    handed[...] = dot(probes[:, : handed.shape[1]].T, near_half(near, 1, probes.shape[0])).T


def rest_kernel(near, probes, samples, rest, handed_last):
    rows, columns = handed_last.shape
    rest[...] = samples[...] - dot(near_half(near, 0, rows), probes[...])
    handed_last[...] = dot(probes[:, probes.shape[1] - columns :].T, near_half(near, 1, rows)).T


def following_kernel(near, rest, following, _h, first, last, _hout):
    columns = first.shape[1]
    block = rest[...] - dot(near_half(near, 1, rest.shape[0]), following[...])
    first[...] = block[:, :columns]
    last[...] = block[:, columns:]


def leaf_kernel(rest, handed, probes, far, inverse, sample_coef, probe_coef, scratch):
    columns = far.shape[1]
    block = rest[...] - handed[...]
    far[...] = block
    products = dot(block, jnp.concatenate([block, probes[...]], axis=1), 0, 0)
    factor = inverse_factor(products[:, :columns], scratch)
    inverse[...] = factor
    coef = dot(factor, products)
    probe_coef[...] = coef[:, columns:]
    sample_coef[...] = coef[:, :columns]


def leaf_last_kernel(rest, handed, far, inverse, basis, sample_coef):
    basis[...] = dot(far[...], inverse[...], 1, 1)
    sample_coef[...] = dot(basis[...], rest[...] - handed[...], 0, 0)


def member_node(level):
    return lax.axis_index("leaf") >> level - 1


def pick_kernel(slots, couplings, *blocks):
    subtree = lax.axis_size("leaf")
    levels = subtree.bit_length() - 1
    for level, out in zip([*range(1, levels + 1), levels - 1], blocks):
        node = member_node(level)
        if out is blocks[-1]:
            node = node ^ 2
        index = subtree - (subtree >> level - 1) + (node >> 1)
        block = couplings[0, slots[0, index], node & 1]
        out[...] = jnp.concatenate([block, block.T], axis=1)


def quad_kernel(level, block, inner, outer, coef, out):
    node = member_node(level)
    inside = (node == 1) | (node == 2)
    main = jnp.where(inside, inner[...], outer[...])
    other = jnp.where(inside, outer[...], inner[...])
    out[...] = coef[...] - dot(block[...], jnp.concatenate([main, other], axis=0))


def term_kernel(level, block, mine, away, out):
    node = member_node(level)
    outer = (node == 0) | (node == 3)
    main = jnp.where(outer, mine[...], away[...])
    other = jnp.where(outer, away[...], mine[...])
    out[...] = dot(block[...], jnp.concatenate([main, other], axis=0))


def corrected_kernel(level, trees, block, one, two, first, out_first, out_last):
    columns = first.shape[1]
    main, other = one[...], two[...]
    if trees:
        straight = (lax.axis_index("clusters") ^ member_node(level)) & 1 == 0
        main, other = jnp.where(straight, main, other), jnp.where(straight, other, main)
    term = dot(block[...], jnp.concatenate([main, other], axis=0))
    out_first[...] = first[...] - term[:, :columns]
    out_last[...] = term[:, columns:]


def factor_kernel(mine, theirs, inverse, scratch):
    both = jnp.concatenate([mine[...], theirs[...]], axis=0)
    gram = dot(both, both, 0, 0)
    inverse[...] = inverse_factor(gram, scratch)


def basis_of(level, mine, theirs, inverse, out):
    size = mine.shape[0]
    own = (lax.axis_index("leaf") >> level - 1) & 1
    block = dot(jnp.concatenate([mine, theirs], axis=0), inverse, 1, 1)
    out[pl.ds(pl.multiple_of(own * size, size), size), :] = block[:size]
    out[pl.ds(pl.multiple_of((1 - own) * size, size), size), :] = block[size:]


def basis_kernel(level, inverse, mine, theirs, basis):
    basis_of(level, mine[...], theirs[...], inverse[...], basis)


def level_products(inverse, size, own, sibling):
    own, sibling = jnp.concatenate(own, axis=1), jnp.concatenate(sibling, axis=1)
    both = jnp.concatenate([own, sibling], axis=0)
    return dot(inverse, dot(both[:, :size], both, 0, 0))


def node_first_kernel(inverse, mine, theirs, first):
    both = jnp.concatenate([mine[...], theirs[...]], axis=0)
    first[...] = dot(inverse[...], dot(both, both, 0, 0))


def node_kernel(mine, theirs, mine_probes, theirs_probes, inverse, probe_coef, half, scratch):
    nodes = jnp.concatenate([mine[...], theirs[...]], axis=0)
    probes = jnp.concatenate([mine_probes[...], theirs_probes[...]], axis=0)
    cross = dot(nodes, probes, 0, 0)
    factor = inverse_factor(dot(nodes, nodes, 0, 0), scratch)
    inverse[...] = factor
    coef = dot(factor, cross)
    probe_coef[...] = coef
    width = half.shape[1]
    upper = lax.axis_index("leaf") & 1 == 1
    half[...] = jnp.where(upper, coef[:, width:], coef[:, :width])


def node_last_kernel(inverse, mine, mine_last, theirs, theirs_last, term, *refs):
    nodes = jnp.concatenate([mine[...], theirs[...]], axis=0)
    both = jnp.concatenate([mine_last[...], theirs_last[...]], axis=0)
    last = refs[0] if len(refs) == 1 else refs[1]
    last[...] = dot(inverse[...], dot(nodes, both, 0, 0)) - term[...]


def top_kernel(level, inverse, *refs):
    mine, theirs, (half, passed) = refs[:3], refs[3:5], refs[5:7]
    earlier, (bases, samples, probe_coef, basis, coefs, done) = refs[7:-6], refs[-6:]
    copies = [
        pltpu.make_async_copy(one, bases.at[0, at], done.at[at]) for at, one in enumerate(earlier)
    ]
    for copy in copies:
        copy.start()
    factor = inverse[...]
    mine, theirs = [ref[...] for ref in mine], [ref[...] for ref in theirs]
    basis_of(level, mine[0], theirs[0], factor, basis)
    at = len(earlier)
    copies.append(pltpu.make_async_copy(basis, bases.at[0, at], done.at[at]))
    copies[-1].start()
    upper = lax.axis_index("leaf") & 1 == 1
    theirs.append(jnp.where(upper, passed[...], half[...]))
    theirs.append(jnp.where(upper, half[...], passed[...]))
    coef = level_products(factor, factor.shape[0], mine, theirs)
    width = samples.shape[2]
    coefs[0] = coef[:, :width]
    coefs[1] = coef[:, width:]
    for at, out in enumerate((samples, probe_coef)):
        copies.append(pltpu.make_async_copy(coefs.at[at], out.at[0], done.at[level + at]))
        copies[-1].start()
    for copy in copies:
        copy.wait()


VMEM = pl.BlockSpec(memory_space=pltpu.VMEM)
SMEM = pl.BlockSpec(memory_space=pltpu.SMEM)
ANY = pl.BlockSpec(memory_space=pl.ANY)


def call(kernel, shapes, *operands, slots=None, flops=0, specs=None, out_specs=None, vmem=32, **options):
    outs = [jax.ShapeDtypeStruct(shape, jnp.float32) for shape in shapes]
    specs = [VMEM] * len(operands) if specs is None else specs
    out_specs = [VMEM] * len(outs) if out_specs is None else out_specs
    if slots is not None:
        operands = (slots,) + operands
        specs = [SMEM] + specs
    moved = 4 * (sum(o.size for o in operands) + sum(o.size for o in outs))
    return pl.pallas_call(
        kernel,
        out_shape=outs,
        in_specs=specs,
        out_specs=out_specs,
        compiler_params=pltpu.CompilerParams(vmem_limit_bytes=vmem * 2**20),
        cost_estimate=pl.CostEstimate(flops=flops, bytes_accessed=moved, transcendentals=0),
        **options,
    )(*operands)


def permuted(value, target):
    trees, subtree = lax.axis_size("clusters"), lax.axis_size("leaf")
    pairs = []
    for member in range(subtree):
        for tree in range(trees):
            to_tree, to_member = target(tree, member)
            if 0 <= to_tree < trees:
                pairs.append((member * trees + tree, to_member * trees + to_tree))
    return lax.ppermute(value, BOTH, pairs)


def flat_shift(value, by):
    subtree = lax.axis_size("leaf")
    return permuted(value, lambda tree, member: divmod(tree * subtree + member + by, subtree))


def swapped(value, mask):
    return permuted(value, lambda tree, member: (tree, member ^ mask))


def outward(value, half):
    return permuted(value, lambda tree, member: (tree - 1 if member < half else tree + 1, member))


def outer_swapped(value, half):
    return permuted(
        value, lambda tree, member: (tree - 1 if member < half else tree + 1, member ^ half)
    )


def tree_swapped(value, odd):
    return permuted(value, lambda tree, member: (tree + 1 if tree & 1 == odd else tree - 1, member))


def body(samples, probes, near_blocks, couplings, node_slot):
    rows, width = probes.shape
    columns = couplings.shape[-1]
    subtree = lax.axis_size("leaf")
    levels = subtree.bit_length() - 1
    chunks = rows // 128
    near = near_blocks.reshape(rows, 2, chunks, 128).transpose(0, 2, 1, 3).reshape(-1, 128)
    work = 12 * rows * rows * width
    tall, tall_last = (rows, columns), (rows, width - columns)
    square, square_last = (columns, columns), (columns, width - columns)

    following = flat_shift(probes, -1)
    (handed,) = call(handed_kernel, [tall], near, probes, flops=work)
    handed = flat_shift(handed, 1)
    blocks = call(pick_kernel, [(columns, 2 * columns)] * (levels + 1), couplings, slots=node_slot)
    following, *blocks = lax.optimization_barrier((following, *blocks))
    rest, handed_last = call(
        rest_kernel, [(rows, width), tall_last], near, probes, samples, flops=work
    )
    rest_first, rest_last, handed_last = call(
        following_kernel, [tall, tall_last, tall_last], near, rest, following, handed_last, flops=work,
        specs=[VMEM, VMEM, VMEM, ANY], out_specs=[VMEM, VMEM, ANY], input_output_aliases={3: 2},
    )
    handed_last = flat_shift(handed_last, 1)
    scratch = dict(scratch_shapes=[pltpu.VMEM((scratch_rows(columns), columns), jnp.float32)])
    far, inverse, first, probe_coef = call(
        leaf_kernel, [tall, square, square, (columns, width)], rest_first, handed, probes,
        flops=work, **scratch,
    )
    if subtree != 4:
        leaf_basis, last = call(
            leaf_last_kernel, [tall, square_last], rest_last, handed_last, far, inverse, flops=work
        )

    ancestors = []
    below = None
    for level in range(1, levels + 1):
        copies = 2 ** (level - 1)
        count = subtree // copies
        if count == 4:
            probe_first, probe_last = probe_coef[:, :columns], probe_coef[:, columns:]
            inner = swapped(probe_first, 2 * copies)
            outer = outer_swapped(probe_first, 2 * copies)
            away = outward(probe_last, 2 * copies)
            theirs_probe = swapped(probe_coef, copies)
            if level == 1:
                inner, handed_last = lax.optimization_barrier((inner, handed_last))
                leaf_basis, last = call(
                    leaf_last_kernel, [tall, square_last], rest_last, handed_last, far, inverse,
                    flops=work,
                )
                inner, outer, last = lax.optimization_barrier((inner, outer, last))
            (first,) = call(
                functools.partial(quad_kernel, level), [square], blocks[level - 1], inner, outer, first
            )
            away, first = lax.optimization_barrier((away, first))
            (term_last,) = call(
                functools.partial(term_kernel, level), [square_last], blocks[-1], probe_last, away
            )
            term_last = swapped(term_last, 2 * copies)
            theirs_first = swapped(first, copies)
        else:
            correct = functools.partial(corrected_kernel, level, count == 2)
            if count == 2:
                fields = [tree_swapped(probe_coef, odd) for odd in (1, 0)]
                *fields, ancestors[-1] = lax.optimization_barrier((*fields, ancestors[-1]))
                theirs_half = swapped(half, copies)
            else:
                theirs_probe = swapped(probe_coef, copies)
                even = (lax.axis_index("leaf") >> level - 1) & 1 == 0
                fields = [flat_shift(probe_coef, by) for by in (2 * copies, -2 * copies)]
                fields = [jnp.where(even, *fields), jnp.where(even, *fields[::-1])]
            first, term_last = call(
                correct, [square, square_last], blocks[level - 1], *fields, first
            )
            theirs_first = swapped(first, copies)
        if below is None:
            last = last - term_last
        else:
            if level < levels:
                (last,) = call(node_last_kernel, [square_last], *below, term_last)
            else:
                last, theirs_half = call(
                    node_last_kernel, [square_last, half.shape], *below, term_last, theirs_half,
                    specs=[VMEM] * 6 + [ANY], out_specs=[VMEM, ANY], input_output_aliases={6: 1},
                )
                theirs_passed = swapped(theirs_half, 1)
        theirs_last = swapped(last, copies)
        if level == levels:
            (inverse,) = call(factor_kernel, [square], first, theirs_first, **scratch)
        else:
            inverse, probe_coef, half = call(
                node_kernel, [square, (columns, width), (columns, width // 2)],
                first, theirs_first, probe_coef, theirs_probe, flops=8 * work, **scratch,
            )
            probe_coef, half, last = lax.optimization_barrier((probe_coef, half, last))
            ancestors += call(
                functools.partial(basis_kernel, level), [(2 * columns, columns)],
                inverse, first, theirs_first,
            )
            below = inverse, first, last, theirs_first, theirs_last
            (first,) = call(node_first_kernel, [square], inverse, first, theirs_first)
    transfer_bases, top_samples, top_probes = call(
        functools.partial(top_kernel, levels),
        [(1, levels, 2 * columns, columns), (1, columns, width), (1, columns, width)],
        inverse, first, last, probe_coef, theirs_first, theirs_last, theirs_half, theirs_passed,
        *ancestors, out_specs=[ANY] * 3,
        scratch_shapes=[
            pltpu.VMEM((2 * columns, columns), jnp.float32),
            pltpu.VMEM((2, columns, width), jnp.float32),
            pltpu.SemaphoreType.DMA((levels + 2,)),
        ],
    )
    return (leaf_basis, transfer_bases, top_samples, top_probes)


def solution(mesh):
    in_specs = (
        P(("clusters", "leaf"), None),
        P(("clusters", "leaf"), None),
        P(("clusters", "leaf"), None, None),
        P("clusters", None, None, None, None),
        P("clusters", None),
    )
    out_specs = (
        P(("clusters", "leaf"), None),
        P(("clusters", "leaf"), None, None, None),
        P("clusters", None, None),
        P("clusters", None, None),
    )
    return jax.shard_map(body, mesh=mesh, in_specs=in_specs, out_specs=out_specs, check_vma=False)
```

```python
import functools

import jax
import jax.numpy as jnp
from jax import lax
from jax.experimental import pallas as pl
from jax.experimental.pallas import tpu as pltpu
from jax.sharding import PartitionSpec as P

HIGHEST = lax.Precision.HIGHEST
ROWS = 8
GROUP = 4
BOTH = ("leaf", "clusters")


def dot(a, b, ca=1, cb=0):
    return lax.dot_general(
        a, b, (((ca,), (cb,)), ((), ())), precision=HIGHEST, preferred_element_type=jnp.float32
    )


def across_lanes(tile, lane):
    return jnp.broadcast_to(tile[:, lane : lane + 1], tile.shape)


def row_of(ref, row):
    return jnp.broadcast_to(ref[pl.ds(row, 1), :], (ROWS, ref.shape[1]))


def inverse_factor(gram, scratch):
    size = gram.shape[0]
    blocks = size // ROWS
    sub = lax.broadcasted_iota(jnp.int32, (ROWS, size), 0)
    lane = lax.broadcasted_iota(jnp.int32, (ROWS, size), 1)
    rows = [gram[ROWS * i : ROWS * (i + 1), :] for i in range(blocks)]
    scaled = [None] * blocks
    used = 0

    def pair_of(k, j):
        return (lane == ROWS * k + j) | (lane == ROWS * k + j + 1)

    def columns_of(tile, k):
        return [across_lanes(tile, ROWS * k + n) for n in range(ROWS)]

    def factors(u, v, step):
        a, b, c, inverse = step[:4]
        return (u * c - v * b) * inverse, (v * a - u * b) * inverse

    def diagonal(k):
        nonlocal used
        tile = rows[k]
        held = scratch.at[pl.ds(used, ROWS * ROWS), :]
        used += ROWS * ROWS
        for n, col in enumerate(columns_of(tile, k)):
            held[pl.ds(ROWS * n, ROWS), :] = col
        block = {(n, m): row_of(held, ROWS * m + n) for n in range(ROWS) for m in range(n + 1)}
        steps = []
        pivots = jnp.ones((ROWS, size), jnp.float32)
        for j in range(0, ROWS, 2):
            tile = jnp.where(pair_of(k, j), jnp.where(lane == sub + ROWS * k, 1.0, 0.0), tile)
            held = scratch.at[pl.ds(used, ROWS), :]
            used += ROWS
            held[...] = tile
            row, next_row = row_of(held, j), row_of(held, j + 1)
            a, b, c = block[j, j], block[j + 1, j], block[j + 1, j + 1]
            det = a * c - b * b
            inverse = pltpu.reciprocal(det, approx=True)
            inverse_a = pltpu.reciprocal(a, approx=True)
            pivots = jnp.where(sub == j, a, jnp.where(sub == j + 1, det * inverse_a, pivots))
            col_rows = [(block[n, j], block[n, j + 1]) for n in range(j + 2, ROWS)]
            step = a, b, c, inverse, row, next_row, col_rows
            steps.append(step)
            f, g = jnp.where(sub == j + 1, b * inverse_a, 0.0), jnp.zeros((ROWS, size), jnp.float32)
            for n in range(j + 2, ROWS):
                f_n, g_n = factors(block[n, j], block[n, j + 1], step)
                f, g = jnp.where(sub == n, f_n, f), jnp.where(sub == n, g_n, g)
                for m in range(j + 2, n + 1):
                    block[n, m] = block[n, m] - (f_n * block[m, j] + g_n * block[m, j + 1])
            tile = tile - (f * row + g * next_row)
        rows[k] = tile
        return steps, pivots

    def below(i, k, steps):
        tile, cols = rows[i], columns_of(rows[i], k)
        for j, step in zip(range(0, ROWS, 2), steps):
            row, next_row, col_rows = step[4:]
            f, g = factors(cols[j], cols[j + 1], step)
            for n, (x, y) in enumerate(col_rows, j + 2):
                cols[n] = cols[n] - (f * x + g * y)
            tile = jnp.where(pair_of(k, j), 0.0, tile) - (f * row + g * next_row)
        rows[i] = tile

    waiting = None
    for first in range(0, blocks, GROUP):
        last = first + GROUP
        ahead = min(last + 1, blocks)
        for k in range(first, last):
            steps, pivots = diagonal(k)
            if waiting is not None:
                done, start, stop = waiting
                change = dot(done.T[ROWS * (stop + 1) :, :], done)
                old = (lane >= ROWS * start) & (lane < ROWS * stop)
                for i in range(stop + 1, blocks):
                    piece = change[ROWS * (i - stop - 1) : ROWS * (i - stop), :]
                    rows[i] = jnp.where(old, 0.0, rows[i]) - piece
                waiting = None
            for i in range(k + 1, ahead):
                below(i, k, steps)
            kept = (lane <= sub + ROWS * k) | (lane >= ROWS * last)
            scaled[k] = jnp.where(kept, rows[k] * lax.rsqrt(pivots), 0.0)
        if ahead < blocks:
            waiting = jnp.concatenate(scaled[first:last], axis=0), first, last
    return jnp.concatenate(
        [jnp.where(lane <= sub + ROWS * k, scaled[k], 0.0) for k in range(blocks)], axis=0
    )


def scratch_rows(size):
    return size * (ROWS + ROWS // 2)


def near_half(view, which, rows, chunks=None):
    chunks = rows // 128 if chunks is None else chunks
    return jnp.concatenate(
        [view[pl.ds(2 * c + which, rows, stride=2 * chunks), :] for c in range(chunks)], axis=1
    )


def handed_kernel(near, probes, handed):
    handed[...] = dot(probes[:, : handed.shape[1]].T, near_half(near, 1, probes.shape[0])).T


def rest_kernel(near, probes, samples, rest, handed_last):
    rows, columns = handed_last.shape
    rest[...] = samples[...] - dot(near_half(near, 0, rows), probes[...])
    handed_last[...] = dot(probes[:, probes.shape[1] - columns :].T, near_half(near, 1, rows)).T


def following_kernel(near, rest, following, _h, first, last, _hout):
    columns = first.shape[1]
    block = rest[...] - dot(near_half(near, 1, rest.shape[0]), following[...])
    first[...] = block[:, :columns]
    last[...] = block[:, columns:]


def leaf_kernel(rest, handed, probes, far, inverse, sample_coef, probe_coef, scratch):
    columns = far.shape[1]
    block = rest[...] - handed[...]
    far[...] = block
    products = dot(block, jnp.concatenate([block, probes[...]], axis=1), 0, 0)
    factor = inverse_factor(products[:, :columns], scratch)
    inverse[...] = factor
    coef = dot(factor, products)
    probe_coef[...] = coef[:, columns:]
    sample_coef[...] = coef[:, :columns]


def leaf_last_kernel(rest, handed, far, inverse, basis, sample_coef):
    basis[...] = dot(far[...], inverse[...], 1, 1)
    sample_coef[...] = dot(basis[...], rest[...] - handed[...], 0, 0)


def member_node(level):
    return lax.axis_index("leaf") >> level - 1


def pick_kernel(slots, couplings, *blocks):
    subtree = lax.axis_size("leaf")
    levels = subtree.bit_length() - 1
    for level, out in zip([*range(1, levels + 1), levels - 1], blocks):
        node = member_node(level)
        if out is blocks[-1]:
            node = node ^ 2
        index = subtree - (subtree >> level - 1) + (node >> 1)
        block = couplings[0, slots[0, index], node & 1]
        out[...] = jnp.concatenate([block, block.T], axis=1)


def quad_kernel(level, block, inner, outer, coef, out):
    node = member_node(level)
    inside = (node == 1) | (node == 2)
    main = jnp.where(inside, inner[...], outer[...])
    other = jnp.where(inside, outer[...], inner[...])
    out[...] = coef[...] - dot(block[...], jnp.concatenate([main, other], axis=0))


def term_kernel(level, block, mine, away, out):
    node = member_node(level)
    outer = (node == 0) | (node == 3)
    main = jnp.where(outer, mine[...], away[...])
    other = jnp.where(outer, away[...], mine[...])
    out[...] = dot(block[...], jnp.concatenate([main, other], axis=0))


def corrected_kernel(level, trees, block, one, two, first, out_first, out_last):
    columns = first.shape[1]
    main, other = one[...], two[...]
    if trees:
        straight = (lax.axis_index("clusters") ^ member_node(level)) & 1 == 0
        main, other = jnp.where(straight, main, other), jnp.where(straight, other, main)
    term = dot(block[...], jnp.concatenate([main, other], axis=0))
    out_first[...] = first[...] - term[:, :columns]
    out_last[...] = term[:, columns:]


def factor_kernel(mine, theirs, inverse, scratch):
    both = jnp.concatenate([mine[...], theirs[...]], axis=0)
    gram = dot(both, both, 0, 0)
    inverse[...] = inverse_factor(gram, scratch)


def basis_of(level, mine, theirs, inverse, out):
    size = mine.shape[0]
    own = (lax.axis_index("leaf") >> level - 1) & 1
    block = dot(jnp.concatenate([mine, theirs], axis=0), inverse, 1, 1)
    out[pl.ds(pl.multiple_of(own * size, size), size), :] = block[:size]
    out[pl.ds(pl.multiple_of((1 - own) * size, size), size), :] = block[size:]


def basis_kernel(level, inverse, mine, theirs, basis):
    basis_of(level, mine[...], theirs[...], inverse[...], basis)


def level_products(inverse, size, own, sibling):
    own, sibling = jnp.concatenate(own, axis=1), jnp.concatenate(sibling, axis=1)
    both = jnp.concatenate([own, sibling], axis=0)
    return dot(inverse, dot(both[:, :size], both, 0, 0))


def node_first_kernel(inverse, mine, theirs, first):
    both = jnp.concatenate([mine[...], theirs[...]], axis=0)
    first[...] = dot(inverse[...], dot(both, both, 0, 0))


def node_kernel(mine, theirs, mine_probes, theirs_probes, inverse, probe_coef, half, scratch):
    nodes = jnp.concatenate([mine[...], theirs[...]], axis=0)
    probes = jnp.concatenate([mine_probes[...], theirs_probes[...]], axis=0)
    cross = dot(nodes, probes, 0, 0)
    factor = inverse_factor(dot(nodes, nodes, 0, 0), scratch)
    inverse[...] = factor
    coef = dot(factor, cross)
    probe_coef[...] = coef
    width = half.shape[1]
    upper = lax.axis_index("leaf") & 1 == 1
    half[...] = jnp.where(upper, coef[:, width:], coef[:, :width])


def node_last_kernel(inverse, mine, mine_last, theirs, theirs_last, term, *refs):
    nodes = jnp.concatenate([mine[...], theirs[...]], axis=0)
    both = jnp.concatenate([mine_last[...], theirs_last[...]], axis=0)
    last = refs[0] if len(refs) == 1 else refs[1]
    last[...] = dot(inverse[...], dot(nodes, both, 0, 0)) - term[...]


def top_kernel(level, inverse, *refs):
    mine, theirs, (half, passed) = refs[:3], refs[3:5], refs[5:7]
    earlier, (bases, samples, probe_coef, basis, coefs, done) = refs[7:-6], refs[-6:]
    copies = [
        pltpu.make_async_copy(one, bases.at[0, at], done.at[at]) for at, one in enumerate(earlier)
    ]
    for copy in copies:
        copy.start()
    factor = inverse[...]
    mine, theirs = [ref[...] for ref in mine], [ref[...] for ref in theirs]
    basis_of(level, mine[0], theirs[0], factor, basis)
    at = len(earlier)
    copies.append(pltpu.make_async_copy(basis, bases.at[0, at], done.at[at]))
    copies[-1].start()
    upper = lax.axis_index("leaf") & 1 == 1
    theirs.append(jnp.where(upper, passed[...], half[...]))
    theirs.append(jnp.where(upper, half[...], passed[...]))
    coef = level_products(factor, factor.shape[0], mine, theirs)
    width = samples.shape[2]
    coefs[0] = coef[:, :width]
    coefs[1] = coef[:, width:]
    for at, out in enumerate((samples, probe_coef)):
        copies.append(pltpu.make_async_copy(coefs.at[at], out.at[0], done.at[level + at]))
        copies[-1].start()
    for copy in copies:
        copy.wait()


VMEM = pl.BlockSpec(memory_space=pltpu.VMEM)
SMEM = pl.BlockSpec(memory_space=pltpu.SMEM)
ANY = pl.BlockSpec(memory_space=pl.ANY)


def call(kernel, shapes, *operands, slots=None, flops=0, specs=None, out_specs=None, vmem=32, **options):
    outs = [jax.ShapeDtypeStruct(shape, jnp.float32) for shape in shapes]
    specs = [VMEM] * len(operands) if specs is None else specs
    out_specs = [VMEM] * len(outs) if out_specs is None else out_specs
    if slots is not None:
        operands = (slots,) + operands
        specs = [SMEM] + specs
    moved = 4 * (sum(o.size for o in operands) + sum(o.size for o in outs))
    return pl.pallas_call(
        kernel,
        out_shape=outs,
        in_specs=specs,
        out_specs=out_specs,
        compiler_params=pltpu.CompilerParams(vmem_limit_bytes=vmem * 2**20),
        cost_estimate=pl.CostEstimate(flops=flops, bytes_accessed=moved, transcendentals=0),
        **options,
    )(*operands)


def permuted(value, target):
    trees, subtree = lax.axis_size("clusters"), lax.axis_size("leaf")
    pairs = []
    for member in range(subtree):
        for tree in range(trees):
            to_tree, to_member = target(tree, member)
            if 0 <= to_tree < trees:
                pairs.append((member * trees + tree, to_member * trees + to_tree))
    return lax.ppermute(value, BOTH, pairs)


def flat_shift(value, by):
    subtree = lax.axis_size("leaf")
    return permuted(value, lambda tree, member: divmod(tree * subtree + member + by, subtree))


def swapped(value, mask):
    return permuted(value, lambda tree, member: (tree, member ^ mask))


def outward(value, half):
    return permuted(value, lambda tree, member: (tree - 1 if member < half else tree + 1, member))


def outer_swapped(value, half):
    return permuted(
        value, lambda tree, member: (tree - 1 if member < half else tree + 1, member ^ half)
    )


def tree_swapped(value, odd):
    return permuted(value, lambda tree, member: (tree + 1 if tree & 1 == odd else tree - 1, member))


def body(samples, probes, near_blocks, couplings, node_slot):
    rows, width = probes.shape
    columns = couplings.shape[-1]
    subtree = lax.axis_size("leaf")
    levels = subtree.bit_length() - 1
    chunks = rows // 128
    near = near_blocks.reshape(rows, 2, chunks, 128).transpose(0, 2, 1, 3).reshape(-1, 128)
    work = 12 * rows * rows * width
    tall, tall_last = (rows, columns), (rows, width - columns)
    square, square_last = (columns, columns), (columns, width - columns)

    following = flat_shift(probes, -1)
    (handed,) = call(handed_kernel, [tall], near, probes, flops=work)
    handed = flat_shift(handed, 1)
    blocks = call(pick_kernel, [(columns, 2 * columns)] * (levels + 1), couplings, slots=node_slot)
    following, *blocks = lax.optimization_barrier((following, *blocks))
    rest, handed_last = call(
        rest_kernel, [(rows, width), tall_last], near, probes, samples, flops=work
    )
    rest_first, rest_last, handed_last = call(
        following_kernel, [tall, tall_last, tall_last], near, rest, following, handed_last, flops=work,
        specs=[VMEM, VMEM, VMEM, ANY], out_specs=[VMEM, VMEM, ANY], input_output_aliases={3: 2},
    )
    handed_last = flat_shift(handed_last, 1)
    scratch = dict(scratch_shapes=[pltpu.VMEM((scratch_rows(columns), columns), jnp.float32)])
    far, inverse, first, probe_coef = call(
        leaf_kernel, [tall, square, square, (columns, width)], rest_first, handed, probes,
        flops=work, **scratch,
    )
    if subtree != 4:
        leaf_basis, last = call(
            leaf_last_kernel, [tall, square_last], rest_last, handed_last, far, inverse, flops=work
        )

    ancestors = []
    below = None
    for level in range(1, levels + 1):
        copies = 2 ** (level - 1)
        count = subtree // copies
        if count == 4:
            probe_first, probe_last = probe_coef[:, :columns], probe_coef[:, columns:]
            inner = swapped(probe_first, 2 * copies)
            outer = outer_swapped(probe_first, 2 * copies)
            away = outward(probe_last, 2 * copies)
            theirs_probe = swapped(probe_coef, copies)
            if level == 1:
                inner, handed_last = lax.optimization_barrier((inner, handed_last))
                leaf_basis, last = call(
                    leaf_last_kernel, [tall, square_last], rest_last, handed_last, far, inverse,
                    flops=work,
                )
                inner, outer, last = lax.optimization_barrier((inner, outer, last))
            (first,) = call(
                functools.partial(quad_kernel, level), [square], blocks[level - 1], inner, outer, first
            )
            away, _ = lax.optimization_barrier((away, first))
            (term_last,) = call(
                functools.partial(term_kernel, level), [square_last], blocks[-1], probe_last, away
            )
            term_last = swapped(term_last, 2 * copies)
            theirs_first = swapped(first, copies)
        else:
            correct = functools.partial(corrected_kernel, level, count == 2)
            if count == 2:
                fields = [tree_swapped(probe_coef, odd) for odd in (1, 0)]
                *fields, ancestors[-1] = lax.optimization_barrier((*fields, ancestors[-1]))
                theirs_half = swapped(half, copies)
            else:
                theirs_probe = swapped(probe_coef, copies)
                even = (lax.axis_index("leaf") >> level - 1) & 1 == 0
                fields = [flat_shift(probe_coef, by) for by in (2 * copies, -2 * copies)]
                fields = [jnp.where(even, *fields), jnp.where(even, *fields[::-1])]
            first, term_last = call(
                correct, [square, square_last], blocks[level - 1], *fields, first
            )
            theirs_first = swapped(first, copies)
        if below is None:
            last = last - term_last
        else:
            if level < levels:
                (last,) = call(node_last_kernel, [square_last], *below, term_last)
            else:
                last, theirs_half = call(
                    node_last_kernel, [square_last, half.shape], *below, term_last, theirs_half,
                    specs=[VMEM] * 6 + [ANY], out_specs=[VMEM, ANY], input_output_aliases={6: 1},
                )
                theirs_passed = swapped(theirs_half, 1)
        leaving = last
        if level == levels:
            theirs_first, leaving = lax.optimization_barrier((theirs_first, last))
        theirs_last = swapped(leaving, copies)
        if level == levels:
            (inverse,) = call(factor_kernel, [square], first, theirs_first, **scratch)
        else:
            inverse, probe_coef, half = call(
                node_kernel, [square, (columns, width), (columns, width // 2)],
                first, theirs_first, probe_coef, theirs_probe, flops=8 * work, **scratch,
            )
            probe_coef, half, last = lax.optimization_barrier((probe_coef, half, last))
            ancestors += call(
                functools.partial(basis_kernel, level), [(2 * columns, columns)],
                inverse, first, theirs_first,
            )
            below = inverse, first, last, theirs_first, theirs_last
            (first,) = call(node_first_kernel, [square], inverse, first, theirs_first)
    transfer_bases, top_samples, top_probes = call(
        functools.partial(top_kernel, levels),
        [(1, levels, 2 * columns, columns), (1, columns, width), (1, columns, width)],
        inverse, first, last, probe_coef, theirs_first, theirs_last, theirs_half, theirs_passed,
        *ancestors, out_specs=[ANY] * 3,
        scratch_shapes=[
            pltpu.VMEM((2 * columns, columns), jnp.float32),
            pltpu.VMEM((2, columns, width), jnp.float32),
            pltpu.SemaphoreType.DMA((levels + 2,)),
        ],
    )
    return (leaf_basis, transfer_bases, top_samples, top_probes)


def solution(mesh):
    in_specs = (
        P(("clusters", "leaf"), None),
        P(("clusters", "leaf"), None),
        P(("clusters", "leaf"), None, None),
        P("clusters", None, None, None, None),
        P("clusters", None),
    )
    out_specs = (
        P(("clusters", "leaf"), None),
        P(("clusters", "leaf"), None, None, None),
        P("clusters", None, None),
        P("clusters", None, None),
    )
    return jax.shard_map(body, mesh=mesh, in_specs=in_specs, out_specs=out_specs, check_vma=False)
```

```python
import functools

import jax
import jax.numpy as jnp
from jax import lax
from jax.experimental import pallas as pl
from jax.experimental.pallas import tpu as pltpu
from jax.sharding import PartitionSpec as P

HIGHEST = lax.Precision.HIGHEST
ROWS = 8
GROUP = 8
BOTH = ("leaf", "clusters")


def dot(a, b, ca=1, cb=0):
    return lax.dot_general(
        a, b, (((ca,), (cb,)), ((), ())), precision=HIGHEST, preferred_element_type=jnp.float32
    )


def across_lanes(tile, lane):
    return jnp.broadcast_to(tile[:, lane : lane + 1], tile.shape)


def row_of(ref, row):
    return jnp.broadcast_to(ref[pl.ds(row, 1), :], (ROWS, ref.shape[1]))


def inverse_factor(gram, scratch):
    size = gram.shape[0]
    blocks = size // ROWS
    sub = lax.broadcasted_iota(jnp.int32, (ROWS, size), 0)
    lane = lax.broadcasted_iota(jnp.int32, (ROWS, size), 1)
    rows = [gram[ROWS * i : ROWS * (i + 1), :] for i in range(blocks)]
    scaled = [None] * blocks
    used = 0

    def panel_lanes(k):
        return (lane >= ROWS * k) & (lane < ROWS * (k + 1))

    def columns_of(tile, k):
        return [across_lanes(tile, ROWS * k + n) for n in range(ROWS)]

    def factors(u, v, step):
        a, b, c, inverse = step[:4]
        return (u * c - v * b) * inverse, (v * a - u * b) * inverse

    def diagonal(k):
        nonlocal used
        tile = rows[k]
        held = scratch.at[pl.ds(used, ROWS * ROWS), :]
        used += ROWS * ROWS
        for n, col in enumerate(columns_of(tile, k)):
            held[pl.ds(ROWS * n, ROWS), :] = col
        block = {(n, m): row_of(held, ROWS * m + n) for n in range(ROWS) for m in range(n + 1)}
        tile = jnp.where(panel_lanes(k), jnp.where(lane == sub + ROWS * k, 1.0, 0.0), tile)
        steps = []
        pivots = jnp.ones((ROWS, size), jnp.float32)
        for j in range(0, ROWS, 2):
            held = scratch.at[pl.ds(used, ROWS), :]
            used += ROWS
            held[...] = tile
            row, next_row = row_of(held, j), row_of(held, j + 1)
            a, b, c = block[j, j], block[j + 1, j], block[j + 1, j + 1]
            det = a * c - b * b
            inverse = pltpu.reciprocal(det, approx=True)
            inverse_a = pltpu.reciprocal(a, approx=True)
            pivots = jnp.where(sub == j, a, jnp.where(sub == j + 1, det * inverse_a, pivots))
            col_rows = [(block[n, j], block[n, j + 1]) for n in range(j + 2, ROWS)]
            step = a, b, c, inverse, row, next_row, col_rows
            steps.append(step)
            f, g = jnp.where(sub == j + 1, b * inverse_a, 0.0), jnp.zeros((ROWS, size), jnp.float32)
            for n in range(j + 2, ROWS):
                f_n, g_n = factors(block[n, j], block[n, j + 1], step)
                f, g = jnp.where(sub == n, f_n, f), jnp.where(sub == n, g_n, g)
                for m in range(j + 2, n + 1):
                    block[n, m] = block[n, m] - (f_n * block[m, j] + g_n * block[m, j + 1])
            tile = tile - (f * row + g * next_row)
        rows[k] = tile
        return steps, pivots

    def below(i, k, steps):
        cols = columns_of(rows[i], k)
        tile = jnp.where(panel_lanes(k), 0.0, rows[i])
        for j, step in zip(range(0, ROWS, 2), steps):
            row, next_row, col_rows = step[4:]
            f, g = factors(cols[j], cols[j + 1], step)
            for n, (x, y) in enumerate(col_rows, j + 2):
                cols[n] = cols[n] - (f * x + g * y)
            tile = tile - (f * row + g * next_row)
        rows[i] = tile

    waiting = None
    for first in range(0, blocks, GROUP):
        last = first + GROUP
        ahead = min(last + 1, blocks)
        for k in range(first, last):
            steps, pivots = diagonal(k)
            if waiting is not None:
                done, start, stop = waiting
                change = dot(done.T[ROWS * (stop + 1) :, :], done)
                old = (lane >= ROWS * start) & (lane < ROWS * stop)
                for i in range(stop + 1, blocks):
                    piece = change[ROWS * (i - stop - 1) : ROWS * (i - stop), :]
                    rows[i] = jnp.where(old, 0.0, rows[i]) - piece
                waiting = None
            for i in range(k + 1, ahead):
                below(i, k, steps)
            kept = (lane <= sub + ROWS * k) | (lane >= ROWS * last)
            scaled[k] = jnp.where(kept, rows[k] * lax.rsqrt(pivots), 0.0)
        if ahead < blocks:
            waiting = jnp.concatenate(scaled[first:last], axis=0), first, last
    return jnp.concatenate(
        [jnp.where(lane <= sub + ROWS * k, scaled[k], 0.0) for k in range(blocks)], axis=0
    )


def scratch_rows(size):
    return size * (ROWS + ROWS // 2)


def near_half(view, which, rows, chunks=None):
    chunks = rows // 128 if chunks is None else chunks
    return jnp.concatenate(
        [view[pl.ds(2 * c + which, rows, stride=2 * chunks), :] for c in range(chunks)], axis=1
    )


def handed_kernel(near, probes, handed):
    handed[...] = dot(probes[:, : handed.shape[1]].T, near_half(near, 1, probes.shape[0])).T


def rest_kernel(near, probes, samples, rest, handed_last):
    rows, columns = handed_last.shape
    rest[...] = samples[...] - dot(near_half(near, 0, rows), probes[...])
    handed_last[...] = dot(probes[:, probes.shape[1] - columns :].T, near_half(near, 1, rows)).T


def following_kernel(near, rest, following, _h, first, last, _hout):
    columns = first.shape[1]
    block = rest[...] - dot(near_half(near, 1, rest.shape[0]), following[...])
    first[...] = block[:, :columns]
    last[...] = block[:, columns:]


def leaf_kernel(rest, handed, probes, far, inverse, sample_coef, probe_coef, scratch):
    columns = far.shape[1]
    block = rest[...] - handed[...]
    far[...] = block
    products = dot(block, jnp.concatenate([block, probes[...]], axis=1), 0, 0)
    factor = inverse_factor(products[:, :columns], scratch)
    inverse[...] = factor
    coef = dot(factor, products)
    probe_coef[...] = coef[:, columns:]
    sample_coef[...] = coef[:, :columns]


def leaf_last_kernel(rest, handed, far, inverse, basis, sample_coef):
    basis[...] = dot(far[...], inverse[...], 1, 1)
    sample_coef[...] = dot(basis[...], rest[...] - handed[...], 0, 0)


def member_node(level):
    return lax.axis_index("leaf") >> level - 1


def pick_kernel(slots, couplings, *blocks):
    subtree = lax.axis_size("leaf")
    levels = subtree.bit_length() - 1
    for level, out in zip([*range(1, levels + 1), levels - 1], blocks):
        node = member_node(level)
        if out is blocks[-1]:
            node = node ^ 2
        index = subtree - (subtree >> level - 1) + (node >> 1)
        block = couplings[0, slots[0, index], node & 1]
        out[...] = jnp.concatenate([block, block.T], axis=1)


def quad_kernel(level, block, inner, outer, coef, out):
    node = member_node(level)
    inside = (node == 1) | (node == 2)
    main = jnp.where(inside, inner[...], outer[...])
    other = jnp.where(inside, outer[...], inner[...])
    out[...] = coef[...] - dot(block[...], jnp.concatenate([main, other], axis=0))


def term_kernel(level, block, mine, away, out):
    node = member_node(level)
    outer = (node == 0) | (node == 3)
    main = jnp.where(outer, mine[...], away[...])
    other = jnp.where(outer, away[...], mine[...])
    out[...] = dot(block[...], jnp.concatenate([main, other], axis=0))


def corrected_kernel(level, trees, block, one, two, first, out_first, out_last):
    columns = first.shape[1]
    main, other = one[...], two[...]
    if trees:
        straight = (lax.axis_index("clusters") ^ member_node(level)) & 1 == 0
        main, other = jnp.where(straight, main, other), jnp.where(straight, other, main)
    term = dot(block[...], jnp.concatenate([main, other], axis=0))
    out_first[...] = first[...] - term[:, :columns]
    out_last[...] = term[:, columns:]


def factor_kernel(mine, theirs, inverse, scratch):
    both = jnp.concatenate([mine[...], theirs[...]], axis=0)
    gram = dot(both, both, 0, 0)
    inverse[...] = inverse_factor(gram, scratch)


def basis_of(level, mine, theirs, inverse, out):
    size = mine.shape[0]
    own = (lax.axis_index("leaf") >> level - 1) & 1
    block = dot(jnp.concatenate([mine, theirs], axis=0), inverse, 1, 1)
    out[pl.ds(pl.multiple_of(own * size, size), size), :] = block[:size]
    out[pl.ds(pl.multiple_of((1 - own) * size, size), size), :] = block[size:]


def basis_kernel(level, inverse, mine, theirs, basis):
    basis_of(level, mine[...], theirs[...], inverse[...], basis)


def level_products(inverse, size, own, sibling):
    own, sibling = jnp.concatenate(own, axis=1), jnp.concatenate(sibling, axis=1)
    both = jnp.concatenate([own, sibling], axis=0)
    return dot(inverse, dot(both[:, :size], both, 0, 0))


def node_first_kernel(inverse, mine, theirs, first):
    both = jnp.concatenate([mine[...], theirs[...]], axis=0)
    first[...] = dot(inverse[...], dot(both, both, 0, 0))


def node_kernel(mine, theirs, mine_probes, theirs_probes, inverse, probe_coef, half, scratch):
    nodes = jnp.concatenate([mine[...], theirs[...]], axis=0)
    probes = jnp.concatenate([mine_probes[...], theirs_probes[...]], axis=0)
    cross = dot(nodes, probes, 0, 0)
    factor = inverse_factor(dot(nodes, nodes, 0, 0), scratch)
    inverse[...] = factor
    coef = dot(factor, cross)
    probe_coef[...] = coef
    width = half.shape[1]
    upper = lax.axis_index("leaf") & 1 == 1
    half[...] = jnp.where(upper, coef[:, width:], coef[:, :width])


def node_last_kernel(inverse, mine, mine_last, theirs, theirs_last, term, *refs):
    nodes = jnp.concatenate([mine[...], theirs[...]], axis=0)
    both = jnp.concatenate([mine_last[...], theirs_last[...]], axis=0)
    last = refs[0] if len(refs) == 1 else refs[1]
    last[...] = dot(inverse[...], dot(nodes, both, 0, 0)) - term[...]


def top_kernel(level, inverse, *refs):
    mine, theirs, (half, passed) = refs[:3], refs[3:5], refs[5:7]
    earlier, (bases, samples, probe_coef, basis, coefs, done) = refs[7:-6], refs[-6:]
    copies = [
        pltpu.make_async_copy(one, bases.at[0, at], done.at[at]) for at, one in enumerate(earlier)
    ]
    for copy in copies:
        copy.start()
    factor = inverse[...]
    mine, theirs = [ref[...] for ref in mine], [ref[...] for ref in theirs]
    basis_of(level, mine[0], theirs[0], factor, basis)
    at = len(earlier)
    copies.append(pltpu.make_async_copy(basis, bases.at[0, at], done.at[at]))
    copies[-1].start()
    upper = lax.axis_index("leaf") & 1 == 1
    theirs.append(jnp.where(upper, passed[...], half[...]))
    theirs.append(jnp.where(upper, half[...], passed[...]))
    coef = level_products(factor, factor.shape[0], mine, theirs)
    width = samples.shape[2]
    coefs[0] = coef[:, :width]
    coefs[1] = coef[:, width:]
    for at, out in enumerate((samples, probe_coef)):
        copies.append(pltpu.make_async_copy(coefs.at[at], out.at[0], done.at[level + at]))
        copies[-1].start()
    for copy in copies:
        copy.wait()


VMEM = pl.BlockSpec(memory_space=pltpu.VMEM)
SMEM = pl.BlockSpec(memory_space=pltpu.SMEM)
ANY = pl.BlockSpec(memory_space=pl.ANY)


def call(kernel, shapes, *operands, slots=None, flops=0, specs=None, out_specs=None, vmem=32, **options):
    outs = [jax.ShapeDtypeStruct(shape, jnp.float32) for shape in shapes]
    specs = [VMEM] * len(operands) if specs is None else specs
    out_specs = [VMEM] * len(outs) if out_specs is None else out_specs
    if slots is not None:
        operands = (slots,) + operands
        specs = [SMEM] + specs
    moved = 4 * (sum(o.size for o in operands) + sum(o.size for o in outs))
    return pl.pallas_call(
        kernel,
        out_shape=outs,
        in_specs=specs,
        out_specs=out_specs,
        compiler_params=pltpu.CompilerParams(vmem_limit_bytes=vmem * 2**20),
        cost_estimate=pl.CostEstimate(flops=flops, bytes_accessed=moved, transcendentals=0),
        **options,
    )(*operands)


def permuted(value, target):
    trees, subtree = lax.axis_size("clusters"), lax.axis_size("leaf")
    pairs = []
    for member in range(subtree):
        for tree in range(trees):
            to_tree, to_member = target(tree, member)
            if 0 <= to_tree < trees:
                pairs.append((member * trees + tree, to_member * trees + to_tree))
    return lax.ppermute(value, BOTH, pairs)


def flat_shift(value, by):
    subtree = lax.axis_size("leaf")
    return permuted(value, lambda tree, member: divmod(tree * subtree + member + by, subtree))


def swapped(value, mask):
    return permuted(value, lambda tree, member: (tree, member ^ mask))


def outward(value, half):
    return permuted(value, lambda tree, member: (tree - 1 if member < half else tree + 1, member))


def outer_swapped(value, half):
    return permuted(
        value, lambda tree, member: (tree - 1 if member < half else tree + 1, member ^ half)
    )


def tree_swapped(value, odd):
    return permuted(value, lambda tree, member: (tree + 1 if tree & 1 == odd else tree - 1, member))


def body(samples, probes, near_blocks, couplings, node_slot):
    rows, width = probes.shape
    columns = couplings.shape[-1]
    subtree = lax.axis_size("leaf")
    levels = subtree.bit_length() - 1
    chunks = rows // 128
    near = near_blocks.reshape(rows, 2, chunks, 128).transpose(0, 2, 1, 3).reshape(-1, 128)
    work = 12 * rows * rows * width
    tall, tall_last = (rows, columns), (rows, width - columns)
    square, square_last = (columns, columns), (columns, width - columns)

    following = flat_shift(probes, -1)
    (handed,) = call(handed_kernel, [tall], near, probes, flops=work)
    handed = flat_shift(handed, 1)
    blocks = call(pick_kernel, [(columns, 2 * columns)] * (levels + 1), couplings, slots=node_slot)
    following, *blocks = lax.optimization_barrier((following, *blocks))
    rest, handed_last = call(
        rest_kernel, [(rows, width), tall_last], near, probes, samples, flops=work
    )
    rest_first, rest_last, handed_last = call(
        following_kernel, [tall, tall_last, tall_last], near, rest, following, handed_last, flops=work,
        specs=[VMEM, VMEM, VMEM, ANY], out_specs=[VMEM, VMEM, ANY], input_output_aliases={3: 2},
    )
    handed_last = flat_shift(handed_last, 1)
    scratch = dict(scratch_shapes=[pltpu.VMEM((scratch_rows(columns), columns), jnp.float32)])
    far, inverse, first, probe_coef = call(
        leaf_kernel, [tall, square, square, (columns, width)], rest_first, handed, probes,
        flops=work, **scratch,
    )
    if subtree != 4:
        leaf_basis, last = call(
            leaf_last_kernel, [tall, square_last], rest_last, handed_last, far, inverse, flops=work
        )

    ancestors = []
    below = None
    for level in range(1, levels + 1):
        copies = 2 ** (level - 1)
        count = subtree // copies
        if count == 4:
            probe_first, probe_last = probe_coef[:, :columns], probe_coef[:, columns:]
            inner = swapped(probe_first, 2 * copies)
            outer = outer_swapped(probe_first, 2 * copies)
            away = outward(probe_last, 2 * copies)
            theirs_probe = swapped(probe_coef, copies)
            if level == 1:
                inner, handed_last = lax.optimization_barrier((inner, handed_last))
                leaf_basis, last = call(
                    leaf_last_kernel, [tall, square_last], rest_last, handed_last, far, inverse,
                    flops=work,
                )
                inner, outer, last = lax.optimization_barrier((inner, outer, last))
            (first,) = call(
                functools.partial(quad_kernel, level), [square], blocks[level - 1], inner, outer, first
            )
            away, _ = lax.optimization_barrier((away, first))
            (term_last,) = call(
                functools.partial(term_kernel, level), [square_last], blocks[-1], probe_last, away
            )
            term_last = swapped(term_last, 2 * copies)
            theirs_first = swapped(first, copies)
        else:
            correct = functools.partial(corrected_kernel, level, count == 2)
            if count == 2:
                fields = [tree_swapped(probe_coef, odd) for odd in (1, 0)]
                *fields, ancestors[-1] = lax.optimization_barrier((*fields, ancestors[-1]))
                theirs_half = swapped(half, copies)
            else:
                theirs_probe = swapped(probe_coef, copies)
                even = (lax.axis_index("leaf") >> level - 1) & 1 == 0
                fields = [flat_shift(probe_coef, by) for by in (2 * copies, -2 * copies)]
                fields = [jnp.where(even, *fields), jnp.where(even, *fields[::-1])]
            first, term_last = call(
                correct, [square, square_last], blocks[level - 1], *fields, first
            )
            theirs_first = swapped(first, copies)
        if below is None:
            last = last - term_last
        else:
            if level < levels:
                (last,) = call(node_last_kernel, [square_last], *below, term_last)
            else:
                last, theirs_half = call(
                    node_last_kernel, [square_last, half.shape], *below, term_last, theirs_half,
                    specs=[VMEM] * 6 + [ANY], out_specs=[VMEM, ANY], input_output_aliases={6: 1},
                )
                theirs_passed = swapped(theirs_half, 1)
        theirs_last = swapped(last, copies)
        if level == levels:
            (inverse,) = call(factor_kernel, [square], first, theirs_first, **scratch)
        else:
            inverse, probe_coef, half = call(
                node_kernel, [square, (columns, width), (columns, width // 2)],
                first, theirs_first, probe_coef, theirs_probe, flops=8 * work, **scratch,
            )
            probe_coef, half, last = lax.optimization_barrier((probe_coef, half, last))
            ancestors += call(
                functools.partial(basis_kernel, level), [(2 * columns, columns)],
                inverse, first, theirs_first,
            )
            below = inverse, first, last, theirs_first, theirs_last
            (first,) = call(node_first_kernel, [square], inverse, first, theirs_first)
    transfer_bases, top_samples, top_probes = call(
        functools.partial(top_kernel, levels),
        [(1, levels, 2 * columns, columns), (1, columns, width), (1, columns, width)],
        inverse, first, last, probe_coef, theirs_first, theirs_last, theirs_half, theirs_passed,
        *ancestors, out_specs=[ANY] * 3,
        scratch_shapes=[
            pltpu.VMEM((2 * columns, columns), jnp.float32),
            pltpu.VMEM((2, columns, width), jnp.float32),
            pltpu.SemaphoreType.DMA((levels + 2,)),
        ],
    )
    return (leaf_basis, transfer_bases, top_samples, top_probes)


def solution(mesh):
    in_specs = (
        P(("clusters", "leaf"), None),
        P(("clusters", "leaf"), None),
        P(("clusters", "leaf"), None, None),
        P("clusters", None, None, None, None),
        P("clusters", None),
    )
    out_specs = (
        P(("clusters", "leaf"), None),
        P(("clusters", "leaf"), None, None, None),
        P("clusters", None, None),
        P("clusters", None, None),
    )
    return jax.shard_map(body, mesh=mesh, in_specs=in_specs, out_specs=out_specs, check_vma=False)
```

```python
import functools

import jax
import jax.numpy as jnp
from jax import lax
from jax.experimental import pallas as pl
from jax.experimental.pallas import tpu as pltpu
from jax.sharding import PartitionSpec as P

HIGHEST = lax.Precision.HIGHEST
ROWS = 8
GROUP = 16
BOTH = ("leaf", "clusters")


def dot(a, b, ca=1, cb=0):
    return lax.dot_general(
        a, b, (((ca,), (cb,)), ((), ())), precision=HIGHEST, preferred_element_type=jnp.float32
    )


def across_lanes(tile, lane):
    return jnp.broadcast_to(tile[:, lane : lane + 1], tile.shape)


def row_of(ref, row):
    return jnp.broadcast_to(ref[pl.ds(row, 1), :], (ROWS, ref.shape[1]))


def inverse_factor(gram, scratch):
    size = gram.shape[0]
    blocks = size // ROWS
    sub = lax.broadcasted_iota(jnp.int32, (ROWS, size), 0)
    lane = lax.broadcasted_iota(jnp.int32, (ROWS, size), 1)
    rows = [gram[ROWS * i : ROWS * (i + 1), :] for i in range(blocks)]
    scaled = [None] * blocks
    used = 0

    def panel_lanes(k):
        return (lane >= ROWS * k) & (lane < ROWS * (k + 1))

    def columns_of(tile, k):
        return [across_lanes(tile, ROWS * k + n) for n in range(ROWS)]

    def factors(u, v, step):
        a, b, c, inverse = step[:4]
        return (u * c - v * b) * inverse, (v * a - u * b) * inverse

    def diagonal(k):
        nonlocal used
        tile = rows[k]
        held = scratch.at[pl.ds(used, ROWS * ROWS), :]
        used += ROWS * ROWS
        for n, col in enumerate(columns_of(tile, k)):
            held[pl.ds(ROWS * n, ROWS), :] = col
        block = {(n, m): row_of(held, ROWS * m + n) for n in range(ROWS) for m in range(n + 1)}
        tile = jnp.where(panel_lanes(k), jnp.where(lane == sub + ROWS * k, 1.0, 0.0), tile)
        steps = []
        pivots = jnp.ones((ROWS, size), jnp.float32)
        for j in range(0, ROWS, 2):
            held = scratch.at[pl.ds(used, ROWS), :]
            used += ROWS
            held[...] = tile
            row, next_row = row_of(held, j), row_of(held, j + 1)
            a, b, c = block[j, j], block[j + 1, j], block[j + 1, j + 1]
            det = a * c - b * b
            inverse = pltpu.reciprocal(det, approx=True)
            inverse_a = pltpu.reciprocal(a, approx=True)
            pivots = jnp.where(sub == j, a, jnp.where(sub == j + 1, det * inverse_a, pivots))
            col_rows = [(block[n, j], block[n, j + 1]) for n in range(j + 2, ROWS)]
            step = a, b, c, inverse, row, next_row, col_rows
            steps.append(step)
            f, g = jnp.where(sub == j + 1, b * inverse_a, 0.0), jnp.zeros((ROWS, size), jnp.float32)
            for n in range(j + 2, ROWS):
                f_n, g_n = factors(block[n, j], block[n, j + 1], step)
                f, g = jnp.where(sub == n, f_n, f), jnp.where(sub == n, g_n, g)
                for m in range(j + 2, n + 1):
                    block[n, m] = block[n, m] - (f_n * block[m, j] + g_n * block[m, j + 1])
            tile = tile - (f * row + g * next_row)
        rows[k] = tile
        return steps, pivots

    def scaled_factors(u, v, step):
        a, b, c, inverse = step[:4]
        a, b, c = a * inverse, b * inverse, c * inverse
        return u * c - v * b, v * a - u * b

    def below(i, k, steps):
        cols = columns_of(rows[i], k)
        tile = jnp.where(panel_lanes(k), 0.0, rows[i])
        for j, step in zip(range(0, ROWS, 2), steps):
            row, next_row, col_rows = step[4:]
            ratios = factors if i == k + 1 else scaled_factors
            f, g = ratios(cols[j], cols[j + 1], step)
            for n, (x, y) in enumerate(col_rows, j + 2):
                cols[n] = cols[n] - (f * x + g * y)
            tile = tile - (f * row + g * next_row)
        rows[i] = tile

    waiting = None
    for first in range(0, blocks, GROUP):
        last = first + GROUP
        ahead = min(last + 1, blocks)
        for k in range(first, last):
            steps, pivots = diagonal(k)
            if waiting is not None:
                done, start, stop = waiting
                change = dot(done.T[ROWS * (stop + 1) :, :], done)
                old = (lane >= ROWS * start) & (lane < ROWS * stop)
                for i in range(stop + 1, blocks):
                    piece = change[ROWS * (i - stop - 1) : ROWS * (i - stop), :]
                    rows[i] = jnp.where(old, 0.0, rows[i]) - piece
                waiting = None
            for i in range(k + 1, ahead):
                below(i, k, steps)
            kept = (lane <= sub + ROWS * k) | (lane >= ROWS * last)
            scaled[k] = jnp.where(kept, rows[k] * lax.rsqrt(pivots), 0.0)
        if ahead < blocks:
            waiting = jnp.concatenate(scaled[first:last], axis=0), first, last
    return jnp.concatenate(
        [jnp.where(lane <= sub + ROWS * k, scaled[k], 0.0) for k in range(blocks)], axis=0
    )


def scratch_rows(size):
    return size * (ROWS + ROWS // 2)


def near_half(view, which, rows, chunks=None):
    chunks = rows // 128 if chunks is None else chunks
    return jnp.concatenate(
        [view[pl.ds(2 * c + which, rows, stride=2 * chunks), :] for c in range(chunks)], axis=1
    )


def handed_kernel(near, probes, handed):
    handed[...] = dot(probes[:, : handed.shape[1]].T, near_half(near, 1, probes.shape[0])).T


def rest_kernel(near, probes, samples, rest, handed_last):
    rows, columns = handed_last.shape
    rest[...] = samples[...] - dot(near_half(near, 0, rows), probes[...])
    handed_last[...] = dot(probes[:, probes.shape[1] - columns :].T, near_half(near, 1, rows)).T


def following_kernel(near, rest, following, _h, first, last, _hout):
    columns = first.shape[1]
    block = rest[...] - dot(near_half(near, 1, rest.shape[0]), following[...])
    first[...] = block[:, :columns]
    last[...] = block[:, columns:]


def leaf_kernel(rest, handed, probes, far, inverse, sample_coef, probe_coef, scratch):
    columns = far.shape[1]
    block = rest[...] - handed[...]
    far[...] = block
    gram = dot(block, block, 0, 0)
    cross = dot(block, probes[...], 0, 0)
    factor = inverse_factor(gram, scratch)
    inverse[...] = factor
    coef = dot(factor, jnp.concatenate([gram, cross], axis=1))
    probe_coef[...] = coef[:, columns:]
    sample_coef[...] = coef[:, :columns]


def leaf_last_kernel(rest, handed, far, inverse, basis, sample_coef):
    basis[...] = dot(far[...], inverse[...], 1, 1)
    sample_coef[...] = dot(basis[...], rest[...] - handed[...], 0, 0)


def member_node(level):
    return lax.axis_index("leaf") >> level - 1


def pick_kernel(slots, couplings, *blocks):
    subtree = lax.axis_size("leaf")
    levels = subtree.bit_length() - 1
    for level, out in zip([*range(1, levels + 1), levels - 1], blocks):
        node = member_node(level)
        if out is blocks[-1]:
            node = node ^ 2
        index = subtree - (subtree >> level - 1) + (node >> 1)
        block = couplings[0, slots[0, index], node & 1]
        out[...] = jnp.concatenate([block, block.T], axis=1)


def quad_kernel(level, block, inner, outer, coef, out):
    node = member_node(level)
    inside = (node == 1) | (node == 2)
    main = jnp.where(inside, inner[...], outer[...])
    other = jnp.where(inside, outer[...], inner[...])
    out[...] = coef[...] - dot(block[...], jnp.concatenate([main, other], axis=0))


def term_kernel(level, block, mine, away, out):
    node = member_node(level)
    outer = (node == 0) | (node == 3)
    main = jnp.where(outer, mine[...], away[...])
    other = jnp.where(outer, away[...], mine[...])
    out[...] = dot(block[...], jnp.concatenate([main, other], axis=0))


def corrected_kernel(level, trees, block, one, two, first, out_first, out_last):
    columns = first.shape[1]
    main, other = one[...], two[...]
    if trees:
        straight = (lax.axis_index("clusters") ^ member_node(level)) & 1 == 0
        main, other = jnp.where(straight, main, other), jnp.where(straight, other, main)
    term = dot(block[...], jnp.concatenate([main, other], axis=0))
    out_first[...] = first[...] - term[:, :columns]
    out_last[...] = term[:, columns:]


def factor_kernel(mine, theirs, inverse, scratch):
    both = jnp.concatenate([mine[...], theirs[...]], axis=0)
    gram = dot(both, both, 0, 0)
    inverse[...] = inverse_factor(gram, scratch)


def basis_of(level, mine, theirs, inverse, out):
    size = mine.shape[0]
    own = (lax.axis_index("leaf") >> level - 1) & 1
    block = dot(jnp.concatenate([mine, theirs], axis=0), inverse, 1, 1)
    out[pl.ds(pl.multiple_of(own * size, size), size), :] = block[:size]
    out[pl.ds(pl.multiple_of((1 - own) * size, size), size), :] = block[size:]


def basis_kernel(level, inverse, mine, theirs, basis):
    basis_of(level, mine[...], theirs[...], inverse[...], basis)


def level_products(inverse, size, own, sibling):
    own, sibling = jnp.concatenate(own, axis=1), jnp.concatenate(sibling, axis=1)
    both = jnp.concatenate([own, sibling], axis=0)
    return dot(inverse, dot(both[:, :size], both, 0, 0))


def node_first_kernel(inverse, mine, theirs, first):
    both = jnp.concatenate([mine[...], theirs[...]], axis=0)
    first[...] = dot(inverse[...], dot(both, both, 0, 0))


def node_kernel(mine, theirs, mine_probes, theirs_probes, inverse, probe_coef, half, scratch):
    nodes = jnp.concatenate([mine[...], theirs[...]], axis=0)
    probes = jnp.concatenate([mine_probes[...], theirs_probes[...]], axis=0)
    cross = dot(nodes, probes, 0, 0)
    factor = inverse_factor(dot(nodes, nodes, 0, 0), scratch)
    inverse[...] = factor
    coef = dot(factor, cross)
    probe_coef[...] = coef
    width = half.shape[1]
    upper = lax.axis_index("leaf") & 1 == 1
    half[...] = jnp.where(upper, coef[:, width:], coef[:, :width])


def node_last_kernel(inverse, mine, mine_last, theirs, theirs_last, term, *refs):
    nodes = jnp.concatenate([mine[...], theirs[...]], axis=0)
    both = jnp.concatenate([mine_last[...], theirs_last[...]], axis=0)
    last = refs[0] if len(refs) == 1 else refs[1]
    last[...] = dot(inverse[...], dot(nodes, both, 0, 0)) - term[...]


def top_kernel(level, inverse, *refs):
    mine, theirs, (half, passed) = refs[:3], refs[3:5], refs[5:7]
    earlier, (bases, samples, probe_coef, basis, coefs, done) = refs[7:-6], refs[-6:]
    copies = [
        pltpu.make_async_copy(one, bases.at[0, at], done.at[at]) for at, one in enumerate(earlier)
    ]
    for copy in copies:
        copy.start()
    factor = inverse[...]
    mine, theirs = [ref[...] for ref in mine], [ref[...] for ref in theirs]
    basis_of(level, mine[0], theirs[0], factor, basis)
    at = len(earlier)
    copies.append(pltpu.make_async_copy(basis, bases.at[0, at], done.at[at]))
    copies[-1].start()
    upper = lax.axis_index("leaf") & 1 == 1
    theirs.append(jnp.where(upper, passed[...], half[...]))
    theirs.append(jnp.where(upper, half[...], passed[...]))
    coef = level_products(factor, factor.shape[0], mine, theirs)
    width = samples.shape[2]
    coefs[0] = coef[:, :width]
    coefs[1] = coef[:, width:]
    for at, out in enumerate((samples, probe_coef)):
        copies.append(pltpu.make_async_copy(coefs.at[at], out.at[0], done.at[level + at]))
        copies[-1].start()
    for copy in copies:
        copy.wait()


VMEM = pl.BlockSpec(memory_space=pltpu.VMEM)
SMEM = pl.BlockSpec(memory_space=pltpu.SMEM)
ANY = pl.BlockSpec(memory_space=pl.ANY)


def call(kernel, shapes, *operands, slots=None, flops=0, specs=None, out_specs=None, vmem=32, **options):
    outs = [jax.ShapeDtypeStruct(shape, jnp.float32) for shape in shapes]
    specs = [VMEM] * len(operands) if specs is None else specs
    out_specs = [VMEM] * len(outs) if out_specs is None else out_specs
    if slots is not None:
        operands = (slots,) + operands
        specs = [SMEM] + specs
    moved = 4 * (sum(o.size for o in operands) + sum(o.size for o in outs))
    return pl.pallas_call(
        kernel,
        out_shape=outs,
        in_specs=specs,
        out_specs=out_specs,
        compiler_params=pltpu.CompilerParams(vmem_limit_bytes=vmem * 2**20),
        cost_estimate=pl.CostEstimate(flops=flops, bytes_accessed=moved, transcendentals=0),
        **options,
    )(*operands)


def permuted(value, target):
    trees, subtree = lax.axis_size("clusters"), lax.axis_size("leaf")
    pairs = []
    for member in range(subtree):
        for tree in range(trees):
            to_tree, to_member = target(tree, member)
            if 0 <= to_tree < trees:
                pairs.append((member * trees + tree, to_member * trees + to_tree))
    return lax.ppermute(value, BOTH, pairs)


def flat_shift(value, by):
    subtree = lax.axis_size("leaf")
    return permuted(value, lambda tree, member: divmod(tree * subtree + member + by, subtree))


def swapped(value, mask):
    return permuted(value, lambda tree, member: (tree, member ^ mask))


def outward(value, half):
    return permuted(value, lambda tree, member: (tree - 1 if member < half else tree + 1, member))


def outer_swapped(value, half):
    return permuted(
        value, lambda tree, member: (tree - 1 if member < half else tree + 1, member ^ half)
    )


def tree_swapped(value, odd):
    return permuted(value, lambda tree, member: (tree + 1 if tree & 1 == odd else tree - 1, member))


def body(samples, probes, near_blocks, couplings, node_slot):
    rows, width = probes.shape
    columns = couplings.shape[-1]
    subtree = lax.axis_size("leaf")
    levels = subtree.bit_length() - 1
    chunks = rows // 128
    near = near_blocks.reshape(rows, 2, chunks, 128).transpose(0, 2, 1, 3).reshape(-1, 128)
    work = 12 * rows * rows * width
    tall, tall_last = (rows, columns), (rows, width - columns)
    square, square_last = (columns, columns), (columns, width - columns)

    following = flat_shift(probes, -1)
    (handed,) = call(handed_kernel, [tall], near, probes, flops=work)
    handed = flat_shift(handed, 1)
    blocks = call(pick_kernel, [(columns, 2 * columns)] * (levels + 1), couplings, slots=node_slot)
    following, *blocks = lax.optimization_barrier((following, *blocks))
    rest, handed_last = call(
        rest_kernel, [(rows, width), tall_last], near, probes, samples, flops=work
    )
    rest_first, rest_last, handed_last = call(
        following_kernel, [tall, tall_last, tall_last], near, rest, following, handed_last, flops=work,
        specs=[VMEM, VMEM, VMEM, ANY], out_specs=[VMEM, VMEM, ANY], input_output_aliases={3: 2},
    )
    handed_last = flat_shift(handed_last, 1)
    scratch = dict(scratch_shapes=[pltpu.VMEM((scratch_rows(columns), columns), jnp.float32)])
    far, inverse, first, probe_coef = call(
        leaf_kernel, [tall, square, square, (columns, width)], rest_first, handed, probes,
        flops=work, **scratch,
    )
    if subtree != 4:
        leaf_basis, last = call(
            leaf_last_kernel, [tall, square_last], rest_last, handed_last, far, inverse, flops=work
        )

    ancestors = []
    below = None
    for level in range(1, levels + 1):
        copies = 2 ** (level - 1)
        count = subtree // copies
        if count == 4:
            probe_first, probe_last = probe_coef[:, :columns], probe_coef[:, columns:]
            inner = swapped(probe_first, 2 * copies)
            outer = outer_swapped(probe_first, 2 * copies)
            away = outward(probe_last, 2 * copies)
            theirs_probe = swapped(probe_coef, copies)
            if level == 1:
                inner, handed_last = lax.optimization_barrier((inner, handed_last))
                leaf_basis, last = call(
                    leaf_last_kernel, [tall, square_last], rest_last, handed_last, far, inverse,
                    flops=work,
                )
                inner, outer, last = lax.optimization_barrier((inner, outer, last))
            (first,) = call(
                functools.partial(quad_kernel, level), [square], blocks[level - 1], inner, outer, first
            )
            away, _ = lax.optimization_barrier((away, first))
            (term_last,) = call(
                functools.partial(term_kernel, level), [square_last], blocks[-1], probe_last, away
            )
            term_last = swapped(term_last, 2 * copies)
            theirs_first = swapped(first, copies)
        else:
            correct = functools.partial(corrected_kernel, level, count == 2)
            if count == 2:
                fields = [tree_swapped(probe_coef, odd) for odd in (1, 0)]
                *fields, ancestors[-1] = lax.optimization_barrier((*fields, ancestors[-1]))
                theirs_half = swapped(half, copies)
            else:
                theirs_probe = swapped(probe_coef, copies)
                even = (lax.axis_index("leaf") >> level - 1) & 1 == 0
                fields = [flat_shift(probe_coef, by) for by in (2 * copies, -2 * copies)]
                fields = [jnp.where(even, *fields), jnp.where(even, *fields[::-1])]
            first, term_last = call(
                correct, [square, square_last], blocks[level - 1], *fields, first
            )
            theirs_first = swapped(first, copies)
        if below is None:
            last = last - term_last
        else:
            if level < levels:
                (last,) = call(node_last_kernel, [square_last], *below, term_last)
            else:
                last, theirs_half = call(
                    node_last_kernel, [square_last, half.shape], *below, term_last, theirs_half,
                    specs=[VMEM] * 6 + [ANY], out_specs=[VMEM, ANY], input_output_aliases={6: 1},
                )
                theirs_passed = swapped(theirs_half, 1)
        theirs_last = swapped(last, copies)
        if level == levels:
            (inverse,) = call(factor_kernel, [square], first, theirs_first, **scratch)
        else:
            inverse, probe_coef, half = call(
                node_kernel, [square, (columns, width), (columns, width // 2)],
                first, theirs_first, probe_coef, theirs_probe, flops=8 * work, **scratch,
            )
            probe_coef, half, last = lax.optimization_barrier((probe_coef, half, last))
            ancestors += call(
                functools.partial(basis_kernel, level), [(2 * columns, columns)],
                inverse, first, theirs_first,
            )
            below = inverse, first, last, theirs_first, theirs_last
            (first,) = call(node_first_kernel, [square], inverse, first, theirs_first)
    transfer_bases, top_samples, top_probes = call(
        functools.partial(top_kernel, levels),
        [(1, levels, 2 * columns, columns), (1, columns, width), (1, columns, width)],
        inverse, first, last, probe_coef, theirs_first, theirs_last, theirs_half, theirs_passed,
        *ancestors, out_specs=[ANY] * 3,
        scratch_shapes=[
            pltpu.VMEM((2 * columns, columns), jnp.float32),
            pltpu.VMEM((2, columns, width), jnp.float32),
            pltpu.SemaphoreType.DMA((levels + 2,)),
        ],
    )
    return (leaf_basis, transfer_bases, top_samples, top_probes)


def solution(mesh):
    in_specs = (
        P(("clusters", "leaf"), None),
        P(("clusters", "leaf"), None),
        P(("clusters", "leaf"), None, None),
        P("clusters", None, None, None, None),
        P("clusters", None),
    )
    out_specs = (
        P(("clusters", "leaf"), None),
        P(("clusters", "leaf"), None, None, None),
        P("clusters", None, None),
        P("clusters", None, None),
    )
    return jax.shard_map(body, mesh=mesh, in_specs=in_specs, out_specs=out_specs, check_vma=False)
```

```python
import functools

import jax
import jax.numpy as jnp
from jax import lax
from jax.experimental import pallas as pl
from jax.experimental.pallas import tpu as pltpu
from jax.sharding import PartitionSpec as P

HIGHEST = lax.Precision.HIGHEST
ROWS = 8
GROUP = 8
BOTH = ("leaf", "clusters")


def dot(a, b, ca=1, cb=0):
    return lax.dot_general(
        a, b, (((ca,), (cb,)), ((), ())), precision=HIGHEST, preferred_element_type=jnp.float32
    )


def across_lanes(tile, lane):
    return jnp.broadcast_to(tile[:, lane : lane + 1], tile.shape)


def row_of(ref, row):
    return jnp.broadcast_to(ref[pl.ds(row, 1), :], (ROWS, ref.shape[1]))


def inverse_factor(gram, scratch):
    size = gram.shape[0]
    blocks = size // ROWS
    sub = lax.broadcasted_iota(jnp.int32, (ROWS, size), 0)
    lane = lax.broadcasted_iota(jnp.int32, (ROWS, size), 1)
    rows = [gram[ROWS * i : ROWS * (i + 1), :] for i in range(blocks)]
    scaled = [None] * blocks
    used = 0

    def panel_lanes(k):
        return (lane >= ROWS * k) & (lane < ROWS * (k + 1))

    def columns_of(tile, k):
        return [across_lanes(tile, ROWS * k + n) for n in range(ROWS)]

    def factors(u, v, step):
        a, b, c, inverse = step[:4]
        return (u * c - v * b) * inverse, (v * a - u * b) * inverse

    def diagonal(k):
        nonlocal used
        tile = rows[k]
        held = scratch.at[pl.ds(used, ROWS * ROWS), :]
        used += ROWS * ROWS
        for n, col in enumerate(columns_of(tile, k)):
            held[pl.ds(ROWS * n, ROWS), :] = col
        block = {(n, m): row_of(held, ROWS * m + n) for n in range(ROWS) for m in range(n + 1)}
        tile = jnp.where(panel_lanes(k), jnp.where(lane == sub + ROWS * k, 1.0, 0.0), tile)
        steps = []
        pivots = jnp.ones((ROWS, size), jnp.float32)
        for j in range(0, ROWS, 2):
            held = scratch.at[pl.ds(used, ROWS), :]
            used += ROWS
            held[...] = tile
            row, next_row = row_of(held, j), row_of(held, j + 1)
            a, b, c = block[j, j], block[j + 1, j], block[j + 1, j + 1]
            det = a * c - b * b
            inverse = pltpu.reciprocal(det, approx=True)
            inverse_a = pltpu.reciprocal(a, approx=True)
            pivots = jnp.where(sub == j, a, jnp.where(sub == j + 1, det * inverse_a, pivots))
            col_rows = [(block[n, j], block[n, j + 1]) for n in range(j + 2, ROWS)]
            step = a, b, c, inverse, row, next_row, col_rows
            steps.append(step)
            f, g = jnp.where(sub == j + 1, b * inverse_a, 0.0), jnp.zeros((ROWS, size), jnp.float32)
            for n in range(j + 2, ROWS):
                f_n, g_n = factors(block[n, j], block[n, j + 1], step)
                f, g = jnp.where(sub == n, f_n, f), jnp.where(sub == n, g_n, g)
                for m in range(j + 2, n + 1):
                    block[n, m] = block[n, m] - (f_n * block[m, j] + g_n * block[m, j + 1])
            tile = tile - (f * row + g * next_row)
        rows[k] = tile
        return steps, pivots

    def below(i, k, steps):
        cols = columns_of(rows[i], k)
        tile = jnp.where(panel_lanes(k), 0.0, rows[i])
        for j, step in zip(range(0, ROWS, 2), steps):
            row, next_row, col_rows = step[4:]
            f, g = factors(cols[j], cols[j + 1], step)
            for n, (x, y) in enumerate(col_rows, j + 2):
                cols[n] = cols[n] - (f * x + g * y)
            tile = tile - (f * row + g * next_row)
        rows[i] = tile

    waiting = None
    for first in range(0, blocks, GROUP):
        last = first + GROUP
        ahead = min(last + 1, blocks)
        for k in range(first, last):
            steps, pivots = diagonal(k)
            if waiting is not None:
                done, start, stop = waiting
                change = dot(done.T[ROWS * (stop + 1) :, :], done)
                old = (lane >= ROWS * start) & (lane < ROWS * stop)
                for i in range(stop + 1, blocks):
                    piece = change[ROWS * (i - stop - 1) : ROWS * (i - stop), :]
                    rows[i] = jnp.where(old, 0.0, rows[i]) - piece
                waiting = None
            for i in range(k + 1, ahead):
                below(i, k, steps)
            kept = (lane <= sub + ROWS * k) | (lane >= ROWS * last)
            scaled[k] = jnp.where(kept, rows[k] * lax.rsqrt(pivots), 0.0)
        if ahead < blocks:
            waiting = jnp.concatenate(scaled[first:last], axis=0), first, last
    return jnp.concatenate(
        [jnp.where(lane <= sub + ROWS * k, scaled[k], 0.0) for k in range(blocks)], axis=0
    )


def scratch_rows(size):
    return size * (ROWS + ROWS // 2)


def near_half(view, which, rows, chunks=None):
    chunks = rows // 128 if chunks is None else chunks
    return jnp.concatenate(
        [view[pl.ds(2 * c + which, rows, stride=2 * chunks), :] for c in range(chunks)], axis=1
    )


def handed_kernel(near, probes, handed):
    handed[...] = dot(probes[:, : handed.shape[1]].T, near_half(near, 1, probes.shape[0])).T


def rest_kernel(near, probes, samples, rest, handed_last):
    rows, columns = handed_last.shape
    rest[...] = samples[...] - dot(near_half(near, 0, rows), probes[...])
    handed_last[...] = dot(probes[:, probes.shape[1] - columns :].T, near_half(near, 1, rows)).T


def following_kernel(near, rest, following, _h, first, last, _hout):
    columns = first.shape[1]
    block = rest[...] - dot(near_half(near, 1, rest.shape[0]), following[...])
    first[...] = block[:, :columns]
    last[...] = block[:, columns:]


def leaf_kernel(rest, handed, probes, far, inverse, sample_coef, probe_coef, scratch):
    columns = far.shape[1]
    block = rest[...] - handed[...]
    far[...] = block
    gram = dot(block, block, 0, 0)
    cross = dot(block, probes[...], 0, 0)
    factor = inverse_factor(gram, scratch)
    inverse[...] = factor
    coef = dot(factor, jnp.concatenate([gram, cross], axis=1))
    probe_coef[...] = coef[:, columns:]
    sample_coef[...] = coef[:, :columns]


def leaf_last_kernel(rest, handed, far, inverse, basis, sample_coef):
    basis[...] = dot(far[...], inverse[...], 1, 1)
    sample_coef[...] = dot(basis[...], rest[...] - handed[...], 0, 0)


def member_node(level):
    return lax.axis_index("leaf") >> level - 1


def pick_kernel(slots, couplings, *blocks):
    subtree = lax.axis_size("leaf")
    levels = subtree.bit_length() - 1
    for level, out in zip([*range(1, levels + 1), levels - 1], blocks):
        node = member_node(level)
        if out is blocks[-1]:
            node = node ^ 2
        index = subtree - (subtree >> level - 1) + (node >> 1)
        block = couplings[0, slots[0, index], node & 1]
        out[...] = jnp.concatenate([block, block.T], axis=1)


def quad_kernel(level, block, outer, inner, coef, out):
    node = member_node(level)
    inside = (node == 1) | (node == 2)
    main = jnp.where(inside, inner[...], outer[...])
    other = jnp.where(inside, outer[...], inner[...])
    out[...] = coef[...] - dot(block[...], jnp.concatenate([main, other], axis=0))


def term_kernel(level, block, mine, away, out):
    node = member_node(level)
    outer = (node == 0) | (node == 3)
    main = jnp.where(outer, mine[...], away[...])
    other = jnp.where(outer, away[...], mine[...])
    out[...] = dot(block[...], jnp.concatenate([main, other], axis=0))


def corrected_kernel(level, trees, block, one, two, first, out_first, out_last):
    columns = first.shape[1]
    main, other = one[...], two[...]
    if trees:
        straight = (lax.axis_index("clusters") ^ member_node(level)) & 1 == 0
        main, other = jnp.where(straight, main, other), jnp.where(straight, other, main)
    term = dot(block[...], jnp.concatenate([main, other], axis=0))
    out_first[...] = first[...] - term[:, :columns]
    out_last[...] = term[:, columns:]


def factor_kernel(mine, theirs, inverse, scratch):
    both = jnp.concatenate([mine[...], theirs[...]], axis=0)
    gram = dot(both, both, 0, 0)
    inverse[...] = inverse_factor(gram, scratch)


def basis_of(level, mine, theirs, inverse, out):
    size = mine.shape[0]
    own = (lax.axis_index("leaf") >> level - 1) & 1
    block = dot(jnp.concatenate([mine, theirs], axis=0), inverse, 1, 1)
    out[pl.ds(pl.multiple_of(own * size, size), size), :] = block[:size]
    out[pl.ds(pl.multiple_of((1 - own) * size, size), size), :] = block[size:]


def basis_kernel(level, inverse, mine, theirs, basis):
    basis_of(level, mine[...], theirs[...], inverse[...], basis)


def level_products(inverse, size, own, sibling):
    own, sibling = jnp.concatenate(own, axis=1), jnp.concatenate(sibling, axis=1)
    both = jnp.concatenate([own, sibling], axis=0)
    return dot(inverse, dot(both[:, :size], both, 0, 0))


def node_first_kernel(inverse, mine, theirs, first):
    both = jnp.concatenate([mine[...], theirs[...]], axis=0)
    first[...] = dot(inverse[...], dot(both, both, 0, 0))


def node_kernel(mine, theirs, mine_probes, theirs_probes, inverse, probe_coef, half, scratch):
    nodes = jnp.concatenate([mine[...], theirs[...]], axis=0)
    probes = jnp.concatenate([mine_probes[...], theirs_probes[...]], axis=0)
    cross = dot(nodes, probes, 0, 0)
    factor = inverse_factor(dot(nodes, nodes, 0, 0), scratch)
    inverse[...] = factor
    coef = dot(factor, cross)
    probe_coef[...] = coef
    width = half.shape[1]
    upper = lax.axis_index("leaf") & 1 == 1
    half[...] = jnp.where(upper, coef[:, width:], coef[:, :width])


def node_last_kernel(inverse, mine, mine_last, theirs, theirs_last, term, *refs):
    nodes = jnp.concatenate([mine[...], theirs[...]], axis=0)
    both = jnp.concatenate([mine_last[...], theirs_last[...]], axis=0)
    last = refs[0] if len(refs) == 1 else refs[1]
    last[...] = dot(inverse[...], dot(nodes, both, 0, 0)) - term[...]


def top_kernel(level, inverse, *refs):
    mine, theirs, (half, passed) = refs[:3], refs[3:5], refs[5:7]
    earlier, (bases, samples, probe_coef, basis, coefs, done) = refs[7:-6], refs[-6:]
    copies = [
        pltpu.make_async_copy(one, bases.at[0, at], done.at[at]) for at, one in enumerate(earlier)
    ]
    for copy in copies:
        copy.start()
    factor = inverse[...]
    mine, theirs = [ref[...] for ref in mine], [ref[...] for ref in theirs]
    basis_of(level, mine[0], theirs[0], factor, basis)
    at = len(earlier)
    copies.append(pltpu.make_async_copy(basis, bases.at[0, at], done.at[at]))
    copies[-1].start()
    upper = lax.axis_index("leaf") & 1 == 1
    theirs.append(jnp.where(upper, passed[...], half[...]))
    theirs.append(jnp.where(upper, half[...], passed[...]))
    coef = level_products(factor, factor.shape[0], mine, theirs)
    width = samples.shape[2]
    coefs[0] = coef[:, :width]
    coefs[1] = coef[:, width:]
    for at, out in enumerate((samples, probe_coef)):
        copies.append(pltpu.make_async_copy(coefs.at[at], out.at[0], done.at[level + at]))
        copies[-1].start()
    for copy in copies:
        copy.wait()


VMEM = pl.BlockSpec(memory_space=pltpu.VMEM)
SMEM = pl.BlockSpec(memory_space=pltpu.SMEM)
ANY = pl.BlockSpec(memory_space=pl.ANY)


def call(kernel, shapes, *operands, slots=None, flops=0, specs=None, out_specs=None, vmem=32, **options):
    outs = [jax.ShapeDtypeStruct(shape, jnp.float32) for shape in shapes]
    specs = [VMEM] * len(operands) if specs is None else specs
    out_specs = [VMEM] * len(outs) if out_specs is None else out_specs
    if slots is not None:
        operands = (slots,) + operands
        specs = [SMEM] + specs
    moved = 4 * (sum(o.size for o in operands) + sum(o.size for o in outs))
    return pl.pallas_call(
        kernel,
        out_shape=outs,
        in_specs=specs,
        out_specs=out_specs,
        compiler_params=pltpu.CompilerParams(vmem_limit_bytes=vmem * 2**20),
        cost_estimate=pl.CostEstimate(flops=flops, bytes_accessed=moved, transcendentals=0),
        **options,
    )(*operands)


def permuted(value, target):
    trees, subtree = lax.axis_size("clusters"), lax.axis_size("leaf")
    pairs = []
    for member in range(subtree):
        for tree in range(trees):
            to_tree, to_member = target(tree, member)
            if 0 <= to_tree < trees:
                pairs.append((member * trees + tree, to_member * trees + to_tree))
    return lax.ppermute(value, BOTH, pairs)


def flat_shift(value, by):
    subtree = lax.axis_size("leaf")
    return permuted(value, lambda tree, member: divmod(tree * subtree + member + by, subtree))


def swapped(value, mask):
    return permuted(value, lambda tree, member: (tree, member ^ mask))


def outward(value, half):
    return permuted(value, lambda tree, member: (tree - 1 if member < half else tree + 1, member))


def outer_swapped(value, half):
    return permuted(
        value, lambda tree, member: (tree - 1 if member < half else tree + 1, member ^ half)
    )


def tree_swapped(value, odd):
    return permuted(value, lambda tree, member: (tree + 1 if tree & 1 == odd else tree - 1, member))


def body(samples, probes, near_blocks, couplings, node_slot):
    rows, width = probes.shape
    columns = couplings.shape[-1]
    subtree = lax.axis_size("leaf")
    levels = subtree.bit_length() - 1
    chunks = rows // 128
    near = near_blocks.reshape(rows, 2, chunks, 128).transpose(0, 2, 1, 3).reshape(-1, 128)
    work = 12 * rows * rows * width
    tall, tall_last = (rows, columns), (rows, width - columns)
    square, square_last = (columns, columns), (columns, width - columns)

    following = flat_shift(probes, -1)
    (handed,) = call(handed_kernel, [tall], near, probes, flops=work)
    handed = flat_shift(handed, 1)
    blocks = call(pick_kernel, [(columns, 2 * columns)] * (levels + 1), couplings, slots=node_slot)
    following, *blocks = lax.optimization_barrier((following, *blocks))
    rest, handed_last = call(
        rest_kernel, [(rows, width), tall_last], near, probes, samples, flops=work
    )
    rest_first, rest_last, handed_last = call(
        following_kernel, [tall, tall_last, tall_last], near, rest, following, handed_last, flops=work,
        specs=[VMEM, VMEM, VMEM, ANY], out_specs=[VMEM, VMEM, ANY], input_output_aliases={3: 2},
    )
    handed_last = flat_shift(handed_last, 1)
    scratch = dict(scratch_shapes=[pltpu.VMEM((scratch_rows(columns), columns), jnp.float32)])
    far, inverse, first, probe_coef = call(
        leaf_kernel, [tall, square, square, (columns, width)], rest_first, handed, probes,
        flops=work, **scratch,
    )
    if subtree != 4:
        leaf_basis, last = call(
            leaf_last_kernel, [tall, square_last], rest_last, handed_last, far, inverse, flops=work
        )

    ancestors = []
    below = None
    for level in range(1, levels + 1):
        copies = 2 ** (level - 1)
        count = subtree // copies
        if count == 4:
            probe_first, probe_last = probe_coef[:, :columns], probe_coef[:, columns:]
            outer = outer_swapped(probe_first, 2 * copies)
            inner = swapped(probe_first, 2 * copies)
            away = outward(probe_last, 2 * copies)
            theirs_probe = swapped(probe_coef, copies)
            if level == 1:
                outer, handed_last = lax.optimization_barrier((outer, handed_last))
                leaf_basis, last = call(
                    leaf_last_kernel, [tall, square_last], rest_last, handed_last, far, inverse,
                    flops=work,
                )
                outer, inner, last = lax.optimization_barrier((outer, inner, last))
            (first,) = call(
                functools.partial(quad_kernel, level), [square], blocks[level - 1], outer, inner, first
            )
            away, _ = lax.optimization_barrier((away, first))
            (term_last,) = call(
                functools.partial(term_kernel, level), [square_last], blocks[-1], probe_last, away
            )
            term_last = swapped(term_last, 2 * copies)
            theirs_first = swapped(first, copies)
        else:
            correct = functools.partial(corrected_kernel, level, count == 2)
            if count == 2:
                fields = [tree_swapped(probe_coef, odd) for odd in (1, 0)]
                *fields, ancestors[-1] = lax.optimization_barrier((*fields, ancestors[-1]))
                theirs_half = swapped(half, copies)
            else:
                theirs_probe = swapped(probe_coef, copies)
                even = (lax.axis_index("leaf") >> level - 1) & 1 == 0
                fields = [flat_shift(probe_coef, by) for by in (2 * copies, -2 * copies)]
                fields = [jnp.where(even, *fields), jnp.where(even, *fields[::-1])]
            first, term_last = call(
                correct, [square, square_last], blocks[level - 1], *fields, first
            )
            theirs_first = swapped(first, copies)
        if below is None:
            last = last - term_last
        else:
            if level < levels:
                (last,) = call(node_last_kernel, [square_last], *below, term_last)
            else:
                last, theirs_half = call(
                    node_last_kernel, [square_last, half.shape], *below, term_last, theirs_half,
                    specs=[VMEM] * 6 + [ANY], out_specs=[VMEM, ANY], input_output_aliases={6: 1},
                )
                theirs_passed = swapped(theirs_half, 1)
        theirs_last = swapped(last, copies)
        if level == levels:
            (inverse,) = call(factor_kernel, [square], first, theirs_first, **scratch)
        else:
            inverse, probe_coef, half = call(
                node_kernel, [square, (columns, width), (columns, width // 2)],
                first, theirs_first, probe_coef, theirs_probe, flops=8 * work, **scratch,
            )
            probe_coef, half, last = lax.optimization_barrier((probe_coef, half, last))
            ancestors += call(
                functools.partial(basis_kernel, level), [(2 * columns, columns)],
                inverse, first, theirs_first,
            )
            below = inverse, first, last, theirs_first, theirs_last
            (first,) = call(node_first_kernel, [square], inverse, first, theirs_first)
    transfer_bases, top_samples, top_probes = call(
        functools.partial(top_kernel, levels),
        [(1, levels, 2 * columns, columns), (1, columns, width), (1, columns, width)],
        inverse, first, last, probe_coef, theirs_first, theirs_last, theirs_half, theirs_passed,
        *ancestors, out_specs=[ANY] * 3,
        scratch_shapes=[
            pltpu.VMEM((2 * columns, columns), jnp.float32),
            pltpu.VMEM((2, columns, width), jnp.float32),
            pltpu.SemaphoreType.DMA((levels + 2,)),
        ],
    )
    return (leaf_basis, transfer_bases, top_samples, top_probes)


def solution(mesh):
    in_specs = (
        P(("clusters", "leaf"), None),
        P(("clusters", "leaf"), None),
        P(("clusters", "leaf"), None, None),
        P("clusters", None, None, None, None),
        P("clusters", None),
    )
    out_specs = (
        P(("clusters", "leaf"), None),
        P(("clusters", "leaf"), None, None, None),
        P("clusters", None, None),
        P("clusters", None, None),
    )
    return jax.shard_map(body, mesh=mesh, in_specs=in_specs, out_specs=out_specs, check_vma=False)
```

```python
import functools

import jax
import jax.numpy as jnp
from jax import lax
from jax.experimental import pallas as pl
from jax.experimental.pallas import tpu as pltpu
from jax.sharding import PartitionSpec as P

HIGHEST = lax.Precision.HIGHEST
ROWS = 8
GROUP = 8
BOTH = ("leaf", "clusters")


def dot(a, b, ca=1, cb=0):
    return lax.dot_general(
        a, b, (((ca,), (cb,)), ((), ())), precision=HIGHEST, preferred_element_type=jnp.float32
    )


def across_lanes(tile, lane):
    return jnp.broadcast_to(tile[:, lane : lane + 1], tile.shape)


def row_of(ref, row):
    return jnp.broadcast_to(ref[pl.ds(row, 1), :], (ROWS, ref.shape[1]))


def inverse_factor(gram, scratch):
    size = gram.shape[0]
    blocks = size // ROWS
    sub = lax.broadcasted_iota(jnp.int32, (ROWS, size), 0)
    lane = lax.broadcasted_iota(jnp.int32, (ROWS, size), 1)
    rows = [gram[ROWS * i : ROWS * (i + 1), :] for i in range(blocks)]
    diagonals = [jnp.where(lane == sub + ROWS * i, rows[i], 0.0) for i in range(blocks)]
    norms = lax.rsqrt(jnp.sum(functools.reduce(jnp.add, diagonals), axis=0, keepdims=True))
    norms = jnp.broadcast_to(norms, (ROWS, size))
    for i in range(blocks):
        own = jnp.sum(jnp.where(lane == sub + ROWS * i, norms, 0.0), axis=1, keepdims=True)
        rows[i] = rows[i] * norms * own
    scaled = [None] * blocks
    used = 0

    def panel_lanes(k):
        return (lane >= ROWS * k) & (lane < ROWS * (k + 1))

    def columns_of(tile, k):
        return [across_lanes(tile, ROWS * k + n) for n in range(ROWS)]

    def factors(u, v, step):
        a, b, c, inverse = step[:4]
        return (u * c - v * b) * inverse, (v * a - u * b) * inverse

    def diagonal(k):
        nonlocal used
        tile = rows[k]
        held = scratch.at[pl.ds(used, ROWS * ROWS), :]
        used += ROWS * ROWS
        for n, col in enumerate(columns_of(tile, k)):
            held[pl.ds(ROWS * n, ROWS), :] = col
        block = {(n, m): row_of(held, ROWS * m + n) for n in range(ROWS) for m in range(n + 1)}
        tile = jnp.where(panel_lanes(k), jnp.where(lane == sub + ROWS * k, 1.0, 0.0), tile)
        steps = []
        pivots = jnp.ones((ROWS, size), jnp.float32)
        for j in range(0, ROWS, 2):
            held = scratch.at[pl.ds(used, ROWS), :]
            used += ROWS
            held[...] = tile
            row, next_row = row_of(held, j), row_of(held, j + 1)
            a, b, c = block[j, j], block[j + 1, j], block[j + 1, j + 1]
            det = a * c - b * b
            inverse = pltpu.reciprocal(det, approx=True)
            inverse_a = pltpu.reciprocal(a, approx=True)
            pivots = jnp.where(sub == j, a, jnp.where(sub == j + 1, det * inverse_a, pivots))
            col_rows = [(block[n, j], block[n, j + 1]) for n in range(j + 2, ROWS)]
            step = a, b, c, inverse, row, next_row, col_rows
            steps.append(step)
            f, g = jnp.where(sub == j + 1, b * inverse_a, 0.0), jnp.zeros((ROWS, size), jnp.float32)
            for n in range(j + 2, ROWS):
                f_n, g_n = factors(block[n, j], block[n, j + 1], step)
                f, g = jnp.where(sub == n, f_n, f), jnp.where(sub == n, g_n, g)
                for m in range(j + 2, n + 1):
                    block[n, m] = block[n, m] - (f_n * block[m, j] + g_n * block[m, j + 1])
            tile = tile - (f * row + g * next_row)
        rows[k] = tile
        return steps, pivots

    def below(i, k, steps):
        cols = columns_of(rows[i], k)
        tile = jnp.where(panel_lanes(k), 0.0, rows[i])
        for j, step in zip(range(0, ROWS, 2), steps):
            row, next_row, col_rows = step[4:]
            f, g = factors(cols[j], cols[j + 1], step)
            for n, (x, y) in enumerate(col_rows, j + 2):
                cols[n] = cols[n] - (f * x + g * y)
            tile = tile - (f * row + g * next_row)
        rows[i] = tile

    waiting = None
    for first in range(0, blocks, GROUP):
        last = first + GROUP
        ahead = min(last + 1, blocks)
        for k in range(first, last):
            steps, pivots = diagonal(k)
            if waiting is not None:
                done, start, stop = waiting
                change = dot(done.T[ROWS * (stop + 1) :, :], done)
                old = (lane >= ROWS * start) & (lane < ROWS * stop)
                for i in range(stop + 1, blocks):
                    piece = change[ROWS * (i - stop - 1) : ROWS * (i - stop), :]
                    rows[i] = jnp.where(old, 0.0, rows[i]) - piece
                waiting = None
            for i in range(k + 1, ahead):
                below(i, k, steps)
            kept = (lane <= sub + ROWS * k) | (lane >= ROWS * last)
            scaled[k] = jnp.where(kept, rows[k] * lax.rsqrt(pivots), 0.0)
        if ahead < blocks:
            waiting = jnp.concatenate(scaled[first:last], axis=0), first, last
    return jnp.concatenate(
        [jnp.where(lane <= sub + ROWS * k, scaled[k] * norms, 0.0) for k in range(blocks)], axis=0
    )


def scratch_rows(size):
    return size * (ROWS + ROWS // 2)


def near_half(view, which, rows, chunks=None):
    chunks = rows // 128 if chunks is None else chunks
    return jnp.concatenate(
        [view[pl.ds(2 * c + which, rows, stride=2 * chunks), :] for c in range(chunks)], axis=1
    )


def handed_kernel(near, probes, handed):
    handed[...] = dot(probes[:, : handed.shape[1]].T, near_half(near, 1, probes.shape[0])).T


def rest_kernel(near, probes, samples, rest, handed_last):
    rows, columns = handed_last.shape
    rest[...] = samples[...] - dot(near_half(near, 0, rows), probes[...])
    handed_last[...] = dot(probes[:, probes.shape[1] - columns :].T, near_half(near, 1, rows)).T


def following_kernel(near, rest, following, _h, first, last, _hout):
    columns = first.shape[1]
    block = rest[...] - dot(near_half(near, 1, rest.shape[0]), following[...])
    first[...] = block[:, :columns]
    last[...] = block[:, columns:]


def leaf_kernel(rest, handed, probes, far, inverse, sample_coef, probe_coef, scratch):
    columns = far.shape[1]
    block = rest[...] - handed[...]
    far[...] = block
    products = dot(block, jnp.concatenate([block, probes[...]], axis=1), 0, 0)
    factor = inverse_factor(products[:, :columns], scratch)
    inverse[...] = factor
    coef = dot(factor, products)
    probe_coef[...] = coef[:, columns:]
    sample_coef[...] = coef[:, :columns]


def leaf_last_kernel(rest, handed, far, inverse, basis, sample_coef):
    basis[...] = dot(far[...], inverse[...], 1, 1)
    sample_coef[...] = dot(basis[...], rest[...] - handed[...], 0, 0)


def member_node(level):
    return lax.axis_index("leaf") >> level - 1


def pick_kernel(slots, couplings, *blocks):
    subtree = lax.axis_size("leaf")
    levels = subtree.bit_length() - 1
    for level, out in zip([*range(1, levels + 1), levels - 1], blocks):
        node = member_node(level)
        if out is blocks[-1]:
            node = node ^ 2
        index = subtree - (subtree >> level - 1) + (node >> 1)
        block = couplings[0, slots[0, index], node & 1]
        out[...] = jnp.concatenate([block, block.T], axis=1)


def quad_kernel(level, block, inner, outer, coef, out):
    node = member_node(level)
    inside = (node == 1) | (node == 2)
    main = jnp.where(inside, inner[...], outer[...])
    other = jnp.where(inside, outer[...], inner[...])
    out[...] = coef[...] - dot(block[...], jnp.concatenate([main, other], axis=0))


def term_kernel(level, block, mine, away, out):
    node = member_node(level)
    outer = (node == 0) | (node == 3)
    main = jnp.where(outer, mine[...], away[...])
    other = jnp.where(outer, away[...], mine[...])
    out[...] = dot(block[...], jnp.concatenate([main, other], axis=0))


def corrected_kernel(level, trees, block, one, two, first, out_first, out_last):
    columns = first.shape[1]
    main, other = one[...], two[...]
    if trees:
        straight = (lax.axis_index("clusters") ^ member_node(level)) & 1 == 0
        main, other = jnp.where(straight, main, other), jnp.where(straight, other, main)
    term = dot(block[...], jnp.concatenate([main, other], axis=0))
    out_first[...] = first[...] - term[:, :columns]
    out_last[...] = term[:, columns:]


def factor_kernel(mine, theirs, inverse, scratch):
    both = jnp.concatenate([mine[...], theirs[...]], axis=0)
    gram = dot(both, both, 0, 0)
    inverse[...] = inverse_factor(gram, scratch)


def basis_of(level, mine, theirs, inverse, out):
    size = mine.shape[0]
    own = (lax.axis_index("leaf") >> level - 1) & 1
    block = dot(jnp.concatenate([mine, theirs], axis=0), inverse, 1, 1)
    out[pl.ds(pl.multiple_of(own * size, size), size), :] = block[:size]
    out[pl.ds(pl.multiple_of((1 - own) * size, size), size), :] = block[size:]


def basis_kernel(level, inverse, mine, theirs, basis):
    basis_of(level, mine[...], theirs[...], inverse[...], basis)


def level_products(inverse, size, own, sibling):
    own, sibling = jnp.concatenate(own, axis=1), jnp.concatenate(sibling, axis=1)
    both = jnp.concatenate([own, sibling], axis=0)
    return dot(inverse, dot(both[:, :size], both, 0, 0))


def node_first_kernel(inverse, mine, theirs, first):
    both = jnp.concatenate([mine[...], theirs[...]], axis=0)
    first[...] = dot(inverse[...], dot(both, both, 0, 0))


def node_kernel(mine, theirs, mine_probes, theirs_probes, inverse, probe_coef, half, scratch):
    nodes = jnp.concatenate([mine[...], theirs[...]], axis=0)
    probes = jnp.concatenate([mine_probes[...], theirs_probes[...]], axis=0)
    cross = dot(nodes, probes, 0, 0)
    factor = inverse_factor(dot(nodes, nodes, 0, 0), scratch)
    inverse[...] = factor
    coef = dot(factor, cross)
    probe_coef[...] = coef
    width = half.shape[1]
    upper = lax.axis_index("leaf") & 1 == 1
    half[...] = jnp.where(upper, coef[:, width:], coef[:, :width])


def node_last_kernel(inverse, mine, mine_last, theirs, theirs_last, term, *refs):
    nodes = jnp.concatenate([mine[...], theirs[...]], axis=0)
    both = jnp.concatenate([mine_last[...], theirs_last[...]], axis=0)
    last = refs[0] if len(refs) == 1 else refs[1]
    last[...] = dot(inverse[...], dot(nodes, both, 0, 0)) - term[...]


def top_kernel(level, inverse, *refs):
    mine, theirs, (half, passed) = refs[:3], refs[3:5], refs[5:7]
    earlier, (bases, samples, probe_coef, basis, coefs, done) = refs[7:-6], refs[-6:]
    copies = [
        pltpu.make_async_copy(one, bases.at[0, at], done.at[at]) for at, one in enumerate(earlier)
    ]
    for copy in copies:
        copy.start()
    factor = inverse[...]
    mine, theirs = [ref[...] for ref in mine], [ref[...] for ref in theirs]
    basis_of(level, mine[0], theirs[0], factor, basis)
    at = len(earlier)
    copies.append(pltpu.make_async_copy(basis, bases.at[0, at], done.at[at]))
    copies[-1].start()
    upper = lax.axis_index("leaf") & 1 == 1
    theirs.append(jnp.where(upper, passed[...], half[...]))
    theirs.append(jnp.where(upper, half[...], passed[...]))
    coef = level_products(factor, factor.shape[0], mine, theirs)
    width = samples.shape[2]
    coefs[0] = coef[:, :width]
    coefs[1] = coef[:, width:]
    for at, out in enumerate((samples, probe_coef)):
        copies.append(pltpu.make_async_copy(coefs.at[at], out.at[0], done.at[level + at]))
        copies[-1].start()
    for copy in copies:
        copy.wait()


VMEM = pl.BlockSpec(memory_space=pltpu.VMEM)
SMEM = pl.BlockSpec(memory_space=pltpu.SMEM)
ANY = pl.BlockSpec(memory_space=pl.ANY)


def call(kernel, shapes, *operands, slots=None, flops=0, specs=None, out_specs=None, vmem=32, **options):
    outs = [jax.ShapeDtypeStruct(shape, jnp.float32) for shape in shapes]
    specs = [VMEM] * len(operands) if specs is None else specs
    out_specs = [VMEM] * len(outs) if out_specs is None else out_specs
    if slots is not None:
        operands = (slots,) + operands
        specs = [SMEM] + specs
    moved = 4 * (sum(o.size for o in operands) + sum(o.size for o in outs))
    return pl.pallas_call(
        kernel,
        out_shape=outs,
        in_specs=specs,
        out_specs=out_specs,
        compiler_params=pltpu.CompilerParams(vmem_limit_bytes=vmem * 2**20),
        cost_estimate=pl.CostEstimate(flops=flops, bytes_accessed=moved, transcendentals=0),
        **options,
    )(*operands)


def permuted(value, target):
    trees, subtree = lax.axis_size("clusters"), lax.axis_size("leaf")
    pairs = []
    for member in range(subtree):
        for tree in range(trees):
            to_tree, to_member = target(tree, member)
            if 0 <= to_tree < trees:
                pairs.append((member * trees + tree, to_member * trees + to_tree))
    return lax.ppermute(value, BOTH, pairs)


def flat_shift(value, by):
    subtree = lax.axis_size("leaf")
    return permuted(value, lambda tree, member: divmod(tree * subtree + member + by, subtree))


def swapped(value, mask):
    return permuted(value, lambda tree, member: (tree, member ^ mask))


def outward(value, half):
    return permuted(value, lambda tree, member: (tree - 1 if member < half else tree + 1, member))


def outer_swapped(value, half):
    return permuted(
        value, lambda tree, member: (tree - 1 if member < half else tree + 1, member ^ half)
    )


def tree_swapped(value, odd):
    return permuted(value, lambda tree, member: (tree + 1 if tree & 1 == odd else tree - 1, member))


def body(samples, probes, near_blocks, couplings, node_slot):
    rows, width = probes.shape
    columns = couplings.shape[-1]
    subtree = lax.axis_size("leaf")
    levels = subtree.bit_length() - 1
    chunks = rows // 128
    near = near_blocks.reshape(rows, 2, chunks, 128).transpose(0, 2, 1, 3).reshape(-1, 128)
    work = 12 * rows * rows * width
    tall, tall_last = (rows, columns), (rows, width - columns)
    square, square_last = (columns, columns), (columns, width - columns)

    following = flat_shift(probes, -1)
    (handed,) = call(handed_kernel, [tall], near, probes, flops=work)
    handed = flat_shift(handed, 1)
    blocks = call(pick_kernel, [(columns, 2 * columns)] * (levels + 1), couplings, slots=node_slot)
    following, *blocks = lax.optimization_barrier((following, *blocks))
    rest, handed_last = call(
        rest_kernel, [(rows, width), tall_last], near, probes, samples, flops=work
    )
    rest_first, rest_last, handed_last = call(
        following_kernel, [tall, tall_last, tall_last], near, rest, following, handed_last, flops=work,
        specs=[VMEM, VMEM, VMEM, ANY], out_specs=[VMEM, VMEM, ANY], input_output_aliases={3: 2},
    )
    handed_last = flat_shift(handed_last, 1)
    scratch = dict(scratch_shapes=[pltpu.VMEM((scratch_rows(columns), columns), jnp.float32)])
    far, inverse, first, probe_coef = call(
        leaf_kernel, [tall, square, square, (columns, width)], rest_first, handed, probes,
        flops=work, **scratch,
    )
    if subtree != 4:
        leaf_basis, last = call(
            leaf_last_kernel, [tall, square_last], rest_last, handed_last, far, inverse, flops=work
        )

    ancestors = []
    below = None
    for level in range(1, levels + 1):
        copies = 2 ** (level - 1)
        count = subtree // copies
        if count == 4:
            probe_first, probe_last = probe_coef[:, :columns], probe_coef[:, columns:]
            inner = swapped(probe_first, 2 * copies)
            outer = outer_swapped(probe_first, 2 * copies)
            away = outward(probe_last, 2 * copies)
            theirs_probe = swapped(probe_coef, copies)
            if level == 1:
                inner, handed_last = lax.optimization_barrier((inner, handed_last))
                leaf_basis, last = call(
                    leaf_last_kernel, [tall, square_last], rest_last, handed_last, far, inverse,
                    flops=work,
                )
                inner, outer, last = lax.optimization_barrier((inner, outer, last))
            (first,) = call(
                functools.partial(quad_kernel, level), [square], blocks[level - 1], inner, outer, first
            )
            away, _ = lax.optimization_barrier((away, first))
            (term_last,) = call(
                functools.partial(term_kernel, level), [square_last], blocks[-1], probe_last, away
            )
            term_last = swapped(term_last, 2 * copies)
            theirs_first = swapped(first, copies)
        else:
            correct = functools.partial(corrected_kernel, level, count == 2)
            if count == 2:
                fields = [tree_swapped(probe_coef, odd) for odd in (1, 0)]
                *fields, ancestors[-1] = lax.optimization_barrier((*fields, ancestors[-1]))
                theirs_half = swapped(half, copies)
            else:
                theirs_probe = swapped(probe_coef, copies)
                even = (lax.axis_index("leaf") >> level - 1) & 1 == 0
                fields = [flat_shift(probe_coef, by) for by in (2 * copies, -2 * copies)]
                fields = [jnp.where(even, *fields), jnp.where(even, *fields[::-1])]
            first, term_last = call(
                correct, [square, square_last], blocks[level - 1], *fields, first
            )
            theirs_first = swapped(first, copies)
        if below is None:
            last = last - term_last
        else:
            if level < levels:
                (last,) = call(node_last_kernel, [square_last], *below, term_last)
            else:
                last, theirs_half = call(
                    node_last_kernel, [square_last, half.shape], *below, term_last, theirs_half,
                    specs=[VMEM] * 6 + [ANY], out_specs=[VMEM, ANY], input_output_aliases={6: 1},
                )
                theirs_passed = swapped(theirs_half, 1)
        theirs_last = swapped(last, copies)
        if level == levels:
            (inverse,) = call(factor_kernel, [square], first, theirs_first, **scratch)
        else:
            inverse, probe_coef, half = call(
                node_kernel, [square, (columns, width), (columns, width // 2)],
                first, theirs_first, probe_coef, theirs_probe, flops=8 * work, **scratch,
            )
            probe_coef, half, last = lax.optimization_barrier((probe_coef, half, last))
            ancestors += call(
                functools.partial(basis_kernel, level), [(2 * columns, columns)],
                inverse, first, theirs_first,
            )
            below = inverse, first, last, theirs_first, theirs_last
            (first,) = call(node_first_kernel, [square], inverse, first, theirs_first)
    transfer_bases, top_samples, top_probes = call(
        functools.partial(top_kernel, levels),
        [(1, levels, 2 * columns, columns), (1, columns, width), (1, columns, width)],
        inverse, first, last, probe_coef, theirs_first, theirs_last, theirs_half, theirs_passed,
        *ancestors, out_specs=[ANY] * 3,
        scratch_shapes=[
            pltpu.VMEM((2 * columns, columns), jnp.float32),
            pltpu.VMEM((2, columns, width), jnp.float32),
            pltpu.SemaphoreType.DMA((levels + 2,)),
        ],
    )
    return (leaf_basis, transfer_bases, top_samples, top_probes)


def solution(mesh):
    in_specs = (
        P(("clusters", "leaf"), None),
        P(("clusters", "leaf"), None),
        P(("clusters", "leaf"), None, None),
        P("clusters", None, None, None, None),
        P("clusters", None),
    )
    out_specs = (
        P(("clusters", "leaf"), None),
        P(("clusters", "leaf"), None, None, None),
        P("clusters", None, None),
        P("clusters", None, None),
    )
    return jax.shard_map(body, mesh=mesh, in_specs=in_specs, out_specs=out_specs, check_vma=False)
```
